256 devices in a mesh: dp: 64 (over x, z, core), segment: 4 (over y).
Axes of the slice: x: 4, y: 4, z: 8, core: 2. Of those that a mesh axis runs over, the one named last changes fastest.
Arguments:
- queries_in: bfloat16 [64, 64, 3584], P('dp'), may hold values from -6 to 6
- passages_in: bfloat16 [64, 64, 3584], P('dp'), may hold values from -6 to 6
- query_len: int32 [64], P('dp'), may hold values from 16 to 64
- passage_len: int32 [64], P('dp'), may hold values from 16 to 64
- positive: int32 [64], P('dp'), may hold values from 0 to 63, each once
- norm_gain: float32 [4, 3584], P('segment'), may hold values from 0.5 to 1.5
- w_in: bfloat16 [4, 3584, 1024], P('segment', 'dp'), may hold values from -0.09375 to 0.09375
- w_out: bfloat16 [4, 1024, 3584], P('segment', 'dp'), may hold values from -0.1875 to 0.1875
Outputs:
- query_grads: bfloat16 [4, 64, 64, 3584], P('segment', 'dp')
- passage_grads: bfloat16 [4, 64, 64, 3584], P('segment', 'dp')
- gain_grads: float32 [4, 3584], P('segment')
The draws below stay inside these ranges and needn't reach their ends.
All inputs are finite; a program needn't handle non-finite values.
Results may differ from the reference program's by a relative error of at most 0.022.
Values may be sent and summed in bfloat16 or wider, within the bound.
A program may use at most 128 MiB of HBM per device.

```python
import math
import jax
import jax.numpy as jnp
from jax import lax

D = 3584
KVW = 1024
SEQ_LEN = 64
NQ = 64
SECTIONS = 4


def plant(values, rng, least, high):
    extent = values.shape
    spot = [jax.random.randint(jax.random.fold_in(rng, axis), (), 0, extent[axis]) for axis in range(len(extent))]
    values = values.at[tuple(spot)].set(least)
    longest = extent.index(max(extent))
    spot[longest] = (spot[longest] + 1) % extent[longest]
    return values.at[tuple(spot)].set(high)


def block_scale(key, extent, pieces, smallest, largest):
    loudness = 1.0
    for axis_at, blocks in pieces:
        heights = jax.random.uniform(jax.random.fold_in(jax.random.fold_in(key, 6), axis_at), (blocks,), jnp.float32, smallest / len(pieces), largest / len(pieces))
        loudness = loudness * jnp.repeat(jnp.exp(heights), extent[axis_at] // blocks).reshape((-1,) + (1,) * (len(extent) - 1 - axis_at))
    return loudness


def bell_draw(own_key, shape, scale, limit, split=(), kind=jnp.bfloat16):
    level = block_scale(own_key, shape, split, -0.22, 0.18) if split else 1.0
    drawn = jax.random.normal(own_key, shape, jnp.float32) * scale * level
    return jnp.minimum(jnp.maximum(drawn, -limit), limit).astype(kind)


def setup_inputs(seed: int = 0) -> dict:
    splits = jax.random.split(jax.random.key(seed), 9)
    return {
        "queries_in": bell_draw(splits[0], (NQ, SEQ_LEN, D), 1.0, 6.0, ((0, 64),)),
        "passages_in": bell_draw(splits[1], (NQ, SEQ_LEN, D), 1.0, 6.0, ((0, 64),)),
        "query_len": plant(jax.random.randint(splits[2], (NQ,), SEQ_LEN // 4, SEQ_LEN + 1), jax.random.fold_in(splits[2], 1), SEQ_LEN // 4, SEQ_LEN).astype(jnp.int32),
        "passage_len": plant(jax.random.randint(splits[3], (NQ,), SEQ_LEN // 4, SEQ_LEN + 1), jax.random.fold_in(splits[3], 1), SEQ_LEN // 4, SEQ_LEN).astype(jnp.int32),
        "positive": jax.random.permutation(splits[4], NQ).astype(jnp.int32),
        "norm_gain": jnp.clip(1.0 + 0.1 * jax.random.normal(splits[5], (SECTIONS, D), jnp.float32), 0.5, 1.5),
        "w_in": bell_draw(splits[6], (SECTIONS, D, KVW), D ** -0.5, 0.09375, ((0, 4), (1, 64))),
        "w_out": bell_draw(splits[7], (SECTIONS, KVW, D), KVW ** -0.5, 0.1875, ((0, 4), (1, 64))),
    }


sharpness_divisor = 0.02

def gelu_slope(pre):
    coeff = math.sqrt(2.0 / math.pi)
    tanh_val = jnp.tanh(coeff * (pre + 0.044715 * pre * pre * pre))
    return 0.5 * (1.0 + tanh_val) + 0.5 * pre * (1.0 - tanh_val * tanh_val) * coeff * (1.0 + 3.0 * 0.044715 * pre * pre)

def section_forward(stream, w_first, w_second, gain_vec):
    stream_f = stream.astype(jnp.float32)
    scale = lax.rsqrt(lax.optimization_barrier(jnp.mean(stream_f * stream_f, axis=-1, keepdims=True)) + 1e-06)
    normed = (stream_f * scale * gain_vec).astype(jnp.bfloat16)
    pre = jnp.dot(normed, w_first, preferred_element_type=jnp.float32)
    act = jax.nn.gelu(pre, approximate=True).astype(jnp.bfloat16)
    return (stream_f + jnp.dot(act, w_second, preferred_element_type=jnp.float32)).astype(jnp.bfloat16)

def section_backward(stream, grad_out, w_first, w_second, gain_vec):
    stream_f = stream.astype(jnp.float32)
    scale = lax.rsqrt(lax.optimization_barrier(jnp.mean(stream_f * stream_f, axis=-1, keepdims=True)) + 1e-06)
    normed = (stream_f * scale * gain_vec).astype(jnp.bfloat16)
    pre = jnp.dot(normed, w_first, preferred_element_type=jnp.float32)
    back = jnp.dot(grad_out, w_second.T, preferred_element_type=jnp.float32)
    grad_pre = (back * gelu_slope(pre)).astype(jnp.bfloat16)
    grad_normed = jnp.dot(grad_pre, w_first.T, preferred_element_type=jnp.float32)
    unit = stream_f * scale
    gain_grad = lax.optimization_barrier(jnp.sum(grad_normed * unit, axis=0))
    grad_unit = grad_normed * gain_vec
    grad_in = grad_out.astype(jnp.float32) + scale * (grad_unit - unit * lax.optimization_barrier(jnp.mean(grad_unit * unit, axis=-1, keepdims=True)))
    return (grad_in.astype(jnp.bfloat16), gain_grad)

def reference(queries_in, passages_in, query_len, passage_len, positive, norm_gain, w_in, w_out):
    row_total = NQ * SEQ_LEN
    stream = jnp.concatenate([queries_in.reshape(row_total, D), passages_in.reshape(row_total, D)], axis=0)
    inputs_kept = []
    for section in range(SECTIONS):
        inputs_kept.append(stream)
        stream = section_forward(stream, w_in[section], w_out[section], norm_gain[section])
    hidden_state = stream.reshape(2 * NQ, SEQ_LEN, D)
    lengths = jnp.concatenate([query_len, passage_len]).astype(jnp.int32)
    validity_mask = (jnp.arange(SEQ_LEN, dtype=jnp.int32)[None, :] < lengths[:, None]).astype(jnp.float32)
    count_totals = lengths.astype(jnp.float32)
    pooled_state = jnp.einsum('np,npi->ni', validity_mask, hidden_state.astype(jnp.float32)) / count_totals[:, None]
    inv_norm = lax.rsqrt(lax.optimization_barrier(jnp.sum(pooled_state * pooled_state, axis=-1)) + 1e-06)
    embedded = pooled_state * inv_norm[:, None]
    question_encodings = embedded[:NQ]
    document_encodings = embedded[NQ:]
    similarity_matrix = jnp.dot(question_encodings, document_encodings.T, precision=lax.Precision.HIGHEST) / sharpness_divisor
    top = lax.optimization_barrier(jnp.max(similarity_matrix, axis=1, keepdims=True))
    expo = jnp.exp(similarity_matrix - top)
    probs = expo / lax.optimization_barrier(jnp.sum(expo, axis=1, keepdims=True))
    onehot = (jnp.arange(NQ, dtype=jnp.int32)[None, :] == positive[:, None]).astype(jnp.float32)
    similarity_derivative = (probs - onehot) / NQ
    question_derivative = jnp.dot(similarity_derivative, document_encodings, precision=lax.Precision.HIGHEST) / sharpness_divisor
    document_derivative = jnp.dot(similarity_derivative.T, question_encodings, precision=lax.Precision.HIGHEST) / sharpness_divisor
    grad_emb = jnp.concatenate([question_derivative, document_derivative], axis=0)
    grad_pooled = inv_norm[:, None] * grad_emb - pooled_state * (inv_norm ** 3)[:, None] * lax.optimization_barrier(jnp.sum(pooled_state * grad_emb, axis=-1, keepdims=True))
    grad_stream = (grad_pooled[:, None, :] * (validity_mask / count_totals[:, None])[:, :, None]).astype(jnp.bfloat16)
    grad_stream = grad_stream.reshape(2 * row_total, D)
    query_list = [None] * SECTIONS
    passage_list = [None] * SECTIONS
    gain_list = [None] * SECTIONS
    for section in range(SECTIONS - 1, -1, -1):
        grad_stream, gain_grad = section_backward(inputs_kept[section], grad_stream, w_in[section], w_out[section], norm_gain[section])
        query_list[section] = grad_stream[:row_total].reshape(NQ, SEQ_LEN, D)
        passage_list[section] = grad_stream[row_total:].reshape(NQ, SEQ_LEN, D)
        gain_list[section] = gain_grad
    return (jnp.stack(query_list), jnp.stack(passage_list), jnp.stack(gain_list))
```

```python
import math

import jax
import jax.numpy as jnp
from jax import lax
from jax.experimental import pallas as pl
from jax.experimental.pallas import tpu as pltpu
from jax.sharding import PartitionSpec as P

MESH = pl.DeviceIdType.MESH
BF, F32 = jnp.bfloat16, jnp.float32
HI = lax.Precision.HIGHEST
D, KVW, SEQ, NQ = 3584, 1024, 64, 64
NX, NZ, NC, NY = 4, 8, 2, 4
TEMP = 0.02
CHUNK = 32
CHUNKS = 2 * SEQ // CHUNK
PACK = 512
PACKS = D // PACK
EPS = 1e-06
C0 = math.sqrt(2.0 / math.pi)
W_IN, W_OUT, EMB = 0, 1, 2
ALL = slice(None)
NT = (((1,), (1,)), ((), ()))


def gelu(v):
    return 0.5 * v * (1.0 + jnp.tanh(C0 * (v + 0.044715 * v * v * v)))


def gelu_slope(v):
    t = jnp.tanh(C0 * (v + 0.044715 * v * v * v))
    return 0.5 * (1.0 + t) + 0.5 * v * (1.0 - t * t) * C0 * (1.0 + 3.0 * 0.044715 * v * v)


def kernel(
    tok_ref, gain_ref, weight_ref, pos_ref, wi_ref, wo_ref,
    grad_ref, gsum_ref,
    win, wout, emb, pair, kept, pre, scales, normed, act, outb, gin, dpre, dn, gacc, pooled, dpool,
    near, far,
    ag_send, ag_recv, pair_sem, hop_send, hop_recv, red_send, red_recv,
):
    me = lax.axis_index("dp")
    seg = lax.axis_index("segment")
    x, z, c = me // (NZ * NC), (me // NC) % NZ, me % NC

    def dev(px, pz, pc):
        return ((px * NZ + pz) * NC + pc, seg)

    def xo(by):
        return (x + by + NX) % NX

    def zo(by):
        return (z + by + NZ) % NZ

    barrier = pltpu.get_barrier_semaphore()
    mates = [dev(xo(dx), z, pc) for dx in range(NX) for pc in (c, 1 - c)][1:]
    mates += [dev(x, zo(dz), c) for dz in range(1, NZ)]
    mates += [(me, (seg + by) % NY) for by in (1, NY - 1)]
    for mate in mates:
        pl.semaphore_signal(barrier, inc=1, device_id=mate, device_id_type=MESH)
    pl.semaphore_wait(barrier, len(mates))

    def piece(tensor, colour, xs, zs, pc):
        if tensor == W_IN:
            rows = pl.ds(0, 48) if colour == 0 else pl.ds(48, 64)
            return win.at[xs, zs, rows, pl.ds(pl.multiple_of(pc * 512, 512), 512)]
        if tensor == W_OUT:
            cols = pl.ds(0, 1536) if colour == 0 else pl.ds(1536, 2048)
            return wout.at[xs, zs, pl.ds(pc, 1), :, cols]
        cols = pl.ds(0, 256) if colour == 0 else pl.ds(256, 256)
        return emb.at[xs, zs, pl.ds(pc, 1), :, cols]

    def copy_of(tensor, slot, ref, target):
        return pltpu.make_async_remote_copy(
            src_ref=ref, dst_ref=ref,
            send_sem=ag_send.at[tensor, slot], recv_sem=ag_recv.at[tensor, slot],
            device_id=target, device_id_type=MESH,
        )

    def gather(tensor, colour, plus, pending):
        def send(slot, xs, zs, target):
            op = copy_of(tensor, slot, piece(tensor, colour, xs, zs, c), target)
            op.start()
            pending.append(op.wait_send)

        def got(slot, xs, zs):
            copy_of(tensor, slot, piece(tensor, colour, xs, zs, c), dev(x, z, 1 - c)).wait_recv()

        def pass_on(slot, xs, zs):
            send(slot, xs, zs, dev(x, z, 1 - c))
            other = copy_of(tensor, slot, piece(tensor, colour, xs, zs, 1 - c), dev(x, z, 1 - c))
            pending.append(other.wait_recv)

        def one(at):
            return pl.ds(at, 1)

        up, down = dev(x, zo(1), c), dev(x, zo(-1), c)
        right, left = dev(xo(1), z, c), dev(xo(-1), z, c)
        if colour == 0:
            for dx in range(1, NX):
                send(dx - 1, one(x), one(z), dev(xo(dx), z, c))
            yield
            for dx in range(1, NX):
                got(dx - 1, one(xo(-dx)), one(z))
            send(3, ALL, one(z), up)
            send(4, ALL, one(z), down)
            pass_on(22, ALL, one(z))
            for step in range(1, 4):
                yield
                got(1 + 2 * step, ALL, one(zo(-step)))
                if step < 3:
                    send(3 + 2 * step, ALL, one(zo(-step)), up)
                else:
                    send(9, pl.ds(0, 2), one(zo(-3)), up)
                got(2 + 2 * step, ALL, one(zo(step)))
                if step < 3:
                    send(4 + 2 * step, ALL, one(zo(step)), down)
                else:
                    send(10, pl.ds(2, 2), one(zo(3)), down)
                pass_on(21 + 2 * step, ALL, one(zo(-step)))
                pass_on(22 + 2 * step, ALL, one(zo(step)))
            yield
            got(9, pl.ds(0, 2), one(zo(-4)))
            got(10, pl.ds(2, 2), one(zo(4)))
            pass_on(29, ALL, one(zo(4)))
        else:
            send(11, one(x), one(z), up)
            send(12, one(x), one(z), down)
            for step in range(1, 4):
                yield
                got(9 + 2 * step, one(x), one(zo(-step)))
                if step < 3:
                    send(11 + 2 * step, one(x), one(zo(-step)), up)
                elif plus:
                    send(17, one(x), one(zo(-3)), up)
                got(10 + 2 * step, one(x), one(zo(step)))
                if step < 3:
                    send(12 + 2 * step, one(x), one(zo(step)), down)
                elif not plus:
                    send(17, one(x), one(zo(3)), down)
            yield
            got(17, one(x), one(zo(4)))
            send(18, one(x), ALL, right)
            send(19, one(x), ALL, left)
            pass_on(30, one(x), ALL)
            yield
            got(18, one(xo(-1)), ALL)
            send(20, one(xo(-1)), pl.ds(0, 4), right)
            got(19, one(xo(1)), ALL)
            send(21, one(xo(1)), pl.ds(4, 4), left)
            pass_on(31, one(xo(-1)), ALL)
            pass_on(32, one(xo(1)), ALL)
            yield
            got(20, one(xo(2)), pl.ds(0, 4))
            got(21, one(xo(2)), pl.ds(4, 4))
            pass_on(33, one(xo(2)), ALL)

    def run(streams, ahead=()):
        waiting = list(ahead)
        for stream in streams:
            next(stream)
            waiting.append(stream)
        while waiting:
            for stream in list(waiting):
                if next(stream, "end") == "end":
                    waiting.remove(stream)

    pending = []
    wout[pl.ds(x, 1), pl.ds(z, 1), pl.ds(c, 1)] = wo_ref[...].reshape(1, 1, 1, 16, D)
    first = [gather(W_OUT, 1, False, pending), gather(W_OUT, 0, False, pending)]
    for stream in first:
        next(stream)
    swap = pltpu.make_async_remote_copy(
        src_ref=wi_ref, dst_ref=pair, send_sem=pair_sem.at[0], recv_sem=pair_sem.at[1],
        device_id=dev(x, z, 1 - c), device_id_type=MESH,
    )
    swap.start()

    @pl.when(seg == 0)
    def _():
        kept[...] = tok_ref[...].reshape(2 * SEQ, D)

    swap.wait()
    mine, theirs = wi_ref[...].astype(F32), pair[...].astype(F32)
    both = jnp.concatenate(
        [jnp.where(c == 0, mine, theirs), jnp.where(c == 0, theirs, mine)], axis=0
    )
    half = jnp.where(c == 0, both[:, :512], both[:, 512:]).astype(BF)
    win[pl.ds(x, 1), pl.ds(z, 1), :, pl.ds(pl.multiple_of(c * 512, 512), 512)] = half.reshape(1, 1, 112, 512)
    run([gather(W_IN, 1, True, pending), gather(W_IN, 0, True, pending)], first)
    for wait in pending:
        wait()

    def hop(step, slot, src, dst, to):
        return pltpu.make_async_remote_copy(
            src_ref=src, dst_ref=dst, send_sem=hop_send.at[step, slot], recv_sem=hop_recv.at[step, slot],
            device_id=(me, to), device_id_type=MESH,
        )

    def chunk_rows(k):
        return pl.ds(pl.multiple_of(k * CHUNK, CHUNK), CHUNK)

    gain = gain_ref[...]
    pooled[...] = jnp.zeros_like(pooled)

    @pl.loop(0, CHUNKS)
    def _(k):
        rows = chunk_rows(k)

        @pl.when(seg > 0)
        def _():
            hop(0, k, outb.at[rows], kept.at[rows], seg).wait_recv()

        for part in range(CHUNK // 16):
            sub = pl.ds(pl.multiple_of(k * CHUNK + part * 16, 16), 16)
            stream = kept[sub, :].astype(F32)
            scale = lax.rsqrt(jnp.mean(stream * stream, axis=-1, keepdims=True) + EPS)
            scales[sub, :] = jnp.broadcast_to(scale, (16, 128))
            normed[pl.ds(part * 16, 16), :] = (stream * scale * gain).astype(BF)

        @pl.loop(0, KVW // 256)
        def _(n):
            cols = pl.ds(pl.multiple_of(n * 256, 256), 256)
            v = jnp.dot(normed[...], win[:, :, :, cols].reshape(D, 256), preferred_element_type=F32)
            pre[rows, cols] = v
            act[:, cols] = gelu(v).astype(BF)

        @pl.loop(0, D // 256)
        def _(n):
            cols = pl.ds(pl.multiple_of(n * 256, 256), 256)
            v = jnp.dot(act[...], wout[:, :, :, :, cols].reshape(KVW, 256), preferred_element_type=F32)
            v = (kept[rows, cols].astype(F32) + v).astype(BF)
            outb[rows, cols] = v

        @pl.when(seg < NY - 1)
        def _():
            hop(0, k, outb.at[rows], kept.at[rows], seg + 1).start()

        @pl.when(seg == NY - 1)
        def _():
            half = (k * CHUNK) // SEQ
            total = jnp.zeros((8, D), F32)
            for part in range(CHUNK // 16):
                sub = pl.ds(pl.multiple_of(k * CHUNK + part * 16, 16), 16)
                scaled = outb[sub, :].astype(F32) * weight_ref[sub, 0:1]
                total = total + scaled[0:8] + scaled[8:16]
            pooled[half] += total

    @pl.when(seg == NY - 1)
    def _():
        here = (x, z, c)
        rowsums, invs, packs = [], [], []
        for side in range(2):
            total = jnp.sum(pooled[side], axis=0, keepdims=True)
            inv = lax.rsqrt(jnp.sum(total * total, axis=-1, keepdims=True) + EPS)
            for k in range(PACKS):
                dpool[side, k : k + 1, :] = total[:, k * PACK : (k + 1) * PACK]
            dpool[side, PACKS : PACKS + 1, :] = jnp.zeros((1, PACK), F32)
            packed = dpool[side]
            if side == 0:
                sent = packed * inv + pos_ref[...]
            else:
                sent = packed * inv
            emb[pl.ds(x, 1), pl.ds(z, 1), pl.ds(c, 1), pl.ds(8 * side, 8), :] = sent.reshape(1, 1, 1, 8, PACK)
            invs.append(inv)
            packs.append(packed)
        waits = []
        run([gather(EMB, 1, True, waits), gather(EMB, 0, True, waits)])
        for wait in waits:
            wait()
        q = emb[:, :, :, 0:8, :].reshape(NQ * 8, PACK)
        p = emb[:, :, :, 8:16, :].reshape(NQ * 8, PACK)
        gram = lax.dot_general(q, p, NT, precision=HI, preferred_element_type=F32)
        r = lax.broadcasted_iota(jnp.int32, (NQ * 8, NQ * 8), 0)
        l = lax.broadcasted_iota(jnp.int32, (NQ * 8, NQ * 8), 1)
        gram = jnp.where((r % 8 == l % 8) & (r % 8 < PACKS), gram, 0.0)
        i64 = lax.broadcasted_iota(jnp.int32, (NQ, NQ * 8), 0)
        i512 = lax.broadcasted_iota(jnp.int32, (NQ, NQ * 8), 1)
        fold = jnp.where(i512 // 8 == i64, 1.0, 0.0)
        pick = jnp.where(i512 == i64 * 8 + PACKS, 1.0, 0.0)
        folded = jnp.dot(fold, gram, precision=HI, preferred_element_type=F32)
        logits = lax.dot_general(folded, fold, NT, precision=HI, preferred_element_type=F32) / TEMP
        onehot = jnp.dot(pick, q[:, 0:128], precision=HI, preferred_element_type=F32)[:, 0:NQ]
        expo = jnp.exp(logits - jnp.max(logits, axis=1, keepdims=True))
        probs = expo / jnp.sum(expo, axis=1, keepdims=True)
        dlogits = (probs - onehot) / NQ
        ii = lax.broadcasted_iota(jnp.int32, (NQ, NQ), 0)
        jj = lax.broadcasted_iota(jnp.int32, (NQ, NQ), 1)
        row = jnp.sum(jnp.where(ii == me, dlogits, 0.0), axis=0, keepdims=True)
        col = jnp.sum(jnp.where(jj == me, dlogits, 0.0), axis=1, keepdims=True)
        row = jnp.dot(row, fold, precision=HI, preferred_element_type=F32)
        col = jnp.sum(col * fold, axis=0, keepdims=True)
        k8 = lax.broadcasted_iota(jnp.int32, (8, NQ * 8), 0)
        l8 = lax.broadcasted_iota(jnp.int32, (8, NQ * 8), 1)
        diag = (l8 % 8 == k8) & (k8 < PACKS)
        for side, (spread, other) in enumerate(((row, p), (col, q))):
            demb = jnp.dot(jnp.where(diag, spread, 0.0), other, precision=HI, preferred_element_type=F32) / TEMP
            inv, packed = invs[side], packs[side]
            along = jnp.sum(jnp.sum(packed * demb, axis=1, keepdims=True), axis=0, keepdims=True)
            grad = inv * demb - packed * (inv * inv * inv) * along
            for k in range(PACKS):
                pooled[side, 0:1, k * PACK : (k + 1) * PACK] = grad[k : k + 1, :]
        for side in range(2):
            grad = pooled[side, 0:1, :]
            for part in range(SEQ // 16):
                sub = pl.ds(side * SEQ + part * 16, 16)
                gin[sub, :] = (weight_ref[sub, 0:1] * grad).astype(BF)

    gacc[...] = jnp.zeros_like(gacc)

    @pl.loop(0, CHUNKS)
    def _(k):
        rows = chunk_rows(k)

        @pl.when(seg < NY - 1)
        def _():
            hop(1, k, outb.at[rows], gin.at[rows], seg).wait_recv()
            hop(0, k, outb.at[rows], kept.at[rows], seg).wait_send()

        dout = gin[rows, :]
        for n in range(NX):
            cols = pl.ds(n * 256, 256)
            back = lax.dot_general(dout, wout[n].reshape(256, D), NT, preferred_element_type=F32)
            dpre[:, cols] = (back * gelu_slope(pre[rows, cols])).astype(BF)
        for n in range(NX):
            cols = pl.ds(n * 896, 896)
            dn[:, cols] = lax.dot_general(dpre[...], win[n].reshape(896, KVW), NT, preferred_element_type=F32)
        for part in range(CHUNK // 16):
            sub = pl.ds(pl.multiple_of(k * CHUNK + part * 16, 16), 16)
            scale = scales[sub, 0:1]
            unit = kept[sub, :].astype(F32) * scale
            dnormed = dn[pl.ds(part * 16, 16), :]
            both = dnormed * unit
            gacc[...] += both[0:8] + both[8:16]
            du = dnormed * gain
            mean = jnp.mean(du * unit, axis=-1, keepdims=True)
            res = gin[sub, :].astype(F32) + scale * (du - unit * mean)
            outb[sub, :] = res.astype(BF)

        @pl.when(seg > 0)
        def _():
            hop(1, k, outb.at[rows], gin.at[rows], seg - 1).start()

    grad_ref[...] = outb[...].reshape(2, SEQ, D)

    def reduce(step, buf, slot, at, peers):
        ops = []
        for j, (target, source) in enumerate(peers):
            op = pltpu.make_async_remote_copy(
                src_ref=buf.at[at], dst_ref=buf.at[at],
                send_sem=red_send.at[step, j], recv_sem=red_recv.at[step, j],
                device_id=target, device_id_type=MESH,
            )
            op.start()
            ops.append(op.wait_send)
            ops.append(pltpu.make_async_remote_copy(
                src_ref=buf.at[source], dst_ref=buf.at[source],
                send_sem=red_send.at[step, j], recv_sem=red_recv.at[step, j],
                device_id=target, device_id_type=MESH,
            ).wait_recv)
        for op in ops:
            op()

    at = x * NC + c
    near[at] = jnp.sum(gacc[...], axis=0, keepdims=True)
    peers = []
    for dx in range(NX):
        for other in range(NC):
            if dx or other:
                pc = c if other == 0 else 1 - c
                peers.append((dev(xo(dx), z, pc), xo(-dx) * NC + pc))
    reduce(0, near, 0, at, peers)
    far[z] = jnp.sum(near[...], axis=0)
    reduce(1, far, 0, z, [(dev(x, zo(dz), c), zo(-dz)) for dz in range(1, NZ)])
    gsum_ref[...] = jnp.sum(far[...], axis=0)

    @pl.when(seg > 0)
    def _():
        for k in range(CHUNKS):
            rows = pl.ds(k * CHUNK, CHUNK)
            hop(1, k, outb.at[rows], gin.at[rows], seg).wait_send()


def local(queries_in, passages_in, query_len, passage_len, positive, norm_gain, w_in, w_out):
    tokens = jnp.concatenate([queries_in, passages_in], axis=0)
    lengths = jnp.concatenate([query_len, passage_len])
    mask = (jnp.arange(SEQ, dtype=jnp.int32)[None, :] < lengths[:, None]).astype(F32)
    weights = mask / lengths.astype(F32)[:, None]
    weights = jnp.broadcast_to(weights.reshape(2 * SEQ, 1), (2 * SEQ, 128))
    spot_row = lax.broadcasted_iota(jnp.int32, (8, PACK), 0)
    spot_col = lax.broadcasted_iota(jnp.int32, (8, PACK), 1)
    chosen = ((spot_row == PACKS) & (spot_col == positive[0])).astype(F32)
    vmem = pl.BlockSpec(memory_space=pltpu.VMEM)
    rows = 2 * SEQ
    grads, gains = pl.pallas_call(
        kernel,
        out_shape=(
            jax.ShapeDtypeStruct((2, SEQ, D), BF),
            jax.ShapeDtypeStruct((1, D), F32),
        ),
        in_specs=[vmem] * 6,
        out_specs=(vmem, vmem),
        scratch_shapes=[
            pltpu.VMEM((NX, NZ, 112, KVW), BF),
            pltpu.VMEM((NX, NZ, NC, 16, D), BF),
            pltpu.VMEM((NX, NZ, NC, 16, PACK), F32),
            pltpu.VMEM((56, KVW), BF),
            pltpu.VMEM((rows, D), BF),
            pltpu.VMEM((rows, KVW), F32),
            pltpu.VMEM((rows, 128), F32),
            pltpu.VMEM((CHUNK, D), BF),
            pltpu.VMEM((CHUNK, KVW), BF),
            pltpu.VMEM((rows, D), BF),
            pltpu.VMEM((rows, D), BF),
            pltpu.VMEM((CHUNK, KVW), BF),
            pltpu.VMEM((CHUNK, D), F32),
            pltpu.VMEM((8, D), F32),
            pltpu.VMEM((2, 8, D), F32),
            pltpu.VMEM((2, 8, PACK), F32),
            pltpu.VMEM((NX * NC, 1, D), F32),
            pltpu.VMEM((NZ, 1, D), F32),
            pltpu.SemaphoreType.DMA((3, 34)),
            pltpu.SemaphoreType.DMA((3, 34)),
            pltpu.SemaphoreType.DMA((2,)),
            pltpu.SemaphoreType.DMA((2, CHUNKS)),
            pltpu.SemaphoreType.DMA((2, CHUNKS)),
            pltpu.SemaphoreType.DMA((2, 7)),
            pltpu.SemaphoreType.DMA((2, 7)),
        ],
        compiler_params=pltpu.CompilerParams(
            collective_id=0, has_side_effects=True, vmem_limit_bytes=48 * 1024 * 1024
        ),
        name="embedder_window",
    )(tokens, norm_gain, weights, chosen, w_in[0], w_out[0])
    return grads[0][None, None], grads[1][None, None], gains


def solution(mesh):
    return jax.shard_map(
        local,
        mesh=mesh,
        in_specs=(
            P("dp", None, None),
            P("dp", None, None),
            P("dp"),
            P("dp"),
            P("dp"),
            P("segment", None),
            P("segment", "dp", None),
            P("segment", "dp", None),
        ),
        out_specs=(
            P("segment", "dp", None, None),
            P("segment", "dp", None, None),
            P("segment", None),
        ),
        check_vma=False,
    )
```

```python
import math

import jax
import jax.numpy as jnp
from jax import lax
from jax.experimental import pallas as pl
from jax.experimental.pallas import tpu as pltpu
from jax.sharding import PartitionSpec as P

MESH = pl.DeviceIdType.MESH
BF, F32 = jnp.bfloat16, jnp.float32
HI = lax.Precision.HIGHEST
D, KVW, SEQ, NQ = 3584, 1024, 64, 64
NX, NZ, NC, NY = 4, 8, 2, 4
TEMP = 0.02
CHUNK = 32
CHUNKS = 2 * SEQ // CHUNK
PARTS = 4
WIDE = D // PARTS
PACKS = D // 128
WEIGHT_ORDER = (
    2, 3, 0, 1, 2, 3, 0, 0, 1, 2, 2, 3, 2, 0, 0, 2, 0, 2, 0, 0, 1, 3, 2, 2, 2, 0, 0, 0, 2, 2, 2, 0, 1, 3, 1, 2, 0, 3,
)
EMB_ORDER = (0, 1, 0, 1, 1, 0, 0, 1, 0, 0, 0, 0, 0, 0, 0, 1, 0, 0, 0, 1)
EPS = 1e-06
C0 = math.sqrt(2.0 / math.pi)
W_IN, W_OUT, EMB = 0, 1, 2
ALL = slice(None)
NT = (((1,), (1,)), ((), ()))


def gelu(v):
    return 0.5 * v * (1.0 + jnp.tanh(C0 * (v + 0.044715 * v * v * v)))


def gelu_slope(v):
    t = jnp.tanh(C0 * (v + 0.044715 * v * v * v))
    return 0.5 * (1.0 + t) + 0.5 * v * (1.0 - t * t) * C0 * (1.0 + 3.0 * 0.044715 * v * v)


def kernel(
    queries_ref, passages_ref, gain_ref, weight_ref, pos_ref, wi_ref, wo_ref,
    qgrad_ref, pgrad_ref, gsum_ref,
    win, wout, win_t, wout_t, emb, embs, pair, kept, pre, scales, normed, act, outb, gin, dpre, gacc, pooled,
    pack, near, far,
    ag_send, ag_recv, pair_sem, hop_send, hop_recv, red_send, red_recv,
):
    me = lax.axis_index("dp")
    seg = lax.axis_index("segment")
    x, z, c = me // (NZ * NC), (me // NC) % NZ, me % NC

    def dev(px, pz, pc):
        return ((px * NZ + pz) * NC + pc, seg)

    def xo(by):
        return (x + by + NX) % NX

    def zo(by):
        return (z + by + NZ) % NZ

    barrier = pltpu.get_barrier_semaphore()
    mates = [dev(xo(dx), z, pc) for dx in range(NX) for pc in (c, 1 - c)][1:]
    mates += [dev(x, zo(dz), c) for dz in range(1, NZ)]
    mates += [(me, (seg + by) % NY) for by in (1, NY - 1)]
    for mate in mates:
        pl.semaphore_signal(barrier, inc=1, device_id=mate, device_id_type=MESH)
    pl.semaphore_wait(barrier, len(mates))

    def piece(tensor, colour, xs, zs, pc):
        if tensor == W_IN:
            rows = pl.ds(0, 48) if colour == 0 else pl.ds(48, 64)
            return win.at[xs, zs, rows, pl.ds(pl.multiple_of(pc * 512, 512), 512)]
        if tensor == W_OUT:
            cols = pl.ds(0, 1536) if colour == 0 else pl.ds(1536, 2048)
            return wout.at[xs, zs, pl.ds(pc, 1), :, cols]
        return emb.at[xs, zs, pl.ds(pc, 1), pl.ds(32 * colour, 32), :]

    def copy_of(tensor, slot, ref, target):
        return pltpu.make_async_remote_copy(
            src_ref=ref, dst_ref=ref,
            send_sem=ag_send.at[tensor, slot], recv_sem=ag_recv.at[tensor, slot],
            device_id=target, device_id_type=MESH,
        )

    def gather(tensor, colour, plus, pending):
        def send(slot, xs, zs, target):
            op = copy_of(tensor, slot, piece(tensor, colour, xs, zs, c), target)
            op.start()
            pending.append(op.wait_send)

        def got(slot, xs, zs):
            copy_of(tensor, slot, piece(tensor, colour, xs, zs, c), dev(x, z, 1 - c)).wait_recv()

        def pass_on(slot, xs, zs):
            send(slot, xs, zs, dev(x, z, 1 - c))
            other = copy_of(tensor, slot, piece(tensor, colour, xs, zs, 1 - c), dev(x, z, 1 - c))
            pending.append(other.wait_recv)

        def one(at):
            return pl.ds(at, 1)

        up, down = dev(x, zo(1), c), dev(x, zo(-1), c)
        right, left = dev(xo(1), z, c), dev(xo(-1), z, c)
        if colour == 0:
            for dx in range(1, NX):
                send(dx - 1, one(x), one(z), dev(xo(dx), z, c))
            yield
            for dx in range(1, NX):
                got(dx - 1, one(xo(-dx)), one(z))
            send(3, ALL, one(z), up)
            send(4, ALL, one(z), down)
            pass_on(42, ALL, one(z))
            for step in range(1, 4):
                yield
                got(1 + 2 * step, ALL, one(zo(-step)))
                if step < 3:
                    send(3 + 2 * step, ALL, one(zo(-step)), up)
                else:
                    send(9, pl.ds(0, 2), one(zo(-3)), up)
                got(2 + 2 * step, ALL, one(zo(step)))
                if step < 3:
                    send(4 + 2 * step, ALL, one(zo(step)), down)
                else:
                    send(10, pl.ds(2, 2), one(zo(3)), down)
                pass_on(41 + 2 * step, ALL, one(zo(-step)))
                pass_on(42 + 2 * step, ALL, one(zo(step)))
            yield
            got(9, pl.ds(0, 2), one(zo(-4)))
            got(10, pl.ds(2, 2), one(zo(4)))
            pass_on(49, ALL, one(zo(4)))
            return
        offsets = (0, -1, 1, -2, 2, -3, 3, 4)

        def sideways(j):
            at = one(zo(offsets[j]))
            send(18 + j, one(x), at, right)
            send(26 + j, one(x), at, left)

        send(11, one(x), one(z), up)
        send(12, one(x), one(z), down)
        sideways(0)
        for step in range(1, 4):
            yield
            got(9 + 2 * step, one(x), one(zo(-step)))
            if step < 3:
                send(11 + 2 * step, one(x), one(zo(-step)), up)
            elif plus:
                send(17, one(x), one(zo(-3)), up)
            sideways(2 * step - 1)
            got(10 + 2 * step, one(x), one(zo(step)))
            if step < 3:
                send(12 + 2 * step, one(x), one(zo(step)), down)
            elif not plus:
                send(17, one(x), one(zo(3)), down)
            sideways(2 * step)
        yield
        got(17, one(x), one(zo(4)))
        sideways(7)
        pass_on(50, one(x), ALL)
        for j, by in enumerate(offsets):
            yield
            got(18 + j, one(xo(-1)), one(zo(by)))
            got(26 + j, one(xo(1)), one(zo(by)))
            if j % 2 == 0:
                send(34 + j, one(xo(-1)), one(zo(by)), right)
            else:
                send(34 + j, one(xo(1)), one(zo(by)), left)
        pass_on(51, one(xo(-1)), ALL)
        pass_on(52, one(xo(1)), ALL)
        yield
        for j, by in enumerate(offsets):
            got(34 + j, one(xo(2)), one(zo(by)))
        pass_on(53, one(xo(2)), ALL)

    def follow(streams, order):
        for at in order:
            next(streams[at], None)

    pending = []
    wout[pl.ds(x, 1), pl.ds(z, 1), pl.ds(c, 1)] = wo_ref[...].reshape(1, 1, 1, 16, D)
    streams = [
        gather(tensor, colour, tensor == W_IN, pending) for tensor in (W_OUT, W_IN) for colour in (1, 0)
    ]
    follow(streams, (0, 1))
    swap = pltpu.make_async_remote_copy(
        src_ref=wi_ref, dst_ref=pair, send_sem=pair_sem.at[0], recv_sem=pair_sem.at[1],
        device_id=dev(x, z, 1 - c), device_id_type=MESH,
    )
    swap.start()

    @pl.when(seg == 0)
    def _():
        kept[pl.ds(0, SEQ), :] = queries_ref[0]
        kept[pl.ds(SEQ, SEQ), :] = passages_ref[0]

    swap.wait()
    mine, theirs = wi_ref[...].astype(F32), pair[...].astype(F32)
    both = jnp.concatenate(
        [jnp.where(c == 0, mine, theirs), jnp.where(c == 0, theirs, mine)], axis=0
    )
    half = jnp.where(c == 0, both[:, :512], both[:, 512:]).astype(BF)
    win[pl.ds(x, 1), pl.ds(z, 1), :, pl.ds(pl.multiple_of(c * 512, 512), 512)] = half.reshape(1, 1, 112, 512)
    follow(streams, WEIGHT_ORDER)
    for wait in pending:
        wait()

    def flip():
        @pl.loop(0, NX)
        def _(n):
            for j in range(8):
                part = win[n, :, :, pl.ds(128 * j, 128)].reshape(896, 128)
                win_t[pl.ds(128 * j, 128), pl.ds(pl.multiple_of(n * 896, 128), 896)] = part.T
            for j in range(7):
                part = wout[n, :, :, :, pl.ds(512 * j, 512)].reshape(256, 512)
                wout_t[pl.ds(512 * j, 512), pl.ds(pl.multiple_of(n * 256, 256), 256)] = part.T

    @pl.when(seg > 0)
    def _():
        flip()

    def hop(step, k, part, src, dst, to):
        rows = pl.ds(pl.multiple_of(k * CHUNK, CHUNK), CHUNK)
        cols = pl.ds(part * WIDE, WIDE)
        return pltpu.make_async_remote_copy(
            src_ref=src.at[rows, cols], dst_ref=dst.at[rows, cols],
            send_sem=hop_send.at[step, k, part], recv_sem=hop_recv.at[step, k, part],
            device_id=(me, to), device_id_type=MESH,
        )

    gain = gain_ref[...]
    pooled[...] = jnp.zeros_like(pooled)

    @pl.loop(0, CHUNKS)
    def _(k):
        rows = pl.ds(pl.multiple_of(k * CHUNK, CHUNK), CHUNK)

        @pl.when(seg > 0)
        def _():
            for part in range(PARTS):
                hop(0, k, part, outb, kept, seg).wait_recv()

        for part in range(CHUNK // 16):
            sub = pl.ds(pl.multiple_of(k * CHUNK + part * 16, 16), 16)
            stream = kept[sub, :].astype(F32)
            scale = lax.rsqrt(jnp.mean(stream * stream, axis=-1, keepdims=True) + EPS)
            scales[sub, :] = jnp.broadcast_to(scale, (16, 128))
            normed[pl.ds(part * 16, 16), :] = (stream * scale * gain).astype(BF)
        for n in range(KVW // 256):
            cols = pl.ds(n * 256, 256)
            v = jnp.dot(normed[...], win[:, :, :, cols].reshape(D, 256), preferred_element_type=F32)
            pre[rows, cols] = v
            act[:, cols] = gelu(v).astype(BF)
        for n in range(PARTS):
            cols = pl.ds(n * WIDE, WIDE)
            v = jnp.dot(act[...], wout[:, :, :, :, cols].reshape(KVW, WIDE), preferred_element_type=F32)
            outb[rows, cols] = (kept[rows, cols].astype(F32) + v).astype(BF)

            @pl.when(seg < NY - 1)
            def _():
                hop(0, k, n, outb, kept, seg + 1).start()

        @pl.when(seg == NY - 1)
        def _():
            half = (k * CHUNK) // SEQ
            total = jnp.zeros((8, D), F32)
            for part in range(CHUNK // 16):
                sub = pl.ds(pl.multiple_of(k * CHUNK + part * 16, 16), 16)
                scaled = outb[sub, :].astype(F32) * weight_ref[sub, 0:1]
                total = total + scaled[0:8] + scaled[8:16]
            pooled[half] += total

    @pl.when(seg == 0)
    def _():
        flip()

    @pl.when(seg == NY - 1)
    def _():
        totals, invs = [], []
        for side in range(2):
            total = jnp.sum(pooled[side], axis=0, keepdims=True)
            inv = lax.rsqrt(jnp.sum(total * total, axis=-1, keepdims=True) + EPS)
            unit = total * inv
            for k in range(PACKS):
                pack[side, k : k + 1, :] = unit[:, k * 128 : (k + 1) * 128]
            pack[side, PACKS : PACKS + 4, :] = pos_ref[0:4, :]
            emb[pl.ds(x, 1), pl.ds(z, 1), pl.ds(c, 1), pl.ds(32 * side, 32), :] = pack[side].reshape(1, 1, 1, 32, 128)
            totals.append(total)
            invs.append(inv)
        waits = []
        follow([gather(EMB, colour, True, waits) for colour in (1, 0)], EMB_ORDER)
        for wait in waits:
            wait()
        flat = emb.reshape(NQ * 64, 128)
        for k in range(PACKS):
            cols = pl.ds(k * 128, 128)
            embs[0, :, cols] = flat[pl.ds(k, NQ, stride=64), :]
            embs[1, :, cols] = flat[pl.ds(32 + k, NQ, stride=64), :]
        onehot = flat[pl.ds(PACKS, NQ, stride=64), :][:, 0:NQ]
        logits = lax.dot_general(embs[0], embs[1], NT, precision=HI, preferred_element_type=F32) / TEMP
        expo = jnp.exp(logits - jnp.max(logits, axis=1, keepdims=True))
        probs = expo / jnp.sum(expo, axis=1, keepdims=True)
        dlogits = (probs - onehot) / NQ
        ii = lax.broadcasted_iota(jnp.int32, (NQ, NQ), 0)
        jj = lax.broadcasted_iota(jnp.int32, (NQ, NQ), 1)
        row = jnp.sum(jnp.where(ii == me, dlogits, 0.0), axis=0, keepdims=True)
        col = jnp.sum(jnp.where(jj == me, dlogits, 0.0), axis=1, keepdims=True)
        row = jnp.broadcast_to(row, (8, NQ))
        dq = jnp.dot(row, embs[1], precision=HI, preferred_element_type=F32)[0:1] / TEMP
        dp = jnp.sum(col * embs[0], axis=0, keepdims=True) / TEMP
        for side, demb in enumerate((dq, dp)):
            inv, total = invs[side], totals[side]
            along = jnp.sum(total * demb, axis=-1, keepdims=True)
            grad = inv * demb - total * (inv * inv * inv) * along
            for part in range(SEQ // 16):
                sub = pl.ds(side * SEQ + part * 16, 16)
                gin[sub, :] = (weight_ref[sub, 0:1] * grad).astype(BF)

    gacc[...] = jnp.zeros_like(gacc)

    @pl.loop(0, CHUNKS)
    def _(k):
        rows = pl.ds(pl.multiple_of(k * CHUNK, CHUNK), CHUNK)

        @pl.when(seg < NY - 1)
        def _():
            for part in range(PARTS):
                hop(1, k, part, outb, gin, seg).wait_recv()
                hop(0, k, part, outb, kept, seg).wait_send()

        along = jnp.zeros((CHUNK, 1), F32)
        for n in range(KVW // 256):
            cols = pl.ds(n * 256, 256)
            back = jnp.dot(gin[rows, :], wout_t[:, cols], preferred_element_type=F32)
            v = pre[rows, cols]
            d = back * gelu_slope(v)
            along = along + jnp.sum(d * v, axis=-1, keepdims=True)
            dpre[:, cols] = d.astype(BF)
        mean = along * (1.0 / D)
        scale = scales[rows, 0:1]
        for n in range(PARTS):
            cols = pl.ds(n * WIDE, WIDE)
            dnormed = jnp.dot(dpre[...], win_t[:, cols], preferred_element_type=F32)
            unit = kept[rows, cols].astype(F32) * scale
            both = dnormed * unit
            gacc[:, cols] += both[0:8] + both[8:16] + both[16:24] + both[24:32]
            res = gin[rows, cols].astype(F32) + scale * (dnormed * gain_ref[:, cols] - unit * mean)
            outb[rows, cols] = res.astype(BF)

            @pl.when(seg > 0)
            def _():
                hop(1, k, n, outb, gin, seg - 1).start()

    qgrad_ref[...] = outb[pl.ds(0, SEQ), :].reshape(1, 1, SEQ, D)
    pgrad_ref[...] = outb[pl.ds(SEQ, SEQ), :].reshape(1, 1, SEQ, D)

    def reduce(step, buf, at, peers):
        ops = []
        for j, (target, source) in enumerate(peers):
            op = pltpu.make_async_remote_copy(
                src_ref=buf.at[at], dst_ref=buf.at[at],
                send_sem=red_send.at[step, j], recv_sem=red_recv.at[step, j],
                device_id=target, device_id_type=MESH,
            )
            op.start()
            ops.append(op.wait_send)
            ops.append(pltpu.make_async_remote_copy(
                src_ref=buf.at[source], dst_ref=buf.at[source],
                send_sem=red_send.at[step, j], recv_sem=red_recv.at[step, j],
                device_id=target, device_id_type=MESH,
            ).wait_recv)
        for op in ops:
            op()

    at = x * NC + c
    gsum = jnp.sum(gacc[...], axis=0, keepdims=True)
    for k in range(PACKS):
        pack[0, k : k + 1, :] = gsum[:, k * 128 : (k + 1) * 128]
    near[at] = pack[0]
    peers = []
    for dx in range(NX):
        for other in range(NC):
            if dx or other:
                pc = c if other == 0 else 1 - c
                peers.append((dev(xo(dx), z, pc), xo(-dx) * NC + pc))
    reduce(0, near, at, peers)
    far[z] = jnp.sum(near[...], axis=0)
    reduce(1, far, z, [(dev(x, zo(dz), c), zo(-dz)) for dz in range(1, NZ)])
    pack[1] = jnp.sum(far[...], axis=0)
    for k in range(PACKS):
        gsum_ref[0:1, k * 128 : (k + 1) * 128] = pack[1, k : k + 1, :]

    @pl.when(seg > 0)
    def _():
        for k in range(CHUNKS):
            for part in range(PARTS):
                hop(1, k, part, outb, gin, seg).wait_send()


def local(queries_in, passages_in, query_len, passage_len, positive, norm_gain, w_in, w_out):
    lengths = jnp.concatenate([query_len, passage_len])
    mask = (jnp.arange(SEQ, dtype=jnp.int32)[None, :] < lengths[:, None]).astype(F32)
    weights = mask / lengths.astype(F32)[:, None]
    weights = jnp.broadcast_to(weights.reshape(2 * SEQ, 1), (2 * SEQ, 128))
    chosen = (lax.broadcasted_iota(jnp.int32, (8, 128), 1) == positive[0]).astype(F32)
    vmem = pl.BlockSpec(memory_space=pltpu.VMEM)
    rows = 2 * SEQ
    return pl.pallas_call(
        kernel,
        out_shape=(
            jax.ShapeDtypeStruct((1, 1, SEQ, D), BF),
            jax.ShapeDtypeStruct((1, 1, SEQ, D), BF),
            jax.ShapeDtypeStruct((1, D), F32),
        ),
        in_specs=[vmem] * 7,
        out_specs=(vmem,) * 3,
        scratch_shapes=[
            pltpu.VMEM((NX, NZ, 112, KVW), BF),
            pltpu.VMEM((NX, NZ, NC, 16, D), BF),
            pltpu.VMEM((KVW, D), BF),
            pltpu.VMEM((D, KVW), BF),
            pltpu.VMEM((NX, NZ, NC, 64, 128), F32),
            pltpu.VMEM((2, NQ, D), F32),
            pltpu.VMEM((56, KVW), BF),
            pltpu.VMEM((rows, D), BF),
            pltpu.VMEM((rows, KVW), F32),
            pltpu.VMEM((rows, 128), F32),
            pltpu.VMEM((CHUNK, D), BF),
            pltpu.VMEM((CHUNK, KVW), BF),
            pltpu.VMEM((rows, D), BF),
            pltpu.VMEM((rows, D), BF),
            pltpu.VMEM((CHUNK, KVW), BF),
            pltpu.VMEM((8, D), F32),
            pltpu.VMEM((2, 8, D), F32),
            pltpu.VMEM((2, 32, 128), F32),
            pltpu.VMEM((NX * NC, 32, 128), F32),
            pltpu.VMEM((NZ, 32, 128), F32),
            pltpu.SemaphoreType.DMA((3, 54)),
            pltpu.SemaphoreType.DMA((3, 54)),
            pltpu.SemaphoreType.DMA((2,)),
            pltpu.SemaphoreType.DMA((2, CHUNKS, PARTS)),
            pltpu.SemaphoreType.DMA((2, CHUNKS, PARTS)),
            pltpu.SemaphoreType.DMA((2, 7)),
            pltpu.SemaphoreType.DMA((2, 7)),
        ],
        compiler_params=pltpu.CompilerParams(
            collective_id=0, has_side_effects=True, vmem_limit_bytes=56 * 1024 * 1024
        ),
        name="embedder_window",
    )(queries_in, passages_in, norm_gain, weights, chosen, w_in[0], w_out[0])


def solution(mesh):
    return jax.shard_map(
        local,
        mesh=mesh,
        in_specs=(
            P("dp", None, None),
            P("dp", None, None),
            P("dp"),
            P("dp"),
            P("dp"),
            P("segment", None),
            P("segment", "dp", None),
            P("segment", "dp", None),
        ),
        out_specs=(
            P("segment", "dp", None, None),
            P("segment", "dp", None, None),
            P("segment", None),
        ),
        check_vma=False,
    )
```

```python
import math

import jax
import jax.numpy as jnp
from jax import lax
from jax.experimental import pallas as pl
from jax.experimental.pallas import tpu as pltpu
from jax.sharding import PartitionSpec as P

MESH = pl.DeviceIdType.MESH
BF, F32 = jnp.bfloat16, jnp.float32
HI = lax.Precision.HIGHEST
D, KVW, SEQ, NQ = 3584, 1024, 64, 64
NX, NZ, NC, NY = 4, 8, 2, 4
TEMP = 0.02
CHUNK = 32
CHUNKS = 2 * SEQ // CHUNK
PARTS = 4
WIDE = D // PARTS
PACKS = D // 128
WEIGHT_ORDER = (
    2, 3, 0, 1, 2, 3, 0, 0, 1, 2, 2, 3, 2, 0, 0, 2, 0, 2, 0, 0, 1, 3, 2, 2, 2, 0, 0, 0, 2, 2, 2, 0, 1, 3, 1, 2, 0, 3,
)
EPS = 1e-06
C0 = math.sqrt(2.0 / math.pi)
EMB_Q, EMB_P, W_IN, W_OUT = 0, 1, 2, 3
ALL = slice(None)
NT = (((1,), (1,)), ((), ()))


def gelu(v):
    return 0.5 * v * (1.0 + jnp.tanh(C0 * (v + 0.044715 * v * v * v)))


def gelu_slope(v):
    t = jnp.tanh(C0 * (v + 0.044715 * v * v * v))
    return 0.5 * (1.0 + t) + 0.5 * v * (1.0 - t * t) * C0 * (1.0 + 3.0 * 0.044715 * v * v)


def kernel(
    qlen_ref, plen_ref, pos_ref, queries_ref, passages_ref, gain_ref, wi_ref, wo_ref,
    grad_ref, gsum_ref,
    win, wout, win_t, wout_t, emb, embs, pair, kept, pre, scales, normed, act, outb, gin, dpre, gacc, pooled,
    pack, near, far,
    ag_send, ag_recv, pair_sem, tok_sem, out_sem, hop_send, hop_recv, red_send, red_recv,
):
    me = lax.axis_index("dp")
    seg = lax.axis_index("segment")
    x, z, c = me // (NZ * NC), (me // NC) % NZ, me % NC

    def dev(px, pz, pc):
        return ((px * NZ + pz) * NC + pc, seg)

    def xo(by):
        return (x + by + NX) % NX

    def zo(by):
        return (z + by + NZ) % NZ

    barrier = pltpu.get_barrier_semaphore()
    mates = [dev(xo(dx), z, pc) for dx in range(NX) for pc in (c, 1 - c)][1:]
    mates += [dev(x, zo(dz), c) for dz in range(1, NZ)]
    mates += [(me, (seg + by) % NY) for by in (1, NY - 1)]
    for mate in mates:
        pl.semaphore_signal(barrier, inc=1, device_id=mate, device_id_type=MESH)
    pl.semaphore_wait(barrier, len(mates))

    def piece(tensor, colour, xs, zs, pc):
        if tensor == W_IN:
            rows = pl.ds(0, 48) if colour == 0 else pl.ds(48, 64)
            return win.at[xs, zs, rows, pl.ds(pl.multiple_of(pc * 512, 512), 512)]
        if tensor == W_OUT:
            cols = pl.ds(0, 1536) if colour == 0 else pl.ds(1536, 2048)
            return wout.at[xs, zs, pl.ds(pc, 1), :, cols]
        return emb.at[xs, zs, pl.ds(pc, 1), pl.ds(16 * (2 * tensor + colour), 16), :]

    def copy_of(tensor, slot, ref, target):
        return pltpu.make_async_remote_copy(
            src_ref=ref, dst_ref=ref,
            send_sem=ag_send.at[tensor, slot], recv_sem=ag_recv.at[tensor, slot],
            device_id=target, device_id_type=MESH,
        )

    def one(at):
        return pl.ds(at, 1)

    def gather(tensor, colour, plus, pending):
        def send(slot, xs, zs, target):
            op = copy_of(tensor, slot, piece(tensor, colour, xs, zs, c), target)
            op.start()
            pending.append(op.wait_send)

        def got(slot, xs, zs):
            copy_of(tensor, slot, piece(tensor, colour, xs, zs, c), dev(x, z, 1 - c)).wait_recv()

        def pass_on(slot, xs, zs):
            send(slot, xs, zs, dev(x, z, 1 - c))
            other = copy_of(tensor, slot, piece(tensor, colour, xs, zs, 1 - c), dev(x, z, 1 - c))
            pending.append(other.wait_recv)

        up, down = dev(x, zo(1), c), dev(x, zo(-1), c)
        right, left = dev(xo(1), z, c), dev(xo(-1), z, c)
        if colour == 0:
            for dx in range(1, NX):
                send(dx - 1, one(x), one(z), dev(xo(dx), z, c))
            yield
            for dx in range(1, NX):
                got(dx - 1, one(xo(-dx)), one(z))
            send(3, ALL, one(z), up)
            send(4, ALL, one(z), down)
            pass_on(42, ALL, one(z))
            for step in range(1, 4):
                yield
                got(1 + 2 * step, ALL, one(zo(-step)))
                if step < 3:
                    send(3 + 2 * step, ALL, one(zo(-step)), up)
                else:
                    send(9, pl.ds(0, 2), one(zo(-3)), up)
                got(2 + 2 * step, ALL, one(zo(step)))
                if step < 3:
                    send(4 + 2 * step, ALL, one(zo(step)), down)
                else:
                    send(10, pl.ds(2, 2), one(zo(3)), down)
                pass_on(41 + 2 * step, ALL, one(zo(-step)))
                pass_on(42 + 2 * step, ALL, one(zo(step)))
            yield
            got(9, pl.ds(0, 2), one(zo(-4)))
            got(10, pl.ds(2, 2), one(zo(4)))
            pass_on(49, ALL, one(zo(4)))
            return
        offsets = (0, -1, 1, -2, 2, -3, 3, 4)

        def sideways(j):
            at = one(zo(offsets[j]))
            send(18 + j, one(x), at, right)
            send(26 + j, one(x), at, left)

        send(11, one(x), one(z), up)
        send(12, one(x), one(z), down)
        sideways(0)
        for step in range(1, 4):
            yield
            got(9 + 2 * step, one(x), one(zo(-step)))
            if step < 3:
                send(11 + 2 * step, one(x), one(zo(-step)), up)
            elif plus:
                send(17, one(x), one(zo(-3)), up)
            sideways(2 * step - 1)
            got(10 + 2 * step, one(x), one(zo(step)))
            if step < 3:
                send(12 + 2 * step, one(x), one(zo(step)), down)
            elif not plus:
                send(17, one(x), one(zo(3)), down)
            sideways(2 * step)
        yield
        got(17, one(x), one(zo(4)))
        sideways(7)
        pass_on(50, one(x), ALL)
        for j, by in enumerate(offsets):
            yield
            got(18 + j, one(xo(-1)), one(zo(by)))
            got(26 + j, one(xo(1)), one(zo(by)))
            if j % 2 == 0:
                send(34 + j, one(xo(-1)), one(zo(by)), right)
            else:
                send(34 + j, one(xo(1)), one(zo(by)), left)
        pass_on(51, one(xo(-1)), ALL)
        pass_on(52, one(xo(1)), ALL)
        yield
        for j, by in enumerate(offsets):
            got(34 + j, one(xo(2)), one(zo(by)))
        pass_on(53, one(xo(2)), ALL)

    def exchange(tensor):
        def own_first():
            ops = [(0, by - 1, one(x), one(z), dev(xo(by), z, c), one(xo(-by)), one(z)) for by in range(1, NX)]
            return ops + [
                (1, 2 + by, one(x), one(z), dev(x, zo(by), c), one(x), one(zo(-by))) for by in range(1, NZ)
            ]

        def along_z():
            return [(0, 9 + by, ALL, one(z), dev(x, zo(by), c), ALL, one(zo(-by))) for by in range(1, NZ)]

        def along_x():
            return [(1, 16 + by, one(x), ALL, dev(xo(by), z, c), one(xo(-by)), ALL) for by in range(1, NX)]

        def to_mate():
            return [(colour, 20 + colour, ALL, ALL, dev(x, z, 1 - c), ALL, ALL) for colour in range(2)]

        def send(ops):
            for colour, slot, xs, zs, target, _, _ in ops:
                copy_of(tensor, slot, piece(tensor, colour, xs, zs, c), target).start()

        def got(ops, pc=c):
            for colour, slot, _, _, target, xs, zs in ops:
                copy_of(tensor, slot, piece(tensor, colour, xs, zs, pc), target).wait_recv()

        def begin():
            send(own_first())

        def middle():
            ops = own_first()
            got(ops[: NX - 1])
            send(along_z())
            got(ops[NX - 1 :])
            send(along_x())

        def end():
            got(along_x())
            send(to_mate()[1:])
            got(along_z())
            send(to_mate()[:1])
            got(to_mate()[::-1], 1 - c)
            for colour, slot, xs, zs, target, _, _ in own_first() + along_z() + along_x() + to_mate():
                copy_of(tensor, slot, piece(tensor, colour, xs, zs, c), target).wait_send()

        return begin, middle, end

    def follow(streams, order):
        for at in order:
            next(streams[at], None)

    pending = []
    wout[pl.ds(x, 1), pl.ds(z, 1), pl.ds(c, 1)] = wo_ref[...].reshape(1, 1, 1, 16, D)
    streams = [
        gather(tensor, colour, tensor == W_IN, pending) for tensor in (W_OUT, W_IN) for colour in (1, 0)
    ]
    follow(streams, (0, 1))
    swap = pltpu.make_async_remote_copy(
        src_ref=wi_ref, dst_ref=pair, send_sem=pair_sem.at[0], recv_sem=pair_sem.at[1],
        device_id=dev(x, z, 1 - c), device_id_type=MESH,
    )
    swap.start()

    tokens = [
        pltpu.make_async_copy(ref.at[0], kept.at[pl.ds(side * SEQ, SEQ)], tok_sem.at[side])
        for side, ref in enumerate((queries_ref, passages_ref))
    ]

    @pl.when(seg == 0)
    def _():
        for op in tokens:
            op.start()

    swap.wait()
    mine, theirs = wi_ref[...].astype(F32), pair[...].astype(F32)
    both = jnp.concatenate(
        [jnp.where(c == 0, mine, theirs), jnp.where(c == 0, theirs, mine)], axis=0
    )
    half = jnp.where(c == 0, both[:, :512], both[:, 512:]).astype(BF)
    win[pl.ds(x, 1), pl.ds(z, 1), :, pl.ds(pl.multiple_of(c * 512, 512), 512)] = half.reshape(1, 1, 112, 512)
    follow(streams, WEIGHT_ORDER)
    for wait in pending:
        wait()

    def flip():
        @pl.loop(0, NX)
        def _(n):
            for j in range(8):
                part = win[n, :, :, pl.ds(128 * j, 128)].reshape(896, 128)
                win_t[pl.ds(128 * j, 128), pl.ds(pl.multiple_of(n * 896, 128), 896)] = part.T
            for j in range(7):
                part = wout[n, :, :, :, pl.ds(512 * j, 512)].reshape(256, 512)
                wout_t[pl.ds(512 * j, 512), pl.ds(pl.multiple_of(n * 256, 256), 256)] = part.T

    @pl.when(seg > 0)
    def _():
        flip()

    @pl.when(seg == 0)
    def _():
        for op in tokens:
            op.wait()

    def hop(step, k, part, src, dst, to):
        rows = pl.ds(pl.multiple_of(k * CHUNK, CHUNK), CHUNK)
        cols = pl.ds(part * WIDE, WIDE)
        return pltpu.make_async_remote_copy(
            src_ref=src.at[rows, cols], dst_ref=dst.at[rows, cols],
            send_sem=hop_send.at[step, k, part], recv_sem=hop_recv.at[step, k, part],
            device_id=(me, to), device_id_type=MESH,
        )

    gain = gain_ref[...]
    pooled[...] = jnp.zeros_like(pooled)

    def weight(start, count, side):
        length = jnp.where(side == 0, qlen_ref[0], plen_ref[0])
        at = lax.broadcasted_iota(jnp.int32, (count, 1), 0) + start
        return jnp.where(at < length, 1.0, 0.0) / length.astype(F32)

    def norm_of(side):
        total = jnp.sum(pooled[side], axis=0, keepdims=True)
        return total, lax.rsqrt(jnp.sum(total * total, axis=-1, keepdims=True) + EPS)

    def embed(side):
        total, inv = norm_of(side)
        unit = total * inv
        for k in range(PACKS):
            pack[side, k : k + 1, :] = unit[:, k * 128 : (k + 1) * 128]
        spot = lax.broadcasted_iota(jnp.int32, (32 - PACKS, 128), 1)
        pack[side, PACKS:32, :] = jnp.where(spot == pos_ref[0], 1.0, 0.0)
        emb[pl.ds(x, 1), pl.ds(z, 1), pl.ds(c, 1), pl.ds(32 * side, 32), :] = pack[side].reshape(1, 1, 1, 32, 128)
        return total, inv

    query_steps, passage_steps = exchange(EMB_Q), exchange(EMB_P)

    @pl.loop(0, CHUNKS)
    def _(k):
        rows = pl.ds(pl.multiple_of(k * CHUNK, CHUNK), CHUNK)

        @pl.when(seg > 0)
        def _():
            for part in range(PARTS):
                hop(0, k, part, outb, kept, seg).wait_recv()

        for part in range(CHUNK // 16):
            sub = pl.ds(pl.multiple_of(k * CHUNK + part * 16, 16), 16)
            stream = kept[sub, :].astype(F32)
            scale = lax.rsqrt(jnp.mean(stream * stream, axis=-1, keepdims=True) + EPS)
            scales[sub, :] = jnp.broadcast_to(scale, (16, 128))
            normed[pl.ds(part * 16, 16), :] = (stream * scale * gain).astype(BF)
        for n in range(KVW // 256):
            cols = pl.ds(n * 256, 256)
            v = jnp.dot(normed[...], win[:, :, :, cols].reshape(D, 256), preferred_element_type=F32)
            pre[rows, cols] = v
            act[:, cols] = gelu(v).astype(BF)

        def rise(n):
            cols = pl.ds(n * WIDE, WIDE)
            return jnp.dot(act[...], wout[:, :, :, :, cols].reshape(KVW, WIDE), preferred_element_type=F32)

        ahead = rise(0)
        for n in range(PARTS):
            cols = pl.ds(n * WIDE, WIDE)
            v, ahead = ahead, rise(n + 1) if n + 1 < PARTS else None
            outb[rows, cols] = (kept[rows, cols].astype(F32) + v).astype(BF)

            @pl.when(seg < NY - 1)
            def _():
                hop(0, k, n, outb, kept, seg + 1).start()

        @pl.when(seg == NY - 1)
        def _():
            side = (k * CHUNK) // SEQ
            total = jnp.zeros((8, D), F32)
            for part in range(CHUNK // 16):
                sub = pl.ds(pl.multiple_of(k * CHUNK + part * 16, 16), 16)
                scaled = outb[sub, :].astype(F32) * weight(part * 16 + (k * CHUNK) % SEQ, 16, side)
                total = total + scaled[0:8] + scaled[8:16]
            pooled[side] += total

            @pl.when(k == CHUNKS // 2 - 1)
            def _():
                embed(0)
                query_steps[0]()

            @pl.when(k == CHUNKS // 2)
            def _():
                query_steps[1]()

    @pl.when(seg == 0)
    def _():
        flip()

    @pl.when(seg == NY - 1)
    def _():
        flat = emb.reshape(NQ * 64, 128)

        def unpack(side):
            for k in range(PACKS):
                embs[side, :, pl.ds(k * 128, 128)] = flat[pl.ds(32 * side + k, NQ, stride=64), :]

        passage = embed(1)
        passage_steps[0]()
        query_steps[2]()
        query = norm_of(0)
        unpack(0)
        passage_steps[1]()
        passage_steps[2]()
        unpack(1)
        onehot = flat[pl.ds(PACKS, NQ, stride=64), :][:, 0:NQ]
        logits = lax.dot_general(embs[0], embs[1], NT, precision=HI, preferred_element_type=F32) / TEMP
        expo = jnp.exp(logits - jnp.max(logits, axis=1, keepdims=True))
        probs = expo / jnp.sum(expo, axis=1, keepdims=True)
        dlogits = (probs - onehot) / NQ
        ii = lax.broadcasted_iota(jnp.int32, (NQ, NQ), 0)
        jj = lax.broadcasted_iota(jnp.int32, (NQ, NQ), 1)
        row = jnp.sum(jnp.where(ii == me, dlogits, 0.0), axis=0, keepdims=True)
        col = jnp.sum(jnp.where(jj == me, dlogits, 0.0), axis=1, keepdims=True)
        row = jnp.broadcast_to(row, (8, NQ))
        dq = jnp.dot(row, embs[1], precision=HI, preferred_element_type=F32)[0:1] / TEMP
        dp = jnp.sum(col * embs[0], axis=0, keepdims=True) / TEMP
        for side, (demb, (total, inv)) in enumerate(((dq, query), (dp, passage))):
            along = jnp.sum(total * demb, axis=-1, keepdims=True)
            grad = inv * demb - total * (inv * inv * inv) * along
            for part in range(SEQ // 16):
                sub = pl.ds(side * SEQ + part * 16, 16)
                gin[sub, :] = (weight(part * 16, 16, side) * grad).astype(BF)

    def store(k):
        rows = pl.ds(pl.multiple_of(k * CHUNK, CHUNK), CHUNK)
        return pltpu.make_async_copy(outb.at[rows], grad_ref.at[rows], out_sem.at[k])

    gacc[...] = jnp.zeros_like(gacc)

    @pl.loop(0, CHUNKS)
    def _(k):
        rows = pl.ds(pl.multiple_of(k * CHUNK, CHUNK), CHUNK)

        @pl.when(seg < NY - 1)
        def _():
            for part in range(PARTS):
                hop(1, k, part, outb, gin, seg).wait_recv()
                hop(0, k, part, outb, kept, seg).wait_send()

        along = jnp.zeros((CHUNK, 1), F32)
        for n in range(KVW // 256):
            cols = pl.ds(n * 256, 256)
            back = jnp.dot(gin[rows, :], wout_t[:, cols], preferred_element_type=F32)
            v = pre[rows, cols]
            d = back * gelu_slope(v)
            along = along + jnp.sum(d * v, axis=-1, keepdims=True)
            dpre[:, cols] = d.astype(BF)
        mean = along * (1.0 / D)
        scale = scales[rows, 0:1]

        def fall(n):
            return jnp.dot(dpre[...], win_t[:, pl.ds(n * WIDE, WIDE)], preferred_element_type=F32)

        ahead = fall(0)
        for n in range(PARTS):
            cols = pl.ds(n * WIDE, WIDE)
            dnormed, ahead = ahead, fall(n + 1) if n + 1 < PARTS else None
            unit = kept[rows, cols].astype(F32) * scale
            both = dnormed * unit
            gacc[:, cols] += both[0:8] + both[8:16] + both[16:24] + both[24:32]
            res = gin[rows, cols].astype(F32) + scale * (dnormed * gain_ref[:, cols] - unit * mean)
            outb[rows, cols] = res.astype(BF)

            @pl.when(seg > 0)
            def _():
                hop(1, k, n, outb, gin, seg - 1).start()

        store(k).start()

    def reduce(step, buf, at, peers):
        ops = []
        for j, (target, source) in enumerate(peers):
            op = pltpu.make_async_remote_copy(
                src_ref=buf.at[at], dst_ref=buf.at[at],
                send_sem=red_send.at[step, j], recv_sem=red_recv.at[step, j],
                device_id=target, device_id_type=MESH,
            )
            op.start()
            ops.append(op.wait_send)
            ops.append(pltpu.make_async_remote_copy(
                src_ref=buf.at[source], dst_ref=buf.at[source],
                send_sem=red_send.at[step, j], recv_sem=red_recv.at[step, j],
                device_id=target, device_id_type=MESH,
            ).wait_recv)
        for op in ops:
            op()

    at = x * NC + c
    gsum = jnp.sum(gacc[...], axis=0, keepdims=True)
    for k in range(PACKS):
        pack[0, k : k + 1, :] = gsum[:, k * 128 : (k + 1) * 128]
    near[at] = pack[0]
    peers = []
    for dx in range(NX):
        for other in range(NC):
            if dx or other:
                pc = c if other == 0 else 1 - c
                peers.append((dev(xo(dx), z, pc), xo(-dx) * NC + pc))
    reduce(0, near, at, peers)
    far[z] = jnp.sum(near[...], axis=0)
    reduce(1, far, z, [(dev(x, zo(dz), c), zo(-dz)) for dz in range(1, NZ)])
    gsum_ref[...] = jnp.sum(far[...], axis=0)
    for k in range(CHUNKS):
        store(k).wait()

    @pl.when(seg > 0)
    def _():
        for k in range(CHUNKS):
            for part in range(PARTS):
                hop(1, k, part, outb, gin, seg).wait_send()


def local(queries_in, passages_in, query_len, passage_len, positive, norm_gain, w_in, w_out):
    vmem, hbm = pl.BlockSpec(memory_space=pltpu.VMEM), pl.BlockSpec(memory_space=pl.ANY)
    smem = pl.BlockSpec(memory_space=pltpu.SMEM)
    rows = 2 * SEQ
    grads, gains = pl.pallas_call(
        kernel,
        out_shape=(
            jax.ShapeDtypeStruct((rows, D), BF),
            jax.ShapeDtypeStruct((32, 128), F32),
        ),
        in_specs=[smem] * 3 + [hbm] * 2 + [vmem] * 3,
        out_specs=(hbm, vmem),
        scratch_shapes=[
            pltpu.VMEM((NX, NZ, 112, KVW), BF),
            pltpu.VMEM((NX, NZ, NC, 16, D), BF),
            pltpu.VMEM((KVW, D), BF),
            pltpu.VMEM((D, KVW), BF),
            pltpu.VMEM((NX, NZ, NC, 64, 128), F32),
            pltpu.VMEM((2, NQ, D), F32),
            pltpu.VMEM((56, KVW), BF),
            pltpu.VMEM((rows, D), BF),
            pltpu.VMEM((rows, KVW), F32),
            pltpu.VMEM((rows, 128), F32),
            pltpu.VMEM((CHUNK, D), BF),
            pltpu.VMEM((CHUNK, KVW), BF),
            pltpu.VMEM((rows, D), BF),
            pltpu.VMEM((rows, D), BF),
            pltpu.VMEM((CHUNK, KVW), BF),
            pltpu.VMEM((8, D), F32),
            pltpu.VMEM((2, 8, D), F32),
            pltpu.VMEM((2, 32, 128), F32),
            pltpu.VMEM((NX * NC, 32, 128), F32),
            pltpu.VMEM((NZ, 32, 128), F32),
            pltpu.SemaphoreType.DMA((4, 54)),
            pltpu.SemaphoreType.DMA((4, 54)),
            pltpu.SemaphoreType.DMA((2,)),
            pltpu.SemaphoreType.DMA((2,)),
            pltpu.SemaphoreType.DMA((CHUNKS,)),
            pltpu.SemaphoreType.DMA((2, CHUNKS, PARTS)),
            pltpu.SemaphoreType.DMA((2, CHUNKS, PARTS)),
            pltpu.SemaphoreType.DMA((2, 7)),
            pltpu.SemaphoreType.DMA((2, 7)),
        ],
        compiler_params=pltpu.CompilerParams(
            collective_id=0, has_side_effects=True, vmem_limit_bytes=56 * 1024 * 1024
        ),
        name="embedder_window",
    )(query_len, passage_len, positive, queries_in, passages_in, norm_gain, w_in[0], w_out[0])
    grads = grads.reshape(2, 1, 1, SEQ, D)
    return grads[0], grads[1], gains[:PACKS].reshape(1, D)


def solution(mesh):
    return jax.shard_map(
        local,
        mesh=mesh,
        in_specs=(
            P("dp", None, None),
            P("dp", None, None),
            P("dp"),
            P("dp"),
            P("dp"),
            P("segment", None),
            P("segment", "dp", None),
            P("segment", "dp", None),
        ),
        out_specs=(
            P("segment", "dp", None, None),
            P("segment", "dp", None, None),
            P("segment", None),
        ),
        check_vma=False,
    )
```

```python
import math

import jax
import jax.numpy as jnp
from jax import lax
from jax.experimental import pallas as pl
from jax.experimental.pallas import tpu as pltpu
from jax.sharding import PartitionSpec as P

MESH = pl.DeviceIdType.MESH
BF, F32 = jnp.bfloat16, jnp.float32
HI = lax.Precision.HIGHEST
D, KVW, SEQ, NQ = 3584, 1024, 64, 64
NX, NZ, NC, NY = 4, 8, 2, 4
TEMP = 0.02
CHUNK = 32
CHUNKS = 2 * SEQ // CHUNK
PARTS = 4
WIDE = D // PARTS
PACKS = D // 128
FAR_X, FAR_Z = (2, 1, 3), (4, 3, 5, 2, 6, 1, 7)
WEIGHT_ORDER = (
    2, 3, 0, 1, 2, 3, 0, 1, 2, 2, 0, 3, 2, 0, 0, 0, 2, 0, 2, 1, 0, 3, 2, 2, 0, 2, 2, 0, 0, 0, 1, 2, 2, 3, 2, 0, 1, 3,
)
EPS = 1e-06
C0 = math.sqrt(2.0 / math.pi)
EMB_Q, EMB_P, W_IN, W_OUT = 0, 1, 2, 3
ALL = slice(None)
NT = (((1,), (1,)), ((), ()))


def gelu(v):
    return 0.5 * v * (1.0 + jnp.tanh(C0 * (v + 0.044715 * v * v * v)))


def gelu_slope(v):
    t = jnp.tanh(C0 * (v + 0.044715 * v * v * v))
    return 0.5 * (1.0 + t) + 0.5 * v * (1.0 - t * t) * C0 * (1.0 + 3.0 * 0.044715 * v * v)


def kernel(
    qlen_ref, plen_ref, pos_ref, queries_ref, passages_ref, gain_hbm, wi_hbm, wo_hbm,
    grad_ref, gsum_ref,
    win, wout, win_t, wout_t, emb, embs, gain_ref, wi_ref, pair, kept, pre, scales, act, outb, gin, dpre, gacc, pooled,
    pack, near, far,
    ag_send, ag_recv, pair_sem, tok_sem, hop_send, hop_recv, red_send, red_recv,
):
    me = lax.axis_index("dp")
    seg = lax.axis_index("segment")
    x, z, c = me // (NZ * NC), (me // NC) % NZ, me % NC

    def dev(px, pz, pc):
        return ((px * NZ + pz) * NC + pc, seg)

    def xo(by):
        return (x + by + NX) % NX

    def zo(by):
        return (z + by + NZ) % NZ

    own = [
        pltpu.make_async_copy(src, dst, tok_sem.at[2 + j])
        for j, (src, dst) in enumerate(((wo_hbm, wout.at[x, z, c]), (wi_hbm, wi_ref), (gain_hbm, gain_ref)))
    ]
    for op in own:
        op.start()
    tokens = [
        pltpu.make_async_copy(ref.at[0], kept.at[pl.ds(side * SEQ, SEQ)], tok_sem.at[side])
        for side, ref in enumerate((queries_ref, passages_ref))
    ]

    @pl.when(seg == 0)
    def _():
        for op in tokens:
            op.start()

    barrier = pltpu.get_barrier_semaphore()
    mates = [dev(xo(dx), z, pc) for dx in range(NX) for pc in (c, 1 - c)][1:]
    mates += [dev(x, zo(dz), c) for dz in range(1, NZ)]
    mates += [(me, (seg + by) % NY) for by in (1, NY - 1)]
    for mate in mates:
        pl.semaphore_signal(barrier, inc=1, device_id=mate, device_id_type=MESH)
    pl.semaphore_wait(barrier, len(mates))

    def piece(tensor, colour, xs, zs, pc):
        if tensor == W_IN:
            rows = pl.ds(0, 48) if colour == 0 else pl.ds(48, 64)
            return win.at[xs, zs, rows, pl.ds(pl.multiple_of(pc * 512, 512), 512)]
        if tensor == W_OUT:
            cols = pl.ds(0, 1536) if colour == 0 else pl.ds(1536, 2048)
            return wout.at[xs, zs, pl.ds(pc, 1), :, cols]
        rows = pl.ds(32 * tensor, 8) if colour == 0 else pl.ds(32 * tensor + 8, 24)
        return emb.at[xs, zs, pl.ds(pc, 1), rows, :]

    def copy_of(tensor, slot, ref, target):
        return pltpu.make_async_remote_copy(
            src_ref=ref, dst_ref=ref,
            send_sem=ag_send.at[tensor, slot], recv_sem=ag_recv.at[tensor, slot],
            device_id=target, device_id_type=MESH,
        )

    def one(at):
        return pl.ds(at, 1)

    def gather(tensor, colour, plus):
        def send(slot, xs, zs, target):
            op = copy_of(tensor, slot, piece(tensor, colour, xs, zs, c), target)
            op.start()
            unsent.append(op.wait_send)

        def got(slot, xs, zs):
            copy_of(tensor, slot, piece(tensor, colour, xs, zs, c), dev(x, z, 1 - c)).wait_recv()

        def pass_on(slot, xs, zs):
            send(slot, xs, zs, dev(x, z, 1 - c))
            other = copy_of(tensor, slot, piece(tensor, colour, xs, zs, 1 - c), dev(x, z, 1 - c))
            pending.append(other.wait_recv)

        up, down = dev(x, zo(1), c), dev(x, zo(-1), c)
        right, left = dev(xo(1), z, c), dev(xo(-1), z, c)
        if colour == 0:
            for dx in range(1, NX):
                send(dx - 1, one(x), one(z), dev(xo(dx), z, c))
            yield
            for dx in range(1, NX):
                got(dx - 1, one(xo(-dx)), one(z))
            send(3, ALL, one(z), up)
            send(4, ALL, one(z), down)
            pass_on(42, ALL, one(z))
            for step in range(1, 4):
                yield
                got(1 + 2 * step, ALL, one(zo(-step)))
                if step < 3:
                    send(3 + 2 * step, ALL, one(zo(-step)), up)
                else:
                    send(9, pl.ds(0, 2), one(zo(-3)), up)
                got(2 + 2 * step, ALL, one(zo(step)))
                if step < 3:
                    send(4 + 2 * step, ALL, one(zo(step)), down)
                else:
                    send(10, pl.ds(2, 2), one(zo(3)), down)
                pass_on(41 + 2 * step, ALL, one(zo(-step)))
                pass_on(42 + 2 * step, ALL, one(zo(step)))
            yield
            got(9, pl.ds(0, 2), one(zo(-4)))
            got(10, pl.ds(2, 2), one(zo(4)))
            pass_on(49, ALL, one(zo(4)))
            return
        offsets = (0, -1, 1, -2, 2, -3, 3, 4)

        def sideways(j):
            at = one(zo(offsets[j]))
            send(18 + j, one(x), at, right)
            send(26 + j, one(x), at, left)

        send(11, one(x), one(z), up)
        send(12, one(x), one(z), down)
        sideways(0)
        for step in range(1, 4):
            yield
            got(9 + 2 * step, one(x), one(zo(-step)))
            if step < 3:
                send(11 + 2 * step, one(x), one(zo(-step)), up)
            elif plus:
                send(17, one(x), one(zo(-3)), up)
            sideways(2 * step - 1)
            got(10 + 2 * step, one(x), one(zo(step)))
            if step < 3:
                send(12 + 2 * step, one(x), one(zo(step)), down)
            elif not plus:
                send(17, one(x), one(zo(3)), down)
            sideways(2 * step)
        yield
        got(17, one(x), one(zo(4)))
        sideways(7)
        pass_on(50, one(x), ALL)
        for j, by in enumerate(offsets):
            yield
            got(18 + j, one(xo(-1)), one(zo(by)))
            got(26 + j, one(xo(1)), one(zo(by)))
            if j % 2 == 0:
                send(34 + j, one(xo(-1)), one(zo(by)), right)
            else:
                send(34 + j, one(xo(1)), one(zo(by)), left)
        pass_on(51, one(xo(-1)), ALL)
        pass_on(52, one(xo(1)), ALL)
        yield
        for j, by in enumerate(offsets):
            got(34 + j, one(xo(2)), one(zo(by)))
        pass_on(53, one(xo(2)), ALL)

    def exchange(tensor):
        def own_first():
            ops = [(0, by - 1, one(x), one(z), dev(xo(by), z, c), one(xo(-by)), one(z)) for by in FAR_X]
            return ops + [(1, 2 + by, one(x), one(z), dev(x, zo(by), c), one(x), one(zo(-by))) for by in FAR_Z]

        def along_z():
            return [(0, 9 + by, ALL, one(z), dev(x, zo(by), c), ALL, one(zo(-by))) for by in FAR_Z]

        def along_x():
            return [(1, 16 + by, one(x), ALL, dev(xo(by), z, c), one(xo(-by)), ALL) for by in FAR_X]

        def to_mate():
            return [(colour, 20 + colour, ALL, ALL, dev(x, z, 1 - c), ALL, ALL) for colour in range(2)]

        def send(ops):
            for colour, slot, xs, zs, target, _, _ in ops:
                copy_of(tensor, slot, piece(tensor, colour, xs, zs, c), target).start()

        def got(ops, pc=c):
            for colour, slot, _, _, target, xs, zs in ops:
                copy_of(tensor, slot, piece(tensor, colour, xs, zs, pc), target).wait_recv()

        def begin():
            send(own_first())

        def middle():
            ops = own_first()
            got(ops[: NX - 1])
            send(along_z())
            got(ops[NX - 1 :])
            send(along_x())

        def end():
            got(along_x())
            send(to_mate()[1:])
            got(along_z())
            send(to_mate()[:1])
            got(to_mate()[::-1], 1 - c)
            for colour, slot, xs, zs, target, _, _ in own_first() + along_z() + along_x() + to_mate():
                copy_of(tensor, slot, piece(tensor, colour, xs, zs, c), target).wait_send()

        return begin, middle, end

    def follow(streams, order):
        for at in order:
            next(streams[at], None)

    pending, unsent = [], []
    for op in own:
        op.wait()
    streams = [
        gather(tensor, colour, tensor == W_IN) for tensor in (W_OUT, W_IN) for colour in (1, 0)
    ]
    follow(streams, (0, 1))
    swap = pltpu.make_async_remote_copy(
        src_ref=wi_ref, dst_ref=pair, send_sem=pair_sem.at[0], recv_sem=pair_sem.at[1],
        device_id=dev(x, z, 1 - c), device_id_type=MESH,
    )
    swap.start()

    swap.wait()
    mine, theirs = wi_ref[...].astype(F32), pair[...].astype(F32)
    both = jnp.concatenate(
        [jnp.where(c == 0, mine, theirs), jnp.where(c == 0, theirs, mine)], axis=0
    )
    half = jnp.where(c == 0, both[:, :512], both[:, 512:]).astype(BF)
    win[pl.ds(x, 1), pl.ds(z, 1), :, pl.ds(pl.multiple_of(c * 512, 512), 512)] = half.reshape(1, 1, 112, 512)
    follow(streams, WEIGHT_ORDER)
    for wait in pending:
        wait()

    def flip():
        @pl.loop(0, NX)
        def _(n):
            for j in range(8):
                part = win[n, :, :, pl.ds(128 * j, 128)].reshape(896, 128)
                win_t[pl.ds(128 * j, 128), pl.ds(pl.multiple_of(n * 896, 128), 896)] = part.T
            for j in range(7):
                part = wout[n, :, :, :, pl.ds(512 * j, 512)].reshape(256, 512)
                wout_t[pl.ds(512 * j, 512), pl.ds(pl.multiple_of(n * 256, 256), 256)] = part.T

    @pl.when(seg > 0)
    def _():
        flip()
        for wait in unsent:
            wait()

    @pl.when(seg == 0)
    def _():
        for op in tokens:
            op.wait()

    def hop(step, k, part, src, dst, to):
        rows = pl.ds(pl.multiple_of(k * CHUNK, CHUNK), CHUNK)
        cols = pl.ds(part * WIDE, WIDE)
        return pltpu.make_async_remote_copy(
            src_ref=src.at[rows, cols], dst_ref=dst.at[rows, cols],
            send_sem=hop_send.at[step, k, part], recv_sem=hop_recv.at[step, k, part],
            device_id=(me, to), device_id_type=MESH,
        )

    pooled[...] = jnp.zeros_like(pooled)

    def weight(start, count, side):
        length = jnp.where(side == 0, qlen_ref[0], plen_ref[0])
        at = lax.broadcasted_iota(jnp.int32, (count, 1), 0) + start
        return jnp.where(at < length, 1.0, 0.0) / length.astype(F32)

    def norm_of(side):
        total = jnp.sum(pooled[side], axis=0, keepdims=True)
        return total, lax.rsqrt(jnp.sum(total * total, axis=-1, keepdims=True) + EPS)

    def embed(side):
        total, inv = norm_of(side)
        unit = total * inv
        for k in range(PACKS):
            pack[side, k : k + 1, :] = unit[:, k * 128 : (k + 1) * 128]
        spot = lax.broadcasted_iota(jnp.int32, (32 - PACKS, 128), 1)
        pack[side, PACKS:32, :] = jnp.where(spot == pos_ref[0], 1.0, 0.0)
        emb[pl.ds(x, 1), pl.ds(z, 1), pl.ds(c, 1), pl.ds(32 * side, 32), :] = pack[side].reshape(1, 1, 1, 32, 128)
        return total, inv

    query_steps, passage_steps = exchange(EMB_Q), exchange(EMB_P)

    @pl.loop(0, CHUNKS)
    def _(k):
        rows = pl.ds(pl.multiple_of(k * CHUNK, CHUNK), CHUNK)

        square = jnp.zeros((CHUNK, 1), F32)
        v = jnp.zeros((CHUNK, KVW), F32)
        for n in range(PARTS):
            cols = pl.ds(n * WIDE, WIDE)

            @pl.when(seg > 0)
            def _():
                hop(0, k, n, outb, kept, seg).wait_recv()

            stream = kept[rows, cols].astype(F32)
            square = square + jnp.sum(stream * stream, axis=-1, keepdims=True)
            gained = (stream * gain_ref[:, cols]).astype(BF)
            v = v + jnp.dot(gained, win[n].reshape(WIDE, KVW), preferred_element_type=F32)
        scale = lax.rsqrt(square * (1.0 / D) + EPS)
        scales[rows, :] = jnp.broadcast_to(scale, (CHUNK, 128))
        v = v * scale
        pre[rows, :] = v
        act[...] = gelu(v).astype(BF)

        def rise(n):
            cols = pl.ds(n * WIDE, WIDE)
            return jnp.dot(act[...], wout[:, :, :, :, cols].reshape(KVW, WIDE), preferred_element_type=F32)

        ahead = rise(0)
        for n in range(PARTS):
            cols = pl.ds(n * WIDE, WIDE)
            v, ahead = ahead, rise(n + 1) if n + 1 < PARTS else None
            outb[rows, cols] = (kept[rows, cols].astype(F32) + v).astype(BF)

            @pl.when(seg < NY - 1)
            def _():
                hop(0, k, n, outb, kept, seg + 1).start()

        @pl.when(seg == NY - 1)
        def _():
            side = (k * CHUNK) // SEQ
            total = jnp.zeros((8, D), F32)
            for part in range(CHUNK // 16):
                sub = pl.ds(pl.multiple_of(k * CHUNK + part * 16, 16), 16)
                scaled = outb[sub, :].astype(F32) * weight(part * 16 + (k * CHUNK) % SEQ, 16, side)
                total = total + scaled[0:8] + scaled[8:16]
            pooled[side] += total

            @pl.when(k == CHUNKS // 2 - 1)
            def _():
                embed(0)
                query_steps[0]()

            @pl.when(k == CHUNKS // 2)
            def _():
                query_steps[1]()

    @pl.when(seg == 0)
    def _():
        flip()
        for wait in unsent:
            wait()

    @pl.when(seg == NY - 1)
    def _():
        flat = emb.reshape(NQ * 64, 128)

        def unpack(side):
            for k in range(PACKS):
                embs[side, :, pl.ds(k * 128, 128)] = flat[pl.ds(32 * side + k, NQ, stride=64), :]

        passage = embed(1)
        passage_steps[0]()
        query_steps[2]()
        query = norm_of(0)
        unpack(0)
        passage_steps[1]()
        passage_steps[2]()
        unpack(1)
        onehot = flat[pl.ds(PACKS, NQ, stride=64), :][:, 0:NQ]
        logits = lax.dot_general(embs[0], embs[1], NT, precision=HI, preferred_element_type=F32) / TEMP
        expo = jnp.exp(logits - jnp.max(logits, axis=1, keepdims=True))
        probs = expo / jnp.sum(expo, axis=1, keepdims=True)
        dlogits = (probs - onehot) / NQ
        ii = lax.broadcasted_iota(jnp.int32, (NQ, NQ), 0)
        jj = lax.broadcasted_iota(jnp.int32, (NQ, NQ), 1)
        row = jnp.sum(jnp.where(ii == me, dlogits, 0.0), axis=0, keepdims=True)
        col = jnp.sum(jnp.where(jj == me, dlogits, 0.0), axis=1, keepdims=True)
        row = jnp.broadcast_to(row, (8, NQ))
        dq = jnp.dot(row, embs[1], precision=HI, preferred_element_type=F32)[0:1] / TEMP
        dp = jnp.sum(col * embs[0], axis=0, keepdims=True) / TEMP
        for side, (demb, (total, inv)) in enumerate(((dq, query), (dp, passage))):
            along = jnp.sum(total * demb, axis=-1, keepdims=True)
            grad = inv * demb - total * (inv * inv * inv) * along
            for part in range(SEQ // 16):
                sub = pl.ds(side * SEQ + part * 16, 16)
                gin[sub, :] = (weight(part * 16, 16, side) * grad).astype(BF)

    gacc[...] = jnp.zeros_like(gacc)

    @pl.loop(0, CHUNKS)
    def _(k):
        rows = pl.ds(pl.multiple_of(k * CHUNK, CHUNK), CHUNK)

        back = jnp.zeros((CHUNK, KVW), F32)
        for n in range(PARTS):
            cols = pl.ds(n * WIDE, WIDE)

            @pl.when(seg < NY - 1)
            def _():
                hop(1, k, n, grad_ref, gin, seg).wait_recv()

            back = back + jnp.dot(gin[rows, cols], wout_t[cols, :], preferred_element_type=F32)
        v = pre[rows, :]
        d = back * gelu_slope(v)
        along = jnp.sum(d * v, axis=-1, keepdims=True)
        dpre[...] = d.astype(BF)
        mean = along * (1.0 / D)
        scale = scales[rows, 0:1]

        def fall(n):
            return jnp.dot(dpre[...], win_t[:, pl.ds(n * WIDE, WIDE)], preferred_element_type=F32)

        ahead = fall(0)
        for n in range(PARTS):
            cols = pl.ds(n * WIDE, WIDE)
            dnormed, ahead = ahead, fall(n + 1) if n + 1 < PARTS else None
            unit = kept[rows, cols].astype(F32) * scale
            both = dnormed * unit
            gacc[:, cols] += both[0:8] + both[8:16] + both[16:24] + both[24:32]
            res = gin[rows, cols].astype(F32) + scale * (dnormed * gain_ref[:, cols] - unit * mean)
            grad_ref[rows, cols] = res.astype(BF)

            @pl.when(seg > 0)
            def _():
                hop(1, k, n, grad_ref, gin, seg - 1).start()

    def reduce(step, buf, at, peers):
        ops, sent = [], []
        for j, (target, source) in enumerate(peers):
            op = pltpu.make_async_remote_copy(
                src_ref=buf.at[at], dst_ref=buf.at[at],
                send_sem=red_send.at[step, j], recv_sem=red_recv.at[step, j],
                device_id=target, device_id_type=MESH,
            )
            op.start()
            sent.append(op.wait_send)
            ops.append(pltpu.make_async_remote_copy(
                src_ref=buf.at[source], dst_ref=buf.at[source],
                send_sem=red_send.at[step, j], recv_sem=red_recv.at[step, j],
                device_id=target, device_id_type=MESH,
            ).wait_recv)
        for op in ops:
            op()
        return sent

    at = x * NC + c
    gsum = jnp.sum(gacc[...], axis=0, keepdims=True)
    for k in range(PACKS):
        pack[0, k : k + 1, :] = gsum[:, k * 128 : (k + 1) * 128]
    near[at] = pack[0]
    peers = []
    for dx in FAR_X + (0,):
        for pc in (c, 1 - c) if dx else (1 - c,):
            peers.append((dev(xo(dx), z, pc), xo(-dx) * NC + pc))
    sent = reduce(0, near, at, peers)
    far[z] = jnp.sum(near[...], axis=0)
    sent += reduce(1, far, z, [(dev(x, zo(dz), c), zo(-dz)) for dz in FAR_Z])
    gsum_ref[...] = jnp.sum(far[...], axis=0)
    for op in sent:
        op()

    @pl.when(seg > 0)
    def _():
        for k in range(CHUNKS):
            for part in range(PARTS):
                hop(1, k, part, grad_ref, gin, seg).wait_send()

    @pl.when(seg < NY - 1)
    def _():
        for k in range(CHUNKS):
            for part in range(PARTS):
                hop(0, k, part, outb, kept, seg).wait_send()


def local(queries_in, passages_in, query_len, passage_len, positive, norm_gain, w_in, w_out):
    vmem, hbm = pl.BlockSpec(memory_space=pltpu.VMEM), pl.BlockSpec(memory_space=pltpu.HBM)
    smem = pl.BlockSpec(memory_space=pltpu.SMEM)
    rows = 2 * SEQ
    grads, gains = pl.pallas_call(
        kernel,
        out_shape=(
            jax.ShapeDtypeStruct((rows, D), BF),
            jax.ShapeDtypeStruct((32, 128), F32),
        ),
        in_specs=[smem] * 3 + [hbm] * 5,
        out_specs=(vmem, vmem),
        scratch_shapes=[
            pltpu.VMEM((NX, NZ, 112, KVW), BF),
            pltpu.VMEM((NX, NZ, NC, 16, D), BF),
            pltpu.VMEM((KVW, D), BF),
            pltpu.VMEM((D, KVW), BF),
            pltpu.VMEM((NX, NZ, NC, 64, 128), F32),
            pltpu.VMEM((2, NQ, D), F32),
            pltpu.VMEM((1, D), F32),
            pltpu.VMEM((56, KVW), BF),
            pltpu.VMEM((56, KVW), BF),
            pltpu.VMEM((rows, D), BF),
            pltpu.VMEM((rows, KVW), F32),
            pltpu.VMEM((rows, 128), F32),
            pltpu.VMEM((CHUNK, KVW), BF),
            pltpu.VMEM((rows, D), BF),
            pltpu.VMEM((rows, D), BF),
            pltpu.VMEM((CHUNK, KVW), BF),
            pltpu.VMEM((8, D), F32),
            pltpu.VMEM((2, 8, D), F32),
            pltpu.VMEM((2, 32, 128), F32),
            pltpu.VMEM((NX * NC, 32, 128), F32),
            pltpu.VMEM((NZ, 32, 128), F32),
            pltpu.SemaphoreType.DMA((4, 54)),
            pltpu.SemaphoreType.DMA((4, 54)),
            pltpu.SemaphoreType.DMA((2,)),
            pltpu.SemaphoreType.DMA((5,)),
            pltpu.SemaphoreType.DMA((2, CHUNKS, PARTS)),
            pltpu.SemaphoreType.DMA((2, CHUNKS, PARTS)),
            pltpu.SemaphoreType.DMA((2, 7)),
            pltpu.SemaphoreType.DMA((2, 7)),
        ],
        compiler_params=pltpu.CompilerParams(
            collective_id=0, has_side_effects=True, vmem_limit_bytes=58 * 1024 * 1024
        ),
        name="embedder_window",
    )(query_len, passage_len, positive, queries_in, passages_in, norm_gain, w_in[0], w_out[0])
    grads = grads.reshape(2, 1, 1, SEQ, D)
    return grads[0], grads[1], gains[:PACKS].reshape(1, D)


def solution(mesh):
    return jax.shard_map(
        local,
        mesh=mesh,
        in_specs=(
            P("dp", None, None),
            P("dp", None, None),
            P("dp"),
            P("dp"),
            P("dp"),
            P("segment", None),
            P("segment", "dp", None),
            P("segment", "dp", None),
        ),
        out_specs=(
            P("segment", "dp", None, None),
            P("segment", "dp", None, None),
            P("segment", None),
        ),
        check_vma=False,
    )
```

```python
import math

import jax
import jax.numpy as jnp
from jax import lax
from jax.experimental import pallas as pl
from jax.experimental.pallas import tpu as pltpu
from jax.sharding import PartitionSpec as P

MESH = pl.DeviceIdType.MESH
BF, F32 = jnp.bfloat16, jnp.float32
HI = lax.Precision.HIGHEST
D, KVW, SEQ, NQ = 3584, 1024, 64, 64
NX, NZ, NC, NY = 4, 8, 2, 4
TEMP = 0.02
CHUNK = 32
CHUNKS = 2 * SEQ // CHUNK
PARTS = 4
WIDE = D // PARTS
PACKS = D // 128
FAR_X, FAR_Z = (2, 1, 3), (4, 3, 5, 2, 6, 1, 7)
WEIGHT_ORDER = (
    2, 3, 0, 1, 2, 3, 0, 1, 2, 2, 0, 3, 2, 0, 0, 0, 2, 0, 2, 1, 0, 3, 2, 2, 0, 2, 2, 0, 0, 0, 1, 2, 2, 3, 2, 0, 1, 3,
)
EPS = 1e-06
C0 = math.sqrt(2.0 / math.pi)
EMB_P, EMB_Q, W_IN, W_OUT = 0, 1, 2, 3
ALL = slice(None)
NT = (((1,), (1,)), ((), ()))


def gelu(v):
    return 0.5 * v * (1.0 + jnp.tanh(C0 * (v + 0.044715 * v * v * v)))


def gelu_slope(v):
    t = jnp.tanh(C0 * (v + 0.044715 * v * v * v))
    return 0.5 * (1.0 + t) + 0.5 * v * (1.0 - t * t) * C0 * (1.0 + 3.0 * 0.044715 * v * v)


def kernel(
    qlen_ref, plen_ref, pos_ref, queries_ref, passages_ref, gain_hbm, wi_hbm, wo_hbm,
    grad_ref, gsum_ref,
    win, wout, win_t, wout_t, emb, embs, gain_ref, wi_ref, pair, kept, pre, scales, act, outb, gin, dpre, gacc, pooled,
    pack, near, far,
    ag_send, ag_recv, pair_sem, tok_sem, hop_send, hop_recv, red_send, red_recv,
):
    me = lax.axis_index("dp")
    seg = lax.axis_index("segment")
    x, z, c = me // (NZ * NC), (me // NC) % NZ, me % NC

    def dev(px, pz, pc):
        return ((px * NZ + pz) * NC + pc, seg)

    def xo(by):
        return (x + by + NX) % NX

    def zo(by):
        return (z + by + NZ) % NZ

    own = [
        pltpu.make_async_copy(src, dst, tok_sem.at[2 + j])
        for j, (src, dst) in enumerate(((wo_hbm, wout.at[x, z, c]), (wi_hbm, wi_ref), (gain_hbm, gain_ref)))
    ]
    for op in own:
        op.start()
    tokens = [
        pltpu.make_async_copy(ref.at[0], kept.at[pl.ds(side * SEQ, SEQ)], tok_sem.at[side])
        for side, ref in enumerate((passages_ref, queries_ref))
    ]

    @pl.when(seg == 0)
    def _():
        for op in tokens:
            op.start()

    barrier = pltpu.get_barrier_semaphore()
    mates = [dev(xo(dx), z, pc) for dx in range(NX) for pc in (c, 1 - c)][1:]
    mates += [dev(x, zo(dz), c) for dz in range(1, NZ)]
    mates += [(me, (seg + by) % NY) for by in (1, NY - 1)]
    for mate in mates:
        pl.semaphore_signal(barrier, inc=1, device_id=mate, device_id_type=MESH)
    pl.semaphore_wait(barrier, len(mates))

    def piece(tensor, colour, xs, zs, pc):
        if tensor == W_IN:
            rows = pl.ds(0, 48) if colour == 0 else pl.ds(48, 64)
            return win.at[xs, zs, rows, pl.ds(pl.multiple_of(pc * 512, 512), 512)]
        if tensor == W_OUT:
            cols = pl.ds(0, 1536) if colour == 0 else pl.ds(1536, 2048)
            return wout.at[xs, zs, pl.ds(pc, 1), :, cols]
        rows = pl.ds(32 * tensor, 8) if colour == 0 else pl.ds(32 * tensor + 8, 24)
        return emb.at[xs, zs, pl.ds(pc, 1), rows, :]

    def copy_of(tensor, slot, ref, target):
        return pltpu.make_async_remote_copy(
            src_ref=ref, dst_ref=ref,
            send_sem=ag_send.at[tensor, slot], recv_sem=ag_recv.at[tensor, slot],
            device_id=target, device_id_type=MESH,
        )

    def one(at):
        return pl.ds(at, 1)

    def gather(tensor, colour, plus):
        def send(slot, xs, zs, target):
            op = copy_of(tensor, slot, piece(tensor, colour, xs, zs, c), target)
            op.start()
            unsent.append(op.wait_send)

        def got(slot, xs, zs):
            copy_of(tensor, slot, piece(tensor, colour, xs, zs, c), dev(x, z, 1 - c)).wait_recv()

        def pass_on(slot, xs, zs):
            send(slot, xs, zs, dev(x, z, 1 - c))
            other = copy_of(tensor, slot, piece(tensor, colour, xs, zs, 1 - c), dev(x, z, 1 - c))
            pending.append(other.wait_recv)

        up, down = dev(x, zo(1), c), dev(x, zo(-1), c)
        right, left = dev(xo(1), z, c), dev(xo(-1), z, c)
        if colour == 0:
            for dx in range(1, NX):
                send(dx - 1, one(x), one(z), dev(xo(dx), z, c))
            yield
            for dx in range(1, NX):
                got(dx - 1, one(xo(-dx)), one(z))
            send(3, ALL, one(z), up)
            send(4, ALL, one(z), down)
            pass_on(42, ALL, one(z))
            for step in range(1, 4):
                yield
                got(1 + 2 * step, ALL, one(zo(-step)))
                if step < 3:
                    send(3 + 2 * step, ALL, one(zo(-step)), up)
                else:
                    send(9, pl.ds(0, 2), one(zo(-3)), up)
                got(2 + 2 * step, ALL, one(zo(step)))
                if step < 3:
                    send(4 + 2 * step, ALL, one(zo(step)), down)
                else:
                    send(10, pl.ds(2, 2), one(zo(3)), down)
                pass_on(41 + 2 * step, ALL, one(zo(-step)))
                pass_on(42 + 2 * step, ALL, one(zo(step)))
            yield
            got(9, pl.ds(0, 2), one(zo(-4)))
            got(10, pl.ds(2, 2), one(zo(4)))
            pass_on(49, ALL, one(zo(4)))
            return
        offsets = (0, -1, 1, -2, 2, -3, 3, 4)

        def sideways(j):
            at = one(zo(offsets[j]))
            send(18 + j, one(x), at, right)
            send(26 + j, one(x), at, left)

        send(11, one(x), one(z), up)
        send(12, one(x), one(z), down)
        sideways(0)
        for step in range(1, 4):
            yield
            got(9 + 2 * step, one(x), one(zo(-step)))
            if step < 3:
                send(11 + 2 * step, one(x), one(zo(-step)), up)
            elif plus:
                send(17, one(x), one(zo(-3)), up)
            sideways(2 * step - 1)
            got(10 + 2 * step, one(x), one(zo(step)))
            if step < 3:
                send(12 + 2 * step, one(x), one(zo(step)), down)
            elif not plus:
                send(17, one(x), one(zo(3)), down)
            sideways(2 * step)
        yield
        got(17, one(x), one(zo(4)))
        sideways(7)
        pass_on(50, one(x), ALL)
        for j, by in enumerate(offsets):
            yield
            got(18 + j, one(xo(-1)), one(zo(by)))
            got(26 + j, one(xo(1)), one(zo(by)))
            if j % 2 == 0:
                send(34 + j, one(xo(-1)), one(zo(by)), right)
            else:
                send(34 + j, one(xo(1)), one(zo(by)), left)
        pass_on(51, one(xo(-1)), ALL)
        pass_on(52, one(xo(1)), ALL)
        yield
        for j, by in enumerate(offsets):
            got(34 + j, one(xo(2)), one(zo(by)))
        pass_on(53, one(xo(2)), ALL)

    def exchange(tensor):
        def own_first():
            ops = [(0, by - 1, one(x), one(z), dev(xo(by), z, c), one(xo(-by)), one(z)) for by in FAR_X]
            return ops + [(1, 2 + by, one(x), one(z), dev(x, zo(by), c), one(x), one(zo(-by))) for by in FAR_Z]

        def along_z():
            return [(0, 9 + by, ALL, one(z), dev(x, zo(by), c), ALL, one(zo(-by))) for by in FAR_Z]

        def along_x():
            return [(1, 16 + by, one(x), ALL, dev(xo(by), z, c), one(xo(-by)), ALL) for by in FAR_X]

        def to_mate():
            return [(colour, 20 + colour, ALL, ALL, dev(x, z, 1 - c), ALL, ALL) for colour in range(2)]

        def send(ops):
            for colour, slot, xs, zs, target, _, _ in ops:
                copy_of(tensor, slot, piece(tensor, colour, xs, zs, c), target).start()

        def got(ops, pc=c):
            for colour, slot, _, _, target, xs, zs in ops:
                copy_of(tensor, slot, piece(tensor, colour, xs, zs, pc), target).wait_recv()

        def begin():
            send(own_first())

        def middle():
            ops = own_first()
            got(ops[: NX - 1])
            send(along_z())
            got(ops[NX - 1 :])
            send(along_x())

        def end():
            got(along_x())
            send(to_mate()[1:])
            got(along_z())
            send(to_mate()[:1])
            got(to_mate()[::-1], 1 - c)
            for colour, slot, xs, zs, target, _, _ in own_first() + along_z() + along_x() + to_mate():
                copy_of(tensor, slot, piece(tensor, colour, xs, zs, c), target).wait_send()

        return begin, middle, end

    def follow(streams, order):
        for at in order:
            next(streams[at], None)

    pending, unsent = [], []
    for op in own:
        op.wait()
    streams = [
        gather(tensor, colour, tensor == W_IN) for tensor in (W_OUT, W_IN) for colour in (1, 0)
    ]
    follow(streams, (0, 1))
    swap = pltpu.make_async_remote_copy(
        src_ref=wi_ref, dst_ref=pair, send_sem=pair_sem.at[0], recv_sem=pair_sem.at[1],
        device_id=dev(x, z, 1 - c), device_id_type=MESH,
    )
    swap.start()

    swap.wait()
    mine, theirs = wi_ref[...].astype(F32), pair[...].astype(F32)
    both = jnp.concatenate(
        [jnp.where(c == 0, mine, theirs), jnp.where(c == 0, theirs, mine)], axis=0
    )
    half = jnp.where(c == 0, both[:, :512], both[:, 512:]).astype(BF)
    win[pl.ds(x, 1), pl.ds(z, 1), :, pl.ds(pl.multiple_of(c * 512, 512), 512)] = half.reshape(1, 1, 112, 512)
    follow(streams, WEIGHT_ORDER)
    for wait in pending:
        wait()

    def flip():
        @pl.loop(0, NX)
        def _(n):
            for j in range(8):
                part = win[n, :, :, pl.ds(128 * j, 128)].reshape(896, 128)
                win_t[pl.ds(128 * j, 128), pl.ds(pl.multiple_of(n * 896, 128), 896)] = part.T
            for j in range(7):
                part = wout[n, :, :, :, pl.ds(512 * j, 512)].reshape(256, 512)
                wout_t[pl.ds(512 * j, 512), pl.ds(pl.multiple_of(n * 256, 256), 256)] = part.T

    @pl.when(seg > 0)
    def _():
        flip()
        for wait in unsent:
            wait()

    @pl.when(seg == 0)
    def _():
        for op in tokens:
            op.wait()

    def hop(step, k, part, src, dst, to):
        rows = pl.ds(pl.multiple_of(k * CHUNK, CHUNK), CHUNK)
        cols = pl.ds(part * WIDE, WIDE)
        return pltpu.make_async_remote_copy(
            src_ref=src.at[rows, cols], dst_ref=dst.at[rows, cols],
            send_sem=hop_send.at[step, k, part], recv_sem=hop_recv.at[step, k, part],
            device_id=(me, to), device_id_type=MESH,
        )

    pooled[...] = jnp.zeros_like(pooled)

    def weight(start, count, side):
        length = jnp.where(side == 0, plen_ref[0], qlen_ref[0])
        at = lax.broadcasted_iota(jnp.int32, (count, 1), 0) + start
        return jnp.where(at < length, 1.0, 0.0) / length.astype(F32)

    def norm_of(side):
        total = jnp.sum(pooled[side], axis=0, keepdims=True)
        return total, lax.rsqrt(jnp.sum(total * total, axis=-1, keepdims=True) + EPS)

    def embed(side):
        total, inv = norm_of(side)
        unit = total * inv
        for k in range(PACKS):
            pack[side, k : k + 1, :] = unit[:, k * 128 : (k + 1) * 128]
        spot = lax.broadcasted_iota(jnp.int32, (32 - PACKS, 128), 1)
        pack[side, PACKS:32, :] = jnp.where(spot == pos_ref[0], 1.0, 0.0)
        emb[pl.ds(x, 1), pl.ds(z, 1), pl.ds(c, 1), pl.ds(32 * side, 32), :] = pack[side].reshape(1, 1, 1, 32, 128)
        return unit

    query_steps, passage_steps = exchange(EMB_Q), exchange(EMB_P)

    @pl.loop(0, CHUNKS)
    def _(k):
        rows = pl.ds(pl.multiple_of(k * CHUNK, CHUNK), CHUNK)

        square = jnp.zeros((CHUNK, 1), F32)
        v = jnp.zeros((CHUNK, KVW), F32)
        for n in range(PARTS):
            cols = pl.ds(n * WIDE, WIDE)

            @pl.when(seg > 0)
            def _():
                hop(0, k, n, outb, kept, seg).wait_recv()

            stream = kept[rows, cols].astype(F32)
            square = square + jnp.sum(stream * stream, axis=-1, keepdims=True)
            gained = (stream * gain_ref[:, cols]).astype(BF)
            v = v + jnp.dot(gained, win[n].reshape(WIDE, KVW), preferred_element_type=F32)
        scale = lax.rsqrt(square * (1.0 / D) + EPS)
        scales[rows, :] = jnp.broadcast_to(scale, (CHUNK, 128))
        v = v * scale
        pre[rows, :] = v
        act[...] = gelu(v).astype(BF)

        def rise(n):
            cols = pl.ds(n * WIDE, WIDE)
            return jnp.dot(act[...], wout[:, :, :, :, cols].reshape(KVW, WIDE), preferred_element_type=F32)

        ahead = rise(0)
        for n in range(PARTS):
            cols = pl.ds(n * WIDE, WIDE)
            v, ahead = ahead, rise(n + 1) if n + 1 < PARTS else None
            outb[rows, cols] = (kept[rows, cols].astype(F32) + v).astype(BF)

            @pl.when(seg < NY - 1)
            def _():
                hop(0, k, n, outb, kept, seg + 1).start()

        @pl.when(seg == NY - 1)
        def _():
            side = (k * CHUNK) // SEQ
            total = jnp.zeros((8, D), F32)
            for part in range(CHUNK // 16):
                sub = pl.ds(pl.multiple_of(k * CHUNK + part * 16, 16), 16)
                scaled = outb[sub, :].astype(F32) * weight(part * 16 + (k * CHUNK) % SEQ, 16, side)
                total = total + scaled[0:8] + scaled[8:16]
            pooled[side] += total

            @pl.when(k == CHUNKS // 2 - 1)
            def _():
                embed(0)
                passage_steps[0]()

            @pl.when(k == CHUNKS // 2)
            def _():
                passage_steps[1]()

    @pl.when(seg == 0)
    def _():
        flip()
        for wait in unsent:
            wait()

    flat = emb.reshape(NQ * 64, 128)

    def unpack(side):
        for k in range(PACKS):
            embs[side, :, pl.ds(k * 128, 128)] = flat[pl.ds(32 * side + k, NQ, stride=64), :]

    def excess(logits, onehot):
        expo = jnp.exp(logits - jnp.max(logits, axis=1, keepdims=True))
        return (expo / jnp.sum(expo, axis=1, keepdims=True) - onehot) / NQ

    def spread_back(side, demb):
        total, inv = norm_of(side)
        along = jnp.sum(total * demb, axis=-1, keepdims=True)
        grad = inv * demb - total * (inv * inv * inv) * along
        for part in range(SEQ // 16):
            sub = pl.ds(side * SEQ + part * 16, 16)
            gin[sub, :] = (weight(part * 16, 16, side) * grad).astype(BF)

    @pl.when(seg == NY - 1)
    def _():
        unit = embed(1)
        query_steps[0]()
        passage_steps[2]()
        unpack(0)
        unit = jnp.broadcast_to(unit, (8, D))
        logits = lax.dot_general(unit, embs[0], NT, precision=HI, preferred_element_type=F32) / TEMP
        spot = lax.broadcasted_iota(jnp.int32, (8, NQ), 1)
        dlogits = excess(logits, jnp.where(spot == pos_ref[0], 1.0, 0.0))
        spread_back(1, jnp.dot(dlogits, embs[0], precision=HI, preferred_element_type=F32)[0:1] / TEMP)

    def passages_back():
        unpack(1)
        onehot = flat[pl.ds(PACKS, NQ, stride=64), :][:, 0:NQ]
        logits = lax.dot_general(embs[1], embs[0], NT, precision=HI, preferred_element_type=F32) / TEMP
        dlogits = excess(logits, onehot)
        jj = lax.broadcasted_iota(jnp.int32, (NQ, NQ), 1)
        col = jnp.sum(jnp.where(jj == me, dlogits, 0.0), axis=1, keepdims=True)
        spread_back(0, jnp.sum(col * embs[1], axis=0, keepdims=True) / TEMP)

    gacc[...] = jnp.zeros_like(gacc)

    @pl.loop(0, CHUNKS)
    def _(step):
        k = CHUNKS - 1 - step
        rows = pl.ds(pl.multiple_of(k * CHUNK, CHUNK), CHUNK)

        back = jnp.zeros((CHUNK, KVW), F32)
        for n in range(PARTS):
            cols = pl.ds(n * WIDE, WIDE)

            @pl.when(seg < NY - 1)
            def _():
                hop(1, k, n, grad_ref, gin, seg).wait_recv()

            back = back + jnp.dot(gin[rows, cols], wout_t[cols, :], preferred_element_type=F32)
        v = pre[rows, :]
        d = back * gelu_slope(v)
        along = jnp.sum(d * v, axis=-1, keepdims=True)
        dpre[...] = d.astype(BF)
        mean = along * (1.0 / D)
        scale = scales[rows, 0:1]

        def fall(n):
            return jnp.dot(dpre[...], win_t[:, pl.ds(n * WIDE, WIDE)], preferred_element_type=F32)

        ahead = fall(0)
        for n in range(PARTS):
            cols = pl.ds(n * WIDE, WIDE)
            dnormed, ahead = ahead, fall(n + 1) if n + 1 < PARTS else None
            unit = kept[rows, cols].astype(F32) * scale
            both = dnormed * unit
            gacc[:, cols] += both[0:8] + both[8:16] + both[16:24] + both[24:32]
            res = gin[rows, cols].astype(F32) + scale * (dnormed * gain_ref[:, cols] - unit * mean)
            grad_ref[rows, cols] = res.astype(BF)

            @pl.when(seg > 0)
            def _():
                hop(1, k, n, grad_ref, gin, seg - 1).start()

        @pl.when((seg == NY - 1) & (step == 0))
        def _():
            query_steps[1]()

        @pl.when((seg == NY - 1) & (step == CHUNKS // 2 - 1))
        def _():
            query_steps[2]()
            passages_back()

    def reduce(step, buf, at, peers):
        ops, sent = [], []
        for j, (target, source) in enumerate(peers):
            op = pltpu.make_async_remote_copy(
                src_ref=buf.at[at], dst_ref=buf.at[at],
                send_sem=red_send.at[step, j], recv_sem=red_recv.at[step, j],
                device_id=target, device_id_type=MESH,
            )
            op.start()
            sent.append(op.wait_send)
            ops.append(pltpu.make_async_remote_copy(
                src_ref=buf.at[source], dst_ref=buf.at[source],
                send_sem=red_send.at[step, j], recv_sem=red_recv.at[step, j],
                device_id=target, device_id_type=MESH,
            ).wait_recv)
        for op in ops:
            op()
        return sent

    at = x * NC + c
    gsum = jnp.sum(gacc[...], axis=0, keepdims=True)
    for k in range(PACKS):
        pack[0, k : k + 1, :] = gsum[:, k * 128 : (k + 1) * 128]
    near[at] = pack[0]
    peers = []
    for dx in FAR_X + (0,):
        for pc in (c, 1 - c) if dx else (1 - c,):
            peers.append((dev(xo(dx), z, pc), xo(-dx) * NC + pc))
    sent = reduce(0, near, at, peers)
    far[z] = jnp.sum(near[...], axis=0)
    sent += reduce(1, far, z, [(dev(x, zo(dz), c), zo(-dz)) for dz in FAR_Z])
    gsum_ref[...] = jnp.sum(far[...], axis=0)
    for op in sent:
        op()

    @pl.when(seg > 0)
    def _():
        for k in range(CHUNKS):
            for part in range(PARTS):
                hop(1, k, part, grad_ref, gin, seg).wait_send()

    @pl.when(seg < NY - 1)
    def _():
        for k in range(CHUNKS):
            for part in range(PARTS):
                hop(0, k, part, outb, kept, seg).wait_send()


def local(queries_in, passages_in, query_len, passage_len, positive, norm_gain, w_in, w_out):
    vmem, hbm = pl.BlockSpec(memory_space=pltpu.VMEM), pl.BlockSpec(memory_space=pltpu.HBM)
    smem = pl.BlockSpec(memory_space=pltpu.SMEM)
    rows = 2 * SEQ
    grads, gains = pl.pallas_call(
        kernel,
        out_shape=(
            jax.ShapeDtypeStruct((rows, D), BF),
            jax.ShapeDtypeStruct((32, 128), F32),
        ),
        in_specs=[smem] * 3 + [hbm] * 5,
        out_specs=(vmem, vmem),
        scratch_shapes=[
            pltpu.VMEM((NX, NZ, 112, KVW), BF),
            pltpu.VMEM((NX, NZ, NC, 16, D), BF),
            pltpu.VMEM((KVW, D), BF),
            pltpu.VMEM((D, KVW), BF),
            pltpu.VMEM((NX, NZ, NC, 64, 128), F32),
            pltpu.VMEM((2, NQ, D), F32),
            pltpu.VMEM((1, D), F32),
            pltpu.VMEM((56, KVW), BF),
            pltpu.VMEM((56, KVW), BF),
            pltpu.VMEM((rows, D), BF),
            pltpu.VMEM((rows, KVW), F32),
            pltpu.VMEM((rows, 128), F32),
            pltpu.VMEM((CHUNK, KVW), BF),
            pltpu.VMEM((rows, D), BF),
            pltpu.VMEM((rows, D), BF),
            pltpu.VMEM((CHUNK, KVW), BF),
            pltpu.VMEM((8, D), F32),
            pltpu.VMEM((2, 8, D), F32),
            pltpu.VMEM((2, 32, 128), F32),
            pltpu.VMEM((NX * NC, 32, 128), F32),
            pltpu.VMEM((NZ, 32, 128), F32),
            pltpu.SemaphoreType.DMA((4, 54)),
            pltpu.SemaphoreType.DMA((4, 54)),
            pltpu.SemaphoreType.DMA((2,)),
            pltpu.SemaphoreType.DMA((5,)),
            pltpu.SemaphoreType.DMA((2, CHUNKS, PARTS)),
            pltpu.SemaphoreType.DMA((2, CHUNKS, PARTS)),
            pltpu.SemaphoreType.DMA((2, 7)),
            pltpu.SemaphoreType.DMA((2, 7)),
        ],
        compiler_params=pltpu.CompilerParams(
            collective_id=0, has_side_effects=True, vmem_limit_bytes=58 * 1024 * 1024
        ),
        name="embedder_window",
    )(query_len, passage_len, positive, queries_in, passages_in, norm_gain, w_in[0], w_out[0])
    grads = grads.reshape(2, 1, 1, SEQ, D)
    return grads[1], grads[0], gains[:PACKS].reshape(1, D)


def solution(mesh):
    return jax.shard_map(
        local,
        mesh=mesh,
        in_specs=(
            P("dp", None, None),
            P("dp", None, None),
            P("dp"),
            P("dp"),
            P("dp"),
            P("segment", None),
            P("segment", "dp", None),
            P("segment", "dp", None),
        ),
        out_specs=(
            P("segment", "dp", None, None),
            P("segment", "dp", None, None),
            P("segment", None),
        ),
        check_vma=False,
    )
```

```python
import math

import jax
import jax.numpy as jnp
from jax import lax
from jax.experimental import pallas as pl
from jax.experimental.pallas import tpu as pltpu
from jax.sharding import PartitionSpec as P

MESH = pl.DeviceIdType.MESH
BF, F32 = jnp.bfloat16, jnp.float32
HI = lax.Precision.HIGHEST
D, KVW, SEQ, NQ = 3584, 1024, 64, 64
NX, NZ, NC, NY = 4, 8, 2, 4
TEMP = 0.02
CHUNK = 16
CHUNKS = 2 * SEQ // CHUNK
PARTS = 4
WIDE = D // PARTS
SLABS = NX // PARTS
PACKS = D // 128
FAR_X, FAR_Z = (2, 1, 3), (4, 3, 5, 2, 6, 1, 7)
WEIGHT_ORDER = (
    2, 3, 0, 1, 2, 3, 0, 1, 2, 2, 0, 3, 2, 0, 0, 0, 2, 0, 2, 1, 0, 3, 2, 2, 0, 2, 2, 0, 0, 0, 1, 2, 2, 3, 2, 0, 1, 3,
)
EPS = 1e-06
C0 = math.sqrt(2.0 / math.pi)
EMB_P, EMB_Q, W_IN, W_OUT = 0, 1, 2, 3
ALL = slice(None)
NT = (((1,), (1,)), ((), ()))


def gelu(v):
    return 0.5 * v * (1.0 + jnp.tanh(C0 * (v + 0.044715 * v * v * v)))


def gelu_slope(v):
    t = jnp.tanh(C0 * (v + 0.044715 * v * v * v))
    return 0.5 * (1.0 + t) + 0.5 * v * (1.0 - t * t) * C0 * (1.0 + 3.0 * 0.044715 * v * v)


def kernel(
    qlen_ref, plen_ref, pos_ref, queries_ref, passages_ref, gain_hbm, wi_hbm, wo_hbm,
    grad_ref, gsum_ref,
    win, wout, win_t, wout_t, emb, embs, gain_ref, wi_ref, pair, kept, pre, scales, act, outb, gin, dpre, gacc, pooled,
    pack, near, far,
    ag_send, ag_recv, pair_sem, tok_sem, hop_send, hop_recv, red_send, red_recv,
):
    me = lax.axis_index("dp")
    seg = lax.axis_index("segment")
    x, z, c = me // (NZ * NC), (me // NC) % NZ, me % NC

    def dev(px, pz, pc):
        return ((px * NZ + pz) * NC + pc, seg)

    def xo(by):
        return (x + by + NX) % NX

    def zo(by):
        return (z + by + NZ) % NZ

    own = [
        pltpu.make_async_copy(src, dst, tok_sem.at[2 + j])
        for j, (src, dst) in enumerate(((wo_hbm, wout.at[x, z, c]), (wi_hbm, wi_ref), (gain_hbm, gain_ref)))
    ]
    for op in own:
        op.start()
    tokens = [
        pltpu.make_async_copy(ref.at[0], kept.at[pl.ds(side * SEQ, SEQ)], tok_sem.at[side])
        for side, ref in enumerate((passages_ref, queries_ref))
    ]

    @pl.when(seg == 0)
    def _():
        for op in tokens:
            op.start()

    barrier = pltpu.get_barrier_semaphore()
    mates = [dev(xo(dx), z, pc) for dx in range(NX) for pc in (c, 1 - c)][1:]
    mates += [dev(x, zo(dz), c) for dz in range(1, NZ)]
    mates += [(me, (seg + by) % NY) for by in (1, NY - 1)]
    for mate in mates:
        pl.semaphore_signal(barrier, inc=1, device_id=mate, device_id_type=MESH)
    pl.semaphore_wait(barrier, len(mates))

    def piece(tensor, colour, xs, zs, pc):
        if tensor == W_IN:
            rows = pl.ds(0, 48) if colour == 0 else pl.ds(48, 64)
            return win.at[xs, zs, rows, pl.ds(pl.multiple_of(pc * 512, 512), 512)]
        if tensor == W_OUT:
            cols = pl.ds(0, 1536) if colour == 0 else pl.ds(1536, 2048)
            return wout.at[xs, zs, pl.ds(pc, 1), :, cols]
        rows = pl.ds(32 * tensor, 8) if colour == 0 else pl.ds(32 * tensor + 8, 24)
        return emb.at[xs, zs, pl.ds(pc, 1), rows, :]

    def copy_of(tensor, slot, ref, target):
        return pltpu.make_async_remote_copy(
            src_ref=ref, dst_ref=ref,
            send_sem=ag_send.at[tensor, slot], recv_sem=ag_recv.at[tensor, slot],
            device_id=target, device_id_type=MESH,
        )

    def one(at):
        return pl.ds(at, 1)

    def gather(tensor, colour, plus):
        def send(slot, xs, zs, target):
            op = copy_of(tensor, slot, piece(tensor, colour, xs, zs, c), target)
            op.start()
            unsent.append(op.wait_send)

        def got(slot, xs, zs):
            copy_of(tensor, slot, piece(tensor, colour, xs, zs, c), dev(x, z, 1 - c)).wait_recv()

        def pass_on(slot, xs, zs):
            send(slot, xs, zs, dev(x, z, 1 - c))
            other = copy_of(tensor, slot, piece(tensor, colour, xs, zs, 1 - c), dev(x, z, 1 - c))
            pending.append(other.wait_recv)

        up, down = dev(x, zo(1), c), dev(x, zo(-1), c)
        right, left = dev(xo(1), z, c), dev(xo(-1), z, c)
        if colour == 0:
            for dx in range(1, NX):
                send(dx - 1, one(x), one(z), dev(xo(dx), z, c))
            yield
            for dx in range(1, NX):
                got(dx - 1, one(xo(-dx)), one(z))
            send(3, ALL, one(z), up)
            send(4, ALL, one(z), down)
            pass_on(42, ALL, one(z))
            for step in range(1, 4):
                yield
                got(1 + 2 * step, ALL, one(zo(-step)))
                if step < 3:
                    send(3 + 2 * step, ALL, one(zo(-step)), up)
                else:
                    send(9, pl.ds(0, 2), one(zo(-3)), up)
                got(2 + 2 * step, ALL, one(zo(step)))
                if step < 3:
                    send(4 + 2 * step, ALL, one(zo(step)), down)
                else:
                    send(10, pl.ds(2, 2), one(zo(3)), down)
                pass_on(41 + 2 * step, ALL, one(zo(-step)))
                pass_on(42 + 2 * step, ALL, one(zo(step)))
            yield
            got(9, pl.ds(0, 2), one(zo(-4)))
            got(10, pl.ds(2, 2), one(zo(4)))
            pass_on(49, ALL, one(zo(4)))
            return
        offsets = (0, -1, 1, -2, 2, -3, 3, 4)

        def sideways(j):
            at = one(zo(offsets[j]))
            send(18 + j, one(x), at, right)
            send(26 + j, one(x), at, left)

        send(11, one(x), one(z), up)
        send(12, one(x), one(z), down)
        sideways(0)
        for step in range(1, 4):
            yield
            got(9 + 2 * step, one(x), one(zo(-step)))
            if step < 3:
                send(11 + 2 * step, one(x), one(zo(-step)), up)
            elif plus:
                send(17, one(x), one(zo(-3)), up)
            sideways(2 * step - 1)
            got(10 + 2 * step, one(x), one(zo(step)))
            if step < 3:
                send(12 + 2 * step, one(x), one(zo(step)), down)
            elif not plus:
                send(17, one(x), one(zo(3)), down)
            sideways(2 * step)
        yield
        got(17, one(x), one(zo(4)))
        sideways(7)
        pass_on(50, one(x), ALL)
        for j, by in enumerate(offsets):
            yield
            got(18 + j, one(xo(-1)), one(zo(by)))
            got(26 + j, one(xo(1)), one(zo(by)))
            if j % 2 == 0:
                send(34 + j, one(xo(-1)), one(zo(by)), right)
            else:
                send(34 + j, one(xo(1)), one(zo(by)), left)
        pass_on(51, one(xo(-1)), ALL)
        pass_on(52, one(xo(1)), ALL)
        yield
        for j, by in enumerate(offsets):
            got(34 + j, one(xo(2)), one(zo(by)))
        pass_on(53, one(xo(2)), ALL)

    def exchange(tensor):
        def own_first():
            ops = [(0, by - 1, one(x), one(z), dev(xo(by), z, c), one(xo(-by)), one(z)) for by in FAR_X]
            return ops + [(1, 2 + by, one(x), one(z), dev(x, zo(by), c), one(x), one(zo(-by))) for by in FAR_Z]

        def along_z():
            return [(0, 9 + by, ALL, one(z), dev(x, zo(by), c), ALL, one(zo(-by))) for by in FAR_Z]

        def along_x():
            return [(1, 16 + by, one(x), ALL, dev(xo(by), z, c), one(xo(-by)), ALL) for by in FAR_X]

        def to_mate():
            return [(colour, 20 + colour, ALL, ALL, dev(x, z, 1 - c), ALL, ALL) for colour in range(2)]

        def send(ops):
            for colour, slot, xs, zs, target, _, _ in ops:
                copy_of(tensor, slot, piece(tensor, colour, xs, zs, c), target).start()

        def got(ops, pc=c):
            for colour, slot, _, _, target, xs, zs in ops:
                copy_of(tensor, slot, piece(tensor, colour, xs, zs, pc), target).wait_recv()

        def begin():
            send(own_first())

        def middle():
            ops = own_first()
            got(ops[: NX - 1])
            send(along_z())
            got(ops[NX - 1 :])
            send(along_x())

        def end():
            got(along_x())
            send(to_mate()[1:])
            got(along_z())
            send(to_mate()[:1])
            got(to_mate()[::-1], 1 - c)
            for colour, slot, xs, zs, target, _, _ in own_first() + along_z() + along_x() + to_mate():
                copy_of(tensor, slot, piece(tensor, colour, xs, zs, c), target).wait_send()

        return begin, middle, end

    def follow(streams, order):
        for at in order:
            next(streams[at], None)

    pending, unsent = [], []
    for op in own:
        op.wait()
    streams = [
        gather(tensor, colour, tensor == W_IN) for tensor in (W_OUT, W_IN) for colour in (1, 0)
    ]
    follow(streams, (0, 1))
    swap = pltpu.make_async_remote_copy(
        src_ref=wi_ref, dst_ref=pair, send_sem=pair_sem.at[0], recv_sem=pair_sem.at[1],
        device_id=dev(x, z, 1 - c), device_id_type=MESH,
    )
    swap.start()

    swap.wait()
    mine, theirs = wi_ref[...].astype(F32), pair[...].astype(F32)
    both = jnp.concatenate(
        [jnp.where(c == 0, mine, theirs), jnp.where(c == 0, theirs, mine)], axis=0
    )
    half = jnp.where(c == 0, both[:, :512], both[:, 512:]).astype(BF)
    win[pl.ds(x, 1), pl.ds(z, 1), :, pl.ds(pl.multiple_of(c * 512, 512), 512)] = half.reshape(1, 1, 112, 512)
    follow(streams, WEIGHT_ORDER)
    for wait in pending:
        wait()

    def flip():
        @pl.loop(0, NX)
        def _(n):
            for j in range(8):
                part = win[n, :, :, pl.ds(128 * j, 128)].reshape(896, 128)
                win_t[pl.ds(128 * j, 128), pl.ds(pl.multiple_of(n * 896, 128), 896)] = part.T
            for j in range(7):
                part = wout[n, :, :, :, pl.ds(512 * j, 512)].reshape(256, 512)
                wout_t[pl.ds(512 * j, 512), pl.ds(pl.multiple_of(n * 256, 256), 256)] = part.T

    @pl.when(seg > 0)
    def _():
        flip()
        for wait in unsent:
            wait()

    @pl.when(seg == 0)
    def _():
        for op in tokens:
            op.wait()

    def hop(step, k, part, src, dst, to):
        rows = pl.ds(pl.multiple_of(k * CHUNK, CHUNK), CHUNK)
        cols = pl.ds(part * WIDE, WIDE)
        return pltpu.make_async_remote_copy(
            src_ref=src.at[rows, cols], dst_ref=dst.at[rows, cols],
            send_sem=hop_send.at[step, k, part], recv_sem=hop_recv.at[step, k, part],
            device_id=(me, to), device_id_type=MESH,
        )

    pooled[...] = jnp.zeros_like(pooled)

    def weight(start, count, side):
        length = jnp.where(side == 0, plen_ref[0], qlen_ref[0])
        at = lax.broadcasted_iota(jnp.int32, (count, 1), 0) + start
        return jnp.where(at < length, 1.0, 0.0) / length.astype(F32)

    def norm_of(side):
        total = jnp.sum(pooled[side], axis=0, keepdims=True)
        return total, lax.rsqrt(jnp.sum(total * total, axis=-1, keepdims=True) + EPS)

    def embed(side):
        total, inv = norm_of(side)
        unit = total * inv
        for k in range(PACKS):
            pack[side, k : k + 1, :] = unit[:, k * 128 : (k + 1) * 128]
        spot = lax.broadcasted_iota(jnp.int32, (32 - PACKS, 128), 1)
        pack[side, PACKS:32, :] = jnp.where(spot == pos_ref[0], 1.0, 0.0)
        emb[pl.ds(x, 1), pl.ds(z, 1), pl.ds(c, 1), pl.ds(32 * side, 32), :] = pack[side].reshape(1, 1, 1, 32, 128)
        return unit

    query_steps, passage_steps = exchange(EMB_Q), exchange(EMB_P)

    @pl.loop(0, CHUNKS)
    def _(k):
        rows = pl.ds(pl.multiple_of(k * CHUNK, CHUNK), CHUNK)

        square = jnp.zeros((CHUNK, 1), F32)
        v = jnp.zeros((CHUNK, KVW), F32)
        for n in range(PARTS):
            cols = pl.ds(n * WIDE, WIDE)

            @pl.when(seg > 0)
            def _():
                hop(0, k, n, outb, kept, seg).wait_recv()

            stream = kept[rows, cols].astype(F32)
            square = square + jnp.sum(stream * stream, axis=-1, keepdims=True)
            gained = (stream * gain_ref[:, cols]).astype(BF)
            v = v + jnp.dot(gained, win[n * SLABS : (n + 1) * SLABS].reshape(WIDE, KVW), preferred_element_type=F32)
        scale = lax.rsqrt(square * (1.0 / D) + EPS)
        scales[rows, :] = jnp.broadcast_to(scale, (CHUNK, 128))
        v = v * scale
        pre[rows, :] = v
        act[...] = gelu(v).astype(BF)

        def rise(n):
            cols = pl.ds(n * WIDE, WIDE)
            return jnp.dot(act[...], wout[:, :, :, :, cols].reshape(KVW, WIDE), preferred_element_type=F32)

        ahead = rise(0)
        for n in range(PARTS):
            cols = pl.ds(n * WIDE, WIDE)
            v, ahead = ahead, rise(n + 1) if n + 1 < PARTS else None
            outb[rows, cols] = (kept[rows, cols].astype(F32) + v).astype(BF)

            @pl.when(seg < NY - 1)
            def _():
                hop(0, k, n, outb, kept, seg + 1).start()

        @pl.when(seg == NY - 1)
        def _():
            side = (k * CHUNK) // SEQ
            total = jnp.zeros((8, D), F32)
            for part in range(CHUNK // 16):
                sub = pl.ds(pl.multiple_of(k * CHUNK + part * 16, 16), 16)
                scaled = outb[sub, :].astype(F32) * weight(part * 16 + (k * CHUNK) % SEQ, 16, side)
                total = total + scaled[0:8] + scaled[8:16]
            pooled[side] += total

            @pl.when(k == CHUNKS // 2 - 1)
            def _():
                embed(0)
                passage_steps[0]()

            @pl.when(k == CHUNKS * 3 // 4 - 1)
            def _():
                passage_steps[1]()

    @pl.when(seg == 0)
    def _():
        flip()
        for wait in unsent:
            wait()

    flat = emb.reshape(NQ * 64, 128)

    def unpack(side):
        for k in range(PACKS):
            embs[side, :, pl.ds(k * 128, 128)] = flat[pl.ds(32 * side + k, NQ, stride=64), :]

    def excess(logits, onehot):
        expo = jnp.exp(logits - jnp.max(logits, axis=1, keepdims=True))
        return (expo / jnp.sum(expo, axis=1, keepdims=True) - onehot) / NQ

    def spread_back(side, demb):
        total, inv = norm_of(side)
        along = jnp.sum(total * demb, axis=-1, keepdims=True)
        grad = inv * demb - total * (inv * inv * inv) * along
        for part in range(SEQ // 16):
            sub = pl.ds(side * SEQ + part * 16, 16)
            gin[sub, :] = (weight(part * 16, 16, side) * grad).astype(BF)

    @pl.when(seg == NY - 1)
    def _():
        unit = embed(1)
        query_steps[0]()
        passage_steps[2]()
        unpack(0)
        unit = jnp.broadcast_to(unit, (8, D))
        logits = lax.dot_general(unit, embs[0], NT, precision=HI, preferred_element_type=F32) / TEMP
        spot = lax.broadcasted_iota(jnp.int32, (8, NQ), 1)
        dlogits = excess(logits, jnp.where(spot == pos_ref[0], 1.0, 0.0))
        spread_back(1, jnp.dot(dlogits, embs[0], precision=HI, preferred_element_type=F32)[0:1] / TEMP)

    def passages_back():
        unpack(1)
        onehot = flat[pl.ds(PACKS, NQ, stride=64), :][:, 0:NQ]
        logits = lax.dot_general(embs[1], embs[0], NT, precision=HI, preferred_element_type=F32) / TEMP
        dlogits = excess(logits, onehot)
        jj = lax.broadcasted_iota(jnp.int32, (NQ, NQ), 1)
        col = jnp.sum(jnp.where(jj == me, dlogits, 0.0), axis=1, keepdims=True)
        spread_back(0, jnp.sum(col * embs[1], axis=0, keepdims=True) / TEMP)

    gacc[...] = jnp.zeros_like(gacc)

    @pl.loop(0, CHUNKS)
    def _(step):
        k = CHUNKS - 1 - step
        rows = pl.ds(pl.multiple_of(k * CHUNK, CHUNK), CHUNK)

        back = jnp.zeros((CHUNK, KVW), F32)
        for n in range(PARTS):
            cols = pl.ds(n * WIDE, WIDE)

            @pl.when(seg < NY - 1)
            def _():
                hop(1, k, n, grad_ref, gin, seg).wait_recv()

            back = back + jnp.dot(gin[rows, cols], wout_t[cols, :], preferred_element_type=F32)
        v = pre[rows, :]
        d = back * gelu_slope(v)
        along = jnp.sum(d * v, axis=-1, keepdims=True)
        dpre[...] = d.astype(BF)
        mean = along * (1.0 / D)
        scale = scales[rows, 0:1]

        def fall(n):
            return jnp.dot(dpre[...], win_t[:, pl.ds(n * WIDE, WIDE)], preferred_element_type=F32)

        ahead = fall(0)
        for n in range(PARTS):
            cols = pl.ds(n * WIDE, WIDE)
            dnormed, ahead = ahead, fall(n + 1) if n + 1 < PARTS else None
            unit = kept[rows, cols].astype(F32) * scale
            both = dnormed * unit
            gacc[:, cols] += sum(both[j : j + 8] for j in range(8, CHUNK, 8)) + both[0:8]
            res = gin[rows, cols].astype(F32) + scale * (dnormed * gain_ref[:, cols] - unit * mean)
            grad_ref[rows, cols] = res.astype(BF)

            @pl.when(seg > 0)
            def _():
                hop(1, k, n, grad_ref, gin, seg - 1).start()

        @pl.when((seg == NY - 1) & (step == CHUNKS // 4 - 1))
        def _():
            query_steps[1]()

        @pl.when((seg == NY - 1) & (step == CHUNKS // 2 - 1))
        def _():
            query_steps[2]()
            passages_back()

    def reduce(step, buf, at, peers):
        ops, sent = [], []
        for j, (target, source) in enumerate(peers):
            op = pltpu.make_async_remote_copy(
                src_ref=buf.at[at], dst_ref=buf.at[at],
                send_sem=red_send.at[step, j], recv_sem=red_recv.at[step, j],
                device_id=target, device_id_type=MESH,
            )
            op.start()
            sent.append(op.wait_send)
            ops.append(pltpu.make_async_remote_copy(
                src_ref=buf.at[source], dst_ref=buf.at[source],
                send_sem=red_send.at[step, j], recv_sem=red_recv.at[step, j],
                device_id=target, device_id_type=MESH,
            ).wait_recv)
        for op in ops:
            op()
        return sent

    at = x * NC + c
    gsum = jnp.sum(gacc[...], axis=0, keepdims=True)
    for k in range(PACKS):
        pack[0, k : k + 1, :] = gsum[:, k * 128 : (k + 1) * 128]
    near[at] = pack[0]
    peers = []
    for dx in FAR_X + (0,):
        for pc in (c, 1 - c) if dx else (1 - c,):
            peers.append((dev(xo(dx), z, pc), xo(-dx) * NC + pc))
    sent = reduce(0, near, at, peers)
    far[z] = jnp.sum(near[...], axis=0)
    sent += reduce(1, far, z, [(dev(x, zo(dz), c), zo(-dz)) for dz in FAR_Z])
    gsum_ref[...] = jnp.sum(far[...], axis=0)
    for op in sent:
        op()

    @pl.when(seg > 0)
    def _():
        for k in range(CHUNKS):
            for part in range(PARTS):
                hop(1, k, part, grad_ref, gin, seg).wait_send()

    @pl.when(seg < NY - 1)
    def _():
        for k in range(CHUNKS):
            for part in range(PARTS):
                hop(0, k, part, outb, kept, seg).wait_send()


def local(queries_in, passages_in, query_len, passage_len, positive, norm_gain, w_in, w_out):
    vmem, hbm = pl.BlockSpec(memory_space=pltpu.VMEM), pl.BlockSpec(memory_space=pltpu.HBM)
    smem = pl.BlockSpec(memory_space=pltpu.SMEM)
    rows = 2 * SEQ
    grads, gains = pl.pallas_call(
        kernel,
        out_shape=(
            jax.ShapeDtypeStruct((rows, D), BF),
            jax.ShapeDtypeStruct((32, 128), F32),
        ),
        in_specs=[smem] * 3 + [hbm] * 5,
        out_specs=(vmem, vmem),
        scratch_shapes=[
            pltpu.VMEM((NX, NZ, 112, KVW), BF),
            pltpu.VMEM((NX, NZ, NC, 16, D), BF),
            pltpu.VMEM((KVW, D), BF),
            pltpu.VMEM((D, KVW), BF),
            pltpu.VMEM((NX, NZ, NC, 64, 128), F32),
            pltpu.VMEM((2, NQ, D), F32),
            pltpu.VMEM((1, D), F32),
            pltpu.VMEM((56, KVW), BF),
            pltpu.VMEM((56, KVW), BF),
            pltpu.VMEM((rows, D), BF),
            pltpu.VMEM((rows, KVW), F32),
            pltpu.VMEM((rows, 128), F32),
            pltpu.VMEM((CHUNK, KVW), BF),
            pltpu.VMEM((rows, D), BF),
            pltpu.VMEM((rows, D), BF),
            pltpu.VMEM((CHUNK, KVW), BF),
            pltpu.VMEM((8, D), F32),
            pltpu.VMEM((2, 8, D), F32),
            pltpu.VMEM((2, 32, 128), F32),
            pltpu.VMEM((NX * NC, 32, 128), F32),
            pltpu.VMEM((NZ, 32, 128), F32),
            pltpu.SemaphoreType.DMA((4, 54)),
            pltpu.SemaphoreType.DMA((4, 54)),
            pltpu.SemaphoreType.DMA((2,)),
            pltpu.SemaphoreType.DMA((5,)),
            pltpu.SemaphoreType.DMA((2, CHUNKS, PARTS)),
            pltpu.SemaphoreType.DMA((2, CHUNKS, PARTS)),
            pltpu.SemaphoreType.DMA((2, 7)),
            pltpu.SemaphoreType.DMA((2, 7)),
        ],
        compiler_params=pltpu.CompilerParams(
            collective_id=0, has_side_effects=True, vmem_limit_bytes=58 * 1024 * 1024
        ),
        name="embedder_window",
    )(query_len, passage_len, positive, queries_in, passages_in, norm_gain, w_in[0], w_out[0])
    grads = grads.reshape(2, 1, 1, SEQ, D)
    return grads[1], grads[0], gains[:PACKS].reshape(1, D)


def solution(mesh):
    return jax.shard_map(
        local,
        mesh=mesh,
        in_specs=(
            P("dp", None, None),
            P("dp", None, None),
            P("dp"),
            P("dp"),
            P("dp"),
            P("segment", None),
            P("segment", "dp", None),
            P("segment", "dp", None),
        ),
        out_specs=(
            P("segment", "dp", None, None),
            P("segment", "dp", None, None),
            P("segment", None),
        ),
        check_vma=False,
    )
```

```python
import math

import jax
import jax.numpy as jnp
from jax import lax
from jax.experimental import pallas as pl
from jax.experimental.pallas import tpu as pltpu
from jax.sharding import PartitionSpec as P

MESH = pl.DeviceIdType.MESH
BF, F32 = jnp.bfloat16, jnp.float32
HI = lax.Precision.HIGHEST
D, KVW, SEQ, NQ = 3584, 1024, 64, 64
NX, NZ, NC, NY = 4, 8, 2, 4
TEMP = 0.02
CHUNK = 16
CHUNKS = 2 * SEQ // CHUNK
PARTS = 4
WIDE = D // PARTS
SLABS = NX // PARTS
PACKS = D // 128
FAR_X, FAR_Z = (2, 1, 3), (4, 3, 5, 2, 6, 1, 7)
WEIGHT_ORDER = (
    2, 3, 0, 1, 0, 2, 3, 2, 0, 1, 2, 3, 0, 2, 2, 0, 1, 2, 0, 0, 0, 0, 2, 2, 2, 3, 0, 2, 2, 0, 2, 0, 1, 3, 0, 2, 1, 3,
)
EPS = 1e-06
C0 = math.sqrt(2.0 / math.pi)
EMB_P, EMB_Q, W_IN, W_OUT = 0, 1, 2, 3
ALL = slice(None)
NT = (((1,), (1,)), ((), ()))


def gelu(v):
    return 0.5 * v * (1.0 + jnp.tanh(C0 * (v + 0.044715 * v * v * v)))


def gelu_slope(v):
    t = jnp.tanh(C0 * (v + 0.044715 * v * v * v))
    return 0.5 * (1.0 + t) + 0.5 * v * (1.0 - t * t) * C0 * (1.0 + 3.0 * 0.044715 * v * v)


def kernel(
    qlen_ref, plen_ref, pos_ref, queries_ref, passages_ref, gain_hbm, wi_hbm, wo_hbm,
    grad_ref, gsum_ref,
    win, wout, win_t, wout_t, emb, embs, gain_ref, wi_ref, pair, kept, pre, scales, act, outb, gin, dpre, gacc, pooled,
    pack, near, far,
    ag_send, ag_recv, pair_sem, tok_sem, hop_send, hop_recv, red_send, red_recv,
):
    me = lax.axis_index("dp")
    seg = lax.axis_index("segment")
    x, z, c = me // (NZ * NC), (me // NC) % NZ, me % NC

    def dev(px, pz, pc):
        return ((px * NZ + pz) * NC + pc, seg)

    def xo(by):
        return (x + by + NX) % NX

    def zo(by):
        return (z + by + NZ) % NZ

    own = [
        pltpu.make_async_copy(src, dst, tok_sem.at[2 + j])
        for j, (src, dst) in enumerate(((wo_hbm, wout.at[x, z, c]), (wi_hbm, wi_ref), (gain_hbm, gain_ref)))
    ]
    for op in own:
        op.start()
    tokens = [
        pltpu.make_async_copy(ref.at[0], kept.at[pl.ds(side * SEQ, SEQ)], tok_sem.at[side])
        for side, ref in enumerate((passages_ref, queries_ref))
    ]

    @pl.when(seg == 0)
    def _():
        for op in tokens:
            op.start()

    barrier = pltpu.get_barrier_semaphore()
    mates = [dev(xo(dx), z, pc) for dx in range(NX) for pc in (c, 1 - c)][1:]
    mates += [dev(x, zo(dz), c) for dz in range(1, NZ)]
    mates += [(me, (seg + by) % NY) for by in (1, NY - 1)]
    for mate in mates:
        pl.semaphore_signal(barrier, inc=1, device_id=mate, device_id_type=MESH)
    pl.semaphore_wait(barrier, len(mates))

    def piece(tensor, colour, xs, zs, pc):
        if tensor == W_IN:
            rows = pl.ds(0, 48) if colour == 0 else pl.ds(48, 64)
            return win.at[xs, zs, rows, pl.ds(pl.multiple_of(pc * 512, 512), 512)]
        if tensor == W_OUT:
            cols = pl.ds(0, 1408) if colour == 0 else pl.ds(1408, 2176)
            return wout.at[xs, zs, pl.ds(pc, 1), :, cols]
        rows = pl.ds(32 * tensor, 8) if colour == 0 else pl.ds(32 * tensor + 8, 24)
        return emb.at[xs, zs, pl.ds(pc, 1), rows, :]

    def copy_of(tensor, slot, ref, target):
        return pltpu.make_async_remote_copy(
            src_ref=ref, dst_ref=ref,
            send_sem=ag_send.at[tensor, slot], recv_sem=ag_recv.at[tensor, slot],
            device_id=target, device_id_type=MESH,
        )

    def one(at):
        return pl.ds(at, 1)

    def gather(tensor, colour, plus):
        def send(slot, xs, zs, target):
            op = copy_of(tensor, slot, piece(tensor, colour, xs, zs, c), target)
            op.start()
            unsent.append(op.wait_send)

        def got(slot, xs, zs):
            copy_of(tensor, slot, piece(tensor, colour, xs, zs, c), dev(x, z, 1 - c)).wait_recv()

        def pass_on(slot, xs, zs):
            send(slot, xs, zs, dev(x, z, 1 - c))
            other = copy_of(tensor, slot, piece(tensor, colour, xs, zs, 1 - c), dev(x, z, 1 - c))
            pending.append(other.wait_recv)

        up, down = dev(x, zo(1), c), dev(x, zo(-1), c)
        right, left = dev(xo(1), z, c), dev(xo(-1), z, c)
        if colour == 0:
            for dx in range(1, NX):
                send(dx - 1, one(x), one(z), dev(xo(dx), z, c))
            yield
            for dx in range(1, NX):
                got(dx - 1, one(xo(-dx)), one(z))
            send(3, ALL, one(z), up)
            send(4, ALL, one(z), down)
            pass_on(42, ALL, one(z))
            for step in range(1, 4):
                yield
                got(1 + 2 * step, ALL, one(zo(-step)))
                if step < 3:
                    send(3 + 2 * step, ALL, one(zo(-step)), up)
                else:
                    send(9, pl.ds(0, 2), one(zo(-3)), up)
                got(2 + 2 * step, ALL, one(zo(step)))
                if step < 3:
                    send(4 + 2 * step, ALL, one(zo(step)), down)
                else:
                    send(10, pl.ds(2, 2), one(zo(3)), down)
                pass_on(41 + 2 * step, ALL, one(zo(-step)))
                pass_on(42 + 2 * step, ALL, one(zo(step)))
            yield
            got(9, pl.ds(0, 2), one(zo(-4)))
            got(10, pl.ds(2, 2), one(zo(4)))
            pass_on(49, ALL, one(zo(4)))
            return
        offsets = (0, -1, 1, -2, 2, -3, 3, 4)

        def sideways(j):
            at = one(zo(offsets[j]))
            send(18 + j, one(x), at, right)
            send(26 + j, one(x), at, left)

        send(11, one(x), one(z), up)
        send(12, one(x), one(z), down)
        sideways(0)
        for step in range(1, 4):
            yield
            got(9 + 2 * step, one(x), one(zo(-step)))
            if step < 3:
                send(11 + 2 * step, one(x), one(zo(-step)), up)
            elif plus:
                send(17, one(x), one(zo(-3)), up)
            sideways(2 * step - 1)
            got(10 + 2 * step, one(x), one(zo(step)))
            if step < 3:
                send(12 + 2 * step, one(x), one(zo(step)), down)
            elif not plus:
                send(17, one(x), one(zo(3)), down)
            sideways(2 * step)
        yield
        got(17, one(x), one(zo(4)))
        sideways(7)
        pass_on(50, one(x), ALL)
        for j, by in enumerate(offsets):
            yield
            got(18 + j, one(xo(-1)), one(zo(by)))
            got(26 + j, one(xo(1)), one(zo(by)))
            if j % 2 == 0:
                send(34 + j, one(xo(-1)), one(zo(by)), right)
            else:
                send(34 + j, one(xo(1)), one(zo(by)), left)
        pass_on(51, one(xo(-1)), ALL)
        pass_on(52, one(xo(1)), ALL)
        yield
        for j, by in enumerate(offsets):
            got(34 + j, one(xo(2)), one(zo(by)))
        pass_on(53, one(xo(2)), ALL)

    def exchange(tensor):
        def own_first():
            ops = [(0, by - 1, one(x), one(z), dev(xo(by), z, c), one(xo(-by)), one(z)) for by in FAR_X]
            return ops + [(1, 2 + by, one(x), one(z), dev(x, zo(by), c), one(x), one(zo(-by))) for by in FAR_Z]

        def along_z():
            return [(0, 9 + by, ALL, one(z), dev(x, zo(by), c), ALL, one(zo(-by))) for by in FAR_Z]

        def along_x():
            return [(1, 16 + by, one(x), ALL, dev(xo(by), z, c), one(xo(-by)), ALL) for by in FAR_X]

        def to_mate():
            return [(colour, 20 + colour, ALL, ALL, dev(x, z, 1 - c), ALL, ALL) for colour in range(2)]

        def send(ops):
            for colour, slot, xs, zs, target, _, _ in ops:
                copy_of(tensor, slot, piece(tensor, colour, xs, zs, c), target).start()

        def got(ops, pc=c):
            for colour, slot, _, _, target, xs, zs in ops:
                copy_of(tensor, slot, piece(tensor, colour, xs, zs, pc), target).wait_recv()

        def begin():
            send(own_first())

        def middle():
            ops = own_first()
            got(ops[: NX - 1])
            send(along_z())
            got(ops[NX - 1 :])
            send(along_x())

        def end():
            got(along_x())
            send(to_mate()[1:])
            got(along_z())
            send(to_mate()[:1])
            got(to_mate()[::-1], 1 - c)
            for colour, slot, xs, zs, target, _, _ in own_first() + along_z() + along_x() + to_mate():
                copy_of(tensor, slot, piece(tensor, colour, xs, zs, c), target).wait_send()

        return begin, middle, end

    def follow(streams, order):
        for at in order:
            next(streams[at], None)

    pending, unsent = [], []
    for op in own:
        op.wait()
    streams = [
        gather(tensor, colour, tensor == W_IN) for tensor in (W_OUT, W_IN) for colour in (1, 0)
    ]
    follow(streams, (0, 1))
    swap = pltpu.make_async_remote_copy(
        src_ref=wi_ref, dst_ref=pair, send_sem=pair_sem.at[0], recv_sem=pair_sem.at[1],
        device_id=dev(x, z, 1 - c), device_id_type=MESH,
    )
    swap.start()

    swap.wait()
    mine, theirs = wi_ref[...].astype(F32), pair[...].astype(F32)
    both = jnp.concatenate(
        [jnp.where(c == 0, mine, theirs), jnp.where(c == 0, theirs, mine)], axis=0
    )
    half = jnp.where(c == 0, both[:, :512], both[:, 512:]).astype(BF)
    win[pl.ds(x, 1), pl.ds(z, 1), :, pl.ds(pl.multiple_of(c * 512, 512), 512)] = half.reshape(1, 1, 112, 512)
    follow(streams, WEIGHT_ORDER)
    for wait in pending:
        wait()

    def flip():
        @pl.loop(0, NX)
        def _(n):
            for j in range(8):
                part = win[n, :, :, pl.ds(128 * j, 128)].reshape(896, 128)
                win_t[pl.ds(128 * j, 128), pl.ds(pl.multiple_of(n * 896, 128), 896)] = part.T
            for j in range(7):
                part = wout[n, :, :, :, pl.ds(512 * j, 512)].reshape(256, 512)
                wout_t[pl.ds(512 * j, 512), pl.ds(pl.multiple_of(n * 256, 256), 256)] = part.T

    @pl.when(seg > 0)
    def _():
        flip()
        for wait in unsent:
            wait()

    @pl.when(seg == 0)
    def _():
        for op in tokens:
            op.wait()

    def hop(step, k, part, src, dst, to):
        rows = pl.ds(pl.multiple_of(k * CHUNK, CHUNK), CHUNK)
        cols = pl.ds(part * WIDE, WIDE)
        return pltpu.make_async_remote_copy(
            src_ref=src.at[rows, cols], dst_ref=dst.at[rows, cols],
            send_sem=hop_send.at[step, k, part], recv_sem=hop_recv.at[step, k, part],
            device_id=(me, to), device_id_type=MESH,
        )

    pooled[...] = jnp.zeros_like(pooled)

    def weight(start, count, side):
        length = jnp.where(side == 0, plen_ref[0], qlen_ref[0])
        at = lax.broadcasted_iota(jnp.int32, (count, 1), 0) + start
        return jnp.where(at < length, 1.0, 0.0) / length.astype(F32)

    def norm_of(side):
        total = jnp.sum(pooled[side], axis=0, keepdims=True)
        return total, lax.rsqrt(jnp.sum(total * total, axis=-1, keepdims=True) + EPS)

    def embed(side):
        total, inv = norm_of(side)
        unit = total * inv
        for k in range(PACKS):
            pack[side, k : k + 1, :] = unit[:, k * 128 : (k + 1) * 128]
        spot = lax.broadcasted_iota(jnp.int32, (32 - PACKS, 128), 1)
        pack[side, PACKS:32, :] = jnp.where(spot == pos_ref[0], 1.0, 0.0)
        emb[pl.ds(x, 1), pl.ds(z, 1), pl.ds(c, 1), pl.ds(32 * side, 32), :] = pack[side].reshape(1, 1, 1, 32, 128)
        return unit

    query_steps, passage_steps = exchange(EMB_Q), exchange(EMB_P)

    @pl.loop(0, CHUNKS)
    def _(k):
        rows = pl.ds(pl.multiple_of(k * CHUNK, CHUNK), CHUNK)

        square = jnp.zeros((CHUNK, 1), F32)
        v = jnp.zeros((CHUNK, KVW), F32)
        for n in range(PARTS):
            cols = pl.ds(n * WIDE, WIDE)

            @pl.when(seg > 0)
            def _():
                hop(0, k, n, outb, kept, seg).wait_recv()

            stream = kept[rows, cols].astype(F32)
            square = square + jnp.sum(stream * stream, axis=-1, keepdims=True)
            gained = (stream * gain_ref[:, cols]).astype(BF)
            v = v + jnp.dot(gained, win[n * SLABS : (n + 1) * SLABS].reshape(WIDE, KVW), preferred_element_type=F32)
        scale = lax.rsqrt(square * (1.0 / D) + EPS)
        scales[rows, :] = jnp.broadcast_to(scale, (CHUNK, 128))
        v = v * scale
        pre[rows, :] = v
        act[...] = gelu(v).astype(BF)

        def rise(n):
            cols = pl.ds(n * WIDE, WIDE)
            return jnp.dot(act[...], wout[:, :, :, :, cols].reshape(KVW, WIDE), preferred_element_type=F32)

        ahead = rise(0)
        for n in range(PARTS):
            cols = pl.ds(n * WIDE, WIDE)
            v, ahead = ahead, rise(n + 1) if n + 1 < PARTS else None
            outb[rows, cols] = (kept[rows, cols].astype(F32) + v).astype(BF)

            @pl.when(seg < NY - 1)
            def _():
                hop(0, k, n, outb, kept, seg + 1).start()

        @pl.when(seg == NY - 1)
        def _():
            side = (k * CHUNK) // SEQ
            total = jnp.zeros((8, D), F32)
            for part in range(CHUNK // 16):
                sub = pl.ds(pl.multiple_of(k * CHUNK + part * 16, 16), 16)
                scaled = outb[sub, :].astype(F32) * weight(part * 16 + (k * CHUNK) % SEQ, 16, side)
                total = total + scaled[0:8] + scaled[8:16]
            pooled[side] += total

            @pl.when(k == CHUNKS // 2 - 1)
            def _():
                embed(0)
                passage_steps[0]()

            @pl.when(k == CHUNKS * 3 // 4 - 1)
            def _():
                passage_steps[1]()

    @pl.when(seg == 0)
    def _():
        flip()
        for wait in unsent:
            wait()

    flat = emb.reshape(NQ * 64, 128)

    def unpack(side):
        for k in range(PACKS):
            embs[side, :, pl.ds(k * 128, 128)] = flat[pl.ds(32 * side + k, NQ, stride=64), :]

    def excess(logits, onehot):
        expo = jnp.exp(logits - jnp.max(logits, axis=1, keepdims=True))
        return (expo / jnp.sum(expo, axis=1, keepdims=True) - onehot) / NQ

    def spread_back(side, demb):
        total, inv = norm_of(side)
        along = jnp.sum(total * demb, axis=-1, keepdims=True)
        grad = inv * demb - total * (inv * inv * inv) * along
        for part in range(SEQ // 16):
            sub = pl.ds(side * SEQ + part * 16, 16)
            gin[sub, :] = (weight(part * 16, 16, side) * grad).astype(BF)

    @pl.when(seg == NY - 1)
    def _():
        unit = embed(1)
        query_steps[0]()
        passage_steps[2]()
        unpack(0)
        unit = jnp.broadcast_to(unit, (8, D))
        logits = lax.dot_general(unit, embs[0], NT, precision=HI, preferred_element_type=F32) / TEMP
        spot = lax.broadcasted_iota(jnp.int32, (8, NQ), 1)
        dlogits = excess(logits, jnp.where(spot == pos_ref[0], 1.0, 0.0))
        spread_back(1, jnp.dot(dlogits, embs[0], precision=HI, preferred_element_type=F32)[0:1] / TEMP)

    def passages_back():
        unpack(1)
        onehot = flat[pl.ds(PACKS, NQ, stride=64), :][:, 0:NQ]
        logits = lax.dot_general(embs[1], embs[0], NT, precision=HI, preferred_element_type=F32) / TEMP
        dlogits = excess(logits, onehot)
        jj = lax.broadcasted_iota(jnp.int32, (NQ, NQ), 1)
        col = jnp.sum(jnp.where(jj == me, dlogits, 0.0), axis=1, keepdims=True)
        spread_back(0, jnp.sum(col * embs[1], axis=0, keepdims=True) / TEMP)

    gacc[...] = jnp.zeros_like(gacc)

    @pl.loop(0, CHUNKS)
    def _(step):
        k = CHUNKS - 1 - step
        rows = pl.ds(pl.multiple_of(k * CHUNK, CHUNK), CHUNK)

        back = jnp.zeros((CHUNK, KVW), F32)
        for n in range(PARTS):
            cols = pl.ds(n * WIDE, WIDE)

            @pl.when(seg < NY - 1)
            def _():
                hop(1, k, n, grad_ref, gin, seg).wait_recv()

            back = back + jnp.dot(gin[rows, cols], wout_t[cols, :], preferred_element_type=F32)
        v = pre[rows, :]
        d = back * gelu_slope(v)
        along = jnp.sum(d * v, axis=-1, keepdims=True)
        dpre[...] = d.astype(BF)
        mean = along * (1.0 / D)
        scale = scales[rows, 0:1]

        def fall(n):
            return jnp.dot(dpre[...], win_t[:, pl.ds(n * WIDE, WIDE)], preferred_element_type=F32)

        ahead = fall(0)
        for n in range(PARTS):
            cols = pl.ds(n * WIDE, WIDE)
            dnormed, ahead = ahead, fall(n + 1) if n + 1 < PARTS else None
            unit = kept[rows, cols].astype(F32) * scale
            both = dnormed * unit
            gacc[:, cols] += sum(both[j : j + 8] for j in range(8, CHUNK, 8)) + both[0:8]
            res = gin[rows, cols].astype(F32) + scale * (dnormed * gain_ref[:, cols] - unit * mean)
            grad_ref[rows, cols] = res.astype(BF)

            @pl.when(seg > 0)
            def _():
                hop(1, k, n, grad_ref, gin, seg - 1).start()

        @pl.when((seg == NY - 1) & (step == CHUNKS // 4 - 1))
        def _():
            query_steps[1]()

        @pl.when((seg == NY - 1) & (step == CHUNKS // 2 - 1))
        def _():
            query_steps[2]()
            passages_back()

    def reduce(step, buf, at, peers):
        ops, sent = [], []
        for j, (target, source) in enumerate(peers):
            op = pltpu.make_async_remote_copy(
                src_ref=buf.at[at], dst_ref=buf.at[at],
                send_sem=red_send.at[step, j], recv_sem=red_recv.at[step, j],
                device_id=target, device_id_type=MESH,
            )
            op.start()
            sent.append(op.wait_send)
            ops.append(pltpu.make_async_remote_copy(
                src_ref=buf.at[source], dst_ref=buf.at[source],
                send_sem=red_send.at[step, j], recv_sem=red_recv.at[step, j],
                device_id=target, device_id_type=MESH,
            ).wait_recv)
        for op in ops:
            op()
        return sent

    at = x * NC + c
    gsum = jnp.sum(gacc[...], axis=0, keepdims=True)
    for k in range(PACKS):
        pack[0, k : k + 1, :] = gsum[:, k * 128 : (k + 1) * 128]
    near[at] = pack[0]
    peers = []
    for dx in FAR_X + (0,):
        for pc in (c, 1 - c) if dx else (1 - c,):
            peers.append((dev(xo(dx), z, pc), xo(-dx) * NC + pc))
    sent = reduce(0, near, at, peers)
    far[z] = jnp.sum(near[...], axis=0)
    sent += reduce(1, far, z, [(dev(x, zo(dz), c), zo(-dz)) for dz in FAR_Z])
    gsum_ref[...] = jnp.sum(far[...], axis=0)
    for op in sent:
        op()

    @pl.when(seg > 0)
    def _():
        for k in range(CHUNKS):
            for part in range(PARTS):
                hop(1, k, part, grad_ref, gin, seg).wait_send()

    @pl.when(seg < NY - 1)
    def _():
        for k in range(CHUNKS):
            for part in range(PARTS):
                hop(0, k, part, outb, kept, seg).wait_send()


def local(queries_in, passages_in, query_len, passage_len, positive, norm_gain, w_in, w_out):
    vmem, hbm = pl.BlockSpec(memory_space=pltpu.VMEM), pl.BlockSpec(memory_space=pltpu.HBM)
    smem = pl.BlockSpec(memory_space=pltpu.SMEM)
    rows = 2 * SEQ
    grads, gains = pl.pallas_call(
        kernel,
        out_shape=(
            jax.ShapeDtypeStruct((rows, D), BF),
            jax.ShapeDtypeStruct((32, 128), F32),
        ),
        in_specs=[smem] * 3 + [hbm] * 5,
        out_specs=(vmem, vmem),
        scratch_shapes=[
            pltpu.VMEM((NX, NZ, 112, KVW), BF),
            pltpu.VMEM((NX, NZ, NC, 16, D), BF),
            pltpu.VMEM((KVW, D), BF),
            pltpu.VMEM((D, KVW), BF),
            pltpu.VMEM((NX, NZ, NC, 64, 128), F32),
            pltpu.VMEM((2, NQ, D), F32),
            pltpu.VMEM((1, D), F32),
            pltpu.VMEM((56, KVW), BF),
            pltpu.VMEM((56, KVW), BF),
            pltpu.VMEM((rows, D), BF),
            pltpu.VMEM((rows, KVW), F32),
            pltpu.VMEM((rows, 128), F32),
            pltpu.VMEM((CHUNK, KVW), BF),
            pltpu.VMEM((rows, D), BF),
            pltpu.VMEM((rows, D), BF),
            pltpu.VMEM((CHUNK, KVW), BF),
            pltpu.VMEM((8, D), F32),
            pltpu.VMEM((2, 8, D), F32),
            pltpu.VMEM((2, 32, 128), F32),
            pltpu.VMEM((NX * NC, 32, 128), F32),
            pltpu.VMEM((NZ, 32, 128), F32),
            pltpu.SemaphoreType.DMA((4, 54)),
            pltpu.SemaphoreType.DMA((4, 54)),
            pltpu.SemaphoreType.DMA((2,)),
            pltpu.SemaphoreType.DMA((5,)),
            pltpu.SemaphoreType.DMA((2, CHUNKS, PARTS)),
            pltpu.SemaphoreType.DMA((2, CHUNKS, PARTS)),
            pltpu.SemaphoreType.DMA((2, 7)),
            pltpu.SemaphoreType.DMA((2, 7)),
        ],
        compiler_params=pltpu.CompilerParams(
            collective_id=0, has_side_effects=True, vmem_limit_bytes=58 * 1024 * 1024
        ),
        name="embedder_window",
    )(query_len, passage_len, positive, queries_in, passages_in, norm_gain, w_in[0], w_out[0])
    grads = grads.reshape(2, 1, 1, SEQ, D)
    return grads[1], grads[0], gains[:PACKS].reshape(1, D)


def solution(mesh):
    return jax.shard_map(
        local,
        mesh=mesh,
        in_specs=(
            P("dp", None, None),
            P("dp", None, None),
            P("dp"),
            P("dp"),
            P("dp"),
            P("segment", None),
            P("segment", "dp", None),
            P("segment", "dp", None),
        ),
        out_specs=(
            P("segment", "dp", None, None),
            P("segment", "dp", None, None),
            P("segment", None),
        ),
        check_vma=False,
    )
```

```python
import math

import jax
import jax.numpy as jnp
from jax import lax
from jax.experimental import pallas as pl
from jax.experimental.pallas import tpu as pltpu
from jax.sharding import PartitionSpec as P

MESH = pl.DeviceIdType.MESH
BF, F32 = jnp.bfloat16, jnp.float32
HI = lax.Precision.HIGHEST
D, KVW, SEQ, NQ = 3584, 1024, 64, 64
NX, NZ, NC, NY = 4, 8, 2, 4
TEMP = 0.02
CHUNK = 16
CHUNKS = 2 * SEQ // CHUNK
PARTS = 4
WIDE = D // PARTS
SLABS = NX // PARTS
PACKS = D // 128
FAR_X, FAR_Z = (2, 1, 3), (4, 3, 5, 2, 6, 1, 7)
WEIGHT_ORDER = (
    2, 3, 0, 1, 0, 2, 3, 2, 0, 1, 2, 3, 0, 2, 2, 0, 1, 2, 0, 0, 0, 0, 2, 2, 2, 3, 0, 2, 2, 0, 2, 0, 1, 3, 0, 2, 1, 3,
)
EPS = 1e-06
C0 = math.sqrt(2.0 / math.pi)
EMB_P, EMB_Q, W_IN, W_OUT = 0, 1, 2, 3
ALL = slice(None)
NT = (((1,), (1,)), ((), ()))


def gelu(v):
    return 0.5 * v * (1.0 + jnp.tanh(C0 * (v + 0.044715 * v * v * v)))


def gelu_slope(v):
    t = jnp.tanh(C0 * (v + 0.044715 * v * v * v))
    return 0.5 * (1.0 + t) + 0.5 * v * (1.0 - t * t) * C0 * (1.0 + 3.0 * 0.044715 * v * v)


def kernel(
    qlen_ref, plen_ref, pos_ref, queries_ref, passages_ref, gain_hbm, wi_hbm, wo_hbm,
    grad_ref, gsum_ref,
    win, wout, win_t, wout_t, emb, embs, gain_ref, wi_ref, pair, kept, pre, scales, act, outb, gin, dpre, gacc, pooled,
    pack, near, far,
    ag_send, ag_recv, pair_sem, tok_sem, hop_send, hop_recv, red_send, red_recv,
):
    me = lax.axis_index("dp")
    seg = lax.axis_index("segment")
    x, z, c = me // (NZ * NC), (me // NC) % NZ, me % NC

    def dev(px, pz, pc):
        return ((px * NZ + pz) * NC + pc, seg)

    def xo(by):
        return (x + by + NX) % NX

    def zo(by):
        return (z + by + NZ) % NZ

    own = [
        pltpu.make_async_copy(src, dst, tok_sem.at[2 + j])
        for j, (src, dst) in enumerate(((wo_hbm, wout.at[x, z, c]), (wi_hbm, wi_ref), (gain_hbm, gain_ref)))
    ]
    for op in own:
        op.start()
    tokens = [
        pltpu.make_async_copy(ref.at[0], kept.at[pl.ds(side * SEQ, SEQ)], tok_sem.at[side])
        for side, ref in enumerate((passages_ref, queries_ref))
    ]

    @pl.when(seg == 0)
    def _():
        for op in tokens:
            op.start()

    barrier = pltpu.get_barrier_semaphore()
    mates = [dev(xo(dx), z, pc) for dx in range(NX) for pc in (c, 1 - c)][1:]
    mates += [dev(x, zo(dz), c) for dz in range(1, NZ)]
    mates += [(me, (seg + by) % NY) for by in (1, NY - 1)]
    for mate in mates:
        pl.semaphore_signal(barrier, inc=1, device_id=mate, device_id_type=MESH)
    pl.semaphore_wait(barrier, len(mates))

    def piece(tensor, colour, xs, zs, pc):
        if tensor == W_IN:
            rows = pl.ds(0, 48) if colour == 0 else pl.ds(48, 64)
            return win.at[xs, zs, rows, pl.ds(pl.multiple_of(pc * 512, 512), 512)]
        if tensor == W_OUT:
            cols = pl.ds(0, 1408) if colour == 0 else pl.ds(1408, 2176)
            return wout.at[xs, zs, pl.ds(pc, 1), :, cols]
        rows = pl.ds(32 * tensor, 8) if colour == 0 else pl.ds(32 * tensor + 8, 24)
        return emb.at[xs, zs, pl.ds(pc, 1), rows, :]

    def copy_of(tensor, slot, ref, target):
        return pltpu.make_async_remote_copy(
            src_ref=ref, dst_ref=ref,
            send_sem=ag_send.at[tensor, slot], recv_sem=ag_recv.at[tensor, slot],
            device_id=target, device_id_type=MESH,
        )

    def one(at):
        return pl.ds(at, 1)

    def gather(tensor, colour, plus):
        def send(slot, xs, zs, target):
            op = copy_of(tensor, slot, piece(tensor, colour, xs, zs, c), target)
            op.start()
            unsent.append(op.wait_send)

        def got(slot, xs, zs):
            copy_of(tensor, slot, piece(tensor, colour, xs, zs, c), dev(x, z, 1 - c)).wait_recv()

        def pass_on(slot, xs, zs):
            send(slot, xs, zs, dev(x, z, 1 - c))
            other = copy_of(tensor, slot, piece(tensor, colour, xs, zs, 1 - c), dev(x, z, 1 - c))
            pending.append(other.wait_recv)

        up, down = dev(x, zo(1), c), dev(x, zo(-1), c)
        right, left = dev(xo(1), z, c), dev(xo(-1), z, c)
        if colour == 0:
            for dx in range(1, NX):
                send(dx - 1, one(x), one(z), dev(xo(dx), z, c))
            yield
            for dx in range(1, NX):
                got(dx - 1, one(xo(-dx)), one(z))
            send(3, ALL, one(z), up)
            send(4, ALL, one(z), down)
            pass_on(42, ALL, one(z))
            for step in range(1, 4):
                yield
                got(1 + 2 * step, ALL, one(zo(-step)))
                if step < 3:
                    send(3 + 2 * step, ALL, one(zo(-step)), up)
                else:
                    send(9, pl.ds(0, 2), one(zo(-3)), up)
                got(2 + 2 * step, ALL, one(zo(step)))
                if step < 3:
                    send(4 + 2 * step, ALL, one(zo(step)), down)
                else:
                    send(10, pl.ds(2, 2), one(zo(3)), down)
                pass_on(41 + 2 * step, ALL, one(zo(-step)))
                pass_on(42 + 2 * step, ALL, one(zo(step)))
            yield
            got(9, pl.ds(0, 2), one(zo(-4)))
            got(10, pl.ds(2, 2), one(zo(4)))
            pass_on(49, ALL, one(zo(4)))
            return
        offsets = (0, -1, 1, -2, 2, -3, 3, 4)

        def sideways(j):
            at = one(zo(offsets[j]))
            send(18 + j, one(x), at, right)
            send(26 + j, one(x), at, left)

        send(11, one(x), one(z), up)
        send(12, one(x), one(z), down)
        sideways(0)
        for step in range(1, 4):
            yield
            got(9 + 2 * step, one(x), one(zo(-step)))
            if step < 3:
                send(11 + 2 * step, one(x), one(zo(-step)), up)
            elif plus:
                send(17, one(x), one(zo(-3)), up)
            sideways(2 * step - 1)
            got(10 + 2 * step, one(x), one(zo(step)))
            if step < 3:
                send(12 + 2 * step, one(x), one(zo(step)), down)
            elif not plus:
                send(17, one(x), one(zo(3)), down)
            sideways(2 * step)
        yield
        got(17, one(x), one(zo(4)))
        sideways(7)
        pass_on(50, one(x), ALL)
        for j, by in enumerate(offsets):
            yield
            got(18 + j, one(xo(-1)), one(zo(by)))
            got(26 + j, one(xo(1)), one(zo(by)))
            if j % 2 == 0:
                send(34 + j, one(xo(-1)), one(zo(by)), right)
            else:
                send(34 + j, one(xo(1)), one(zo(by)), left)
        pass_on(51, one(xo(-1)), ALL)
        pass_on(52, one(xo(1)), ALL)
        yield
        for j, by in enumerate(offsets):
            got(34 + j, one(xo(2)), one(zo(by)))
        pass_on(53, one(xo(2)), ALL)

    def exchange(tensor):
        def own_first():
            ops = [(0, by - 1, one(x), one(z), dev(xo(by), z, c), one(xo(-by)), one(z)) for by in FAR_X]
            return ops + [(1, 2 + by, one(x), one(z), dev(x, zo(by), c), one(x), one(zo(-by))) for by in FAR_Z]

        def along_z():
            return [(0, 9 + by, ALL, one(z), dev(x, zo(by), c), ALL, one(zo(-by))) for by in FAR_Z]

        def along_x():
            return [(1, 16 + by, one(x), ALL, dev(xo(by), z, c), one(xo(-by)), ALL) for by in FAR_X]

        def to_mate():
            return [(colour, 20 + colour, ALL, ALL, dev(x, z, 1 - c), ALL, ALL) for colour in range(2)]

        def send(ops):
            for colour, slot, xs, zs, target, _, _ in ops:
                copy_of(tensor, slot, piece(tensor, colour, xs, zs, c), target).start()

        def got(ops, pc=c):
            for colour, slot, _, _, target, xs, zs in ops:
                copy_of(tensor, slot, piece(tensor, colour, xs, zs, pc), target).wait_recv()

        def begin():
            send(own_first())

        def middle():
            ops = own_first()
            got(ops[: NX - 1])
            send(along_z())
            got(ops[NX - 1 :])
            send(along_x())

        def end():
            got(along_x())
            send(to_mate()[1:])
            got(along_z())
            send(to_mate()[:1])
            got(to_mate()[::-1], 1 - c)
            for colour, slot, xs, zs, target, _, _ in own_first() + along_z() + along_x() + to_mate():
                copy_of(tensor, slot, piece(tensor, colour, xs, zs, c), target).wait_send()

        return begin, middle, end

    def follow(streams, order):
        for at in order:
            next(streams[at], None)

    pending, unsent = [], []
    for op in own:
        op.wait()
    streams = [
        gather(tensor, colour, tensor == W_IN) for tensor in (W_OUT, W_IN) for colour in (1, 0)
    ]
    follow(streams, (0, 1))
    swap = pltpu.make_async_remote_copy(
        src_ref=wi_ref, dst_ref=pair, send_sem=pair_sem.at[0], recv_sem=pair_sem.at[1],
        device_id=dev(x, z, 1 - c), device_id_type=MESH,
    )
    swap.start()

    swap.wait()
    mine, theirs = wi_ref[...].astype(F32), pair[...].astype(F32)
    both = jnp.concatenate(
        [jnp.where(c == 0, mine, theirs), jnp.where(c == 0, theirs, mine)], axis=0
    )
    half = jnp.where(c == 0, both[:, :512], both[:, 512:]).astype(BF)
    win[pl.ds(x, 1), pl.ds(z, 1), :, pl.ds(pl.multiple_of(c * 512, 512), 512)] = half.reshape(1, 1, 112, 512)
    follow(streams, WEIGHT_ORDER)
    for wait in pending:
        wait()

    def flip():
        @pl.loop(0, NX)
        def _(n):
            for j in range(8):
                part = win[n, :, :, pl.ds(128 * j, 128)].reshape(896, 128)
                win_t[pl.ds(128 * j, 128), pl.ds(pl.multiple_of(n * 896, 128), 896)] = part.T
            for j in range(7):
                part = wout[n, :, :, :, pl.ds(512 * j, 512)].reshape(256, 512)
                wout_t[pl.ds(512 * j, 512), pl.ds(pl.multiple_of(n * 256, 256), 256)] = part.T

    @pl.when(seg > 0)
    def _():
        flip()
        for wait in unsent:
            wait()

    @pl.when(seg == 0)
    def _():
        for op in tokens:
            op.wait()

    def hop(step, k, part, src, dst, to):
        rows = pl.ds(pl.multiple_of(k * CHUNK, CHUNK), CHUNK)
        cols = pl.ds(part * WIDE, WIDE)
        return pltpu.make_async_remote_copy(
            src_ref=src.at[rows, cols], dst_ref=dst.at[rows, cols],
            send_sem=hop_send.at[step, k, part], recv_sem=hop_recv.at[step, k, part],
            device_id=(me, to), device_id_type=MESH,
        )

    pooled[...] = jnp.zeros_like(pooled)

    def weight(start, count, side):
        length = jnp.where(side == 0, plen_ref[0], qlen_ref[0])
        at = lax.broadcasted_iota(jnp.int32, (count, 1), 0) + start
        return jnp.where(at < length, 1.0, 0.0) / length.astype(F32)

    def norm_of(side):
        total = jnp.sum(pooled[side], axis=0, keepdims=True)
        return total, lax.rsqrt(jnp.sum(total * total, axis=-1, keepdims=True) + EPS)

    def embed(side):
        total, inv = norm_of(side)
        unit = total * inv
        for k in range(PACKS):
            pack[side, k : k + 1, :] = unit[:, k * 128 : (k + 1) * 128]
        spot = lax.broadcasted_iota(jnp.int32, (32 - PACKS, 128), 1)
        pack[side, PACKS:32, :] = jnp.where(spot == pos_ref[0], 1.0, 0.0)
        emb[pl.ds(x, 1), pl.ds(z, 1), pl.ds(c, 1), pl.ds(32 * side, 32), :] = pack[side].reshape(1, 1, 1, 32, 128)
        return unit

    query_steps, passage_steps = exchange(EMB_Q), exchange(EMB_P)

    @pl.loop(0, CHUNKS)
    def _(k):
        rows = pl.ds(pl.multiple_of(k * CHUNK, CHUNK), CHUNK)

        square = jnp.zeros((CHUNK, 1), F32)
        v = jnp.zeros((CHUNK, KVW), F32)
        for n in range(PARTS):
            cols = pl.ds(n * WIDE, WIDE)

            @pl.when(seg > 0)
            def _():
                hop(0, k, n, outb, kept, seg).wait_recv()

            stream = kept[rows, cols].astype(F32)
            square = square + jnp.sum(stream * stream, axis=-1, keepdims=True)
            gained = (stream * gain_ref[:, cols]).astype(BF)
            v = v + jnp.dot(gained, win[n * SLABS : (n + 1) * SLABS].reshape(WIDE, KVW), preferred_element_type=F32)
        scale = lax.rsqrt(square * (1.0 / D) + EPS)
        scales[rows, :] = jnp.broadcast_to(scale, (CHUNK, 128))
        v = v * scale
        pre[rows, :] = v
        act[...] = gelu(v).astype(BF)

        def rise(n):
            cols = pl.ds(n * WIDE, WIDE)
            return jnp.dot(act[...], wout[:, :, :, :, cols].reshape(KVW, WIDE), preferred_element_type=F32)

        ahead = rise(0)
        for n in range(PARTS):
            cols = pl.ds(n * WIDE, WIDE)
            v, ahead = ahead, rise(n + 1) if n + 1 < PARTS else None
            outb[rows, cols] = (kept[rows, cols].astype(F32) + v).astype(BF)

            @pl.when(seg < NY - 1)
            def _():
                hop(0, k, n, outb, kept, seg + 1).start()

        @pl.when(seg == NY - 1)
        def _():
            side = (k * CHUNK) // SEQ
            total = jnp.zeros((8, D), F32)
            for part in range(CHUNK // 16):
                sub = pl.ds(pl.multiple_of(k * CHUNK + part * 16, 16), 16)
                scaled = outb[sub, :].astype(F32) * weight(part * 16 + (k * CHUNK) % SEQ, 16, side)
                total = total + scaled[0:8] + scaled[8:16]
            pooled[side] += total

            @pl.when(k == CHUNKS // 2 - 1)
            def _():
                embed(0)
                passage_steps[0]()

            @pl.when(k == CHUNKS * 3 // 4 - 1)
            def _():
                passage_steps[1]()

    @pl.when(seg == 0)
    def _():
        flip()
        for wait in unsent:
            wait()

    flat = emb.reshape(NQ * 64, 128)

    def unpack(side):
        for k in range(PACKS):
            embs[side, :, pl.ds(k * 128, 128)] = flat[pl.ds(32 * side + k, NQ, stride=64), :]

    def excess(logits, onehot):
        expo = jnp.exp(logits - jnp.max(logits, axis=1, keepdims=True))
        return (expo / jnp.sum(expo, axis=1, keepdims=True) - onehot) / NQ

    def spread_back(side, demb):
        total, inv = norm_of(side)
        along = jnp.sum(total * demb, axis=-1, keepdims=True)
        grad = inv * demb - total * (inv * inv * inv) * along
        for part in range(SEQ // 16):
            sub = pl.ds(side * SEQ + part * 16, 16)
            gin[sub, :] = (weight(part * 16, 16, side) * grad).astype(BF)

    @pl.when(seg == NY - 1)
    def _():
        unit = embed(1)
        query_steps[0]()
        passage_steps[2]()
        unpack(0)
        unit = jnp.broadcast_to(unit, (8, D))
        logits = lax.dot_general(unit, embs[0], NT, precision=HI, preferred_element_type=F32) / TEMP
        spot = lax.broadcasted_iota(jnp.int32, (8, NQ), 1)
        dlogits = excess(logits, jnp.where(spot == pos_ref[0], 1.0, 0.0))
        spread_back(1, jnp.dot(dlogits, embs[0], precision=HI, preferred_element_type=F32)[0:1] / TEMP)

    def passages_back():
        unpack(1)
        onehot = flat[pl.ds(PACKS, NQ, stride=64), :][:, 0:NQ]
        logits = lax.dot_general(embs[1], embs[0], NT, precision=HI, preferred_element_type=F32) / TEMP
        dlogits = excess(logits, onehot)
        jj = lax.broadcasted_iota(jnp.int32, (NQ, NQ), 1)
        col = jnp.sum(jnp.where(jj == me, dlogits, 0.0), axis=1, keepdims=True)
        spread_back(0, jnp.sum(col * embs[1], axis=0, keepdims=True) / TEMP)

    gacc[...] = jnp.zeros_like(gacc)

    @pl.loop(0, CHUNKS)
    def _(step):
        k = CHUNKS - 1 - step
        rows = pl.ds(pl.multiple_of(k * CHUNK, CHUNK), CHUNK)

        back = jnp.zeros((CHUNK, KVW), F32)
        for n in range(PARTS):
            cols = pl.ds(n * WIDE, WIDE)

            @pl.when(seg < NY - 1)
            def _():
                hop(1, k, n, grad_ref, gin, seg).wait_recv()

            back = back + jnp.dot(gin[rows, cols], wout_t[cols, :], preferred_element_type=F32)
        v = pre[rows, :]
        d = back * gelu_slope(v)
        along = jnp.sum(d * v, axis=-1, keepdims=True)
        dpre[...] = d.astype(BF)
        mean = along * (1.0 / D)
        scale = scales[rows, 0:1]

        def fall(n):
            return jnp.dot(dpre[...], win_t[:, pl.ds(n * WIDE, WIDE)], preferred_element_type=F32)

        ahead = fall(0)
        for n in range(PARTS):
            cols = pl.ds(n * WIDE, WIDE)
            dnormed, ahead = ahead, fall(n + 1) if n + 1 < PARTS else None
            unit = kept[rows, cols].astype(F32) * scale
            both = dnormed * unit
            gacc[:, cols] += sum(both[j : j + 8] for j in range(8, CHUNK, 8)) + both[0:8]
            res = gin[rows, cols].astype(F32) + scale * (dnormed * gain_ref[:, cols] - unit * mean)
            grad_ref[rows, cols] = res.astype(BF)

            @pl.when(seg > 0)
            def _():
                hop(1, k, n, grad_ref, gin, seg - 1).start()

        @pl.when((seg == NY - 1) & (step == 0))
        def _():
            query_steps[1]()

        @pl.when((seg == NY - 1) & (step == CHUNKS // 2 - 1))
        def _():
            query_steps[2]()
            passages_back()

    def reduce(step, buf, at, peers):
        ops, sent = [], []
        for j, (target, source) in enumerate(peers):
            op = pltpu.make_async_remote_copy(
                src_ref=buf.at[at], dst_ref=buf.at[at],
                send_sem=red_send.at[step, j], recv_sem=red_recv.at[step, j],
                device_id=target, device_id_type=MESH,
            )
            op.start()
            sent.append(op.wait_send)
            ops.append(pltpu.make_async_remote_copy(
                src_ref=buf.at[source], dst_ref=buf.at[source],
                send_sem=red_send.at[step, j], recv_sem=red_recv.at[step, j],
                device_id=target, device_id_type=MESH,
            ).wait_recv)
        for op in ops:
            op()
        return sent

    at = x * NC + c
    gsum = jnp.sum(gacc[...], axis=0, keepdims=True)
    for k in range(PACKS):
        pack[0, k : k + 1, :] = gsum[:, k * 128 : (k + 1) * 128]
    near[at] = pack[0]
    peers = []
    for dx in FAR_X + (0,):
        for pc in (c, 1 - c) if dx else (1 - c,):
            peers.append((dev(xo(dx), z, pc), xo(-dx) * NC + pc))
    sent = reduce(0, near, at, peers)
    far[z] = jnp.sum(near[...], axis=0)
    sent += reduce(1, far, z, [(dev(x, zo(dz), c), zo(-dz)) for dz in FAR_Z])
    gsum_ref[...] = jnp.sum(far[...], axis=0)
    for op in sent:
        op()

    @pl.when(seg > 0)
    def _():
        for k in range(CHUNKS):
            for part in range(PARTS):
                hop(1, k, part, grad_ref, gin, seg).wait_send()

    @pl.when(seg < NY - 1)
    def _():
        for k in range(CHUNKS):
            for part in range(PARTS):
                hop(0, k, part, outb, kept, seg).wait_send()


def local(queries_in, passages_in, query_len, passage_len, positive, norm_gain, w_in, w_out):
    vmem, hbm = pl.BlockSpec(memory_space=pltpu.VMEM), pl.BlockSpec(memory_space=pltpu.HBM)
    smem = pl.BlockSpec(memory_space=pltpu.SMEM)
    rows = 2 * SEQ
    grads, gains = pl.pallas_call(
        kernel,
        out_shape=(
            jax.ShapeDtypeStruct((rows, D), BF),
            jax.ShapeDtypeStruct((32, 128), F32),
        ),
        in_specs=[smem] * 3 + [hbm] * 5,
        out_specs=(vmem, vmem),
        scratch_shapes=[
            pltpu.VMEM((NX, NZ, 112, KVW), BF),
            pltpu.VMEM((NX, NZ, NC, 16, D), BF),
            pltpu.VMEM((KVW, D), BF),
            pltpu.VMEM((D, KVW), BF),
            pltpu.VMEM((NX, NZ, NC, 64, 128), F32),
            pltpu.VMEM((2, NQ, D), F32),
            pltpu.VMEM((1, D), F32),
            pltpu.VMEM((56, KVW), BF),
            pltpu.VMEM((56, KVW), BF),
            pltpu.VMEM((rows, D), BF),
            pltpu.VMEM((rows, KVW), F32),
            pltpu.VMEM((rows, 128), F32),
            pltpu.VMEM((CHUNK, KVW), BF),
            pltpu.VMEM((rows, D), BF),
            pltpu.VMEM((rows, D), BF),
            pltpu.VMEM((CHUNK, KVW), BF),
            pltpu.VMEM((8, D), F32),
            pltpu.VMEM((2, 8, D), F32),
            pltpu.VMEM((2, 32, 128), F32),
            pltpu.VMEM((NX * NC, 32, 128), F32),
            pltpu.VMEM((NZ, 32, 128), F32),
            pltpu.SemaphoreType.DMA((4, 54)),
            pltpu.SemaphoreType.DMA((4, 54)),
            pltpu.SemaphoreType.DMA((2,)),
            pltpu.SemaphoreType.DMA((5,)),
            pltpu.SemaphoreType.DMA((2, CHUNKS, PARTS)),
            pltpu.SemaphoreType.DMA((2, CHUNKS, PARTS)),
            pltpu.SemaphoreType.DMA((2, 7)),
            pltpu.SemaphoreType.DMA((2, 7)),
        ],
        compiler_params=pltpu.CompilerParams(
            collective_id=0, has_side_effects=True, vmem_limit_bytes=58 * 1024 * 1024
        ),
        name="embedder_window",
    )(query_len, passage_len, positive, queries_in, passages_in, norm_gain, w_in[0], w_out[0])
    grads = grads.reshape(2, 1, 1, SEQ, D)
    return grads[1], grads[0], gains[:PACKS].reshape(1, D)


def solution(mesh):
    return jax.shard_map(
        local,
        mesh=mesh,
        in_specs=(
            P("dp", None, None),
            P("dp", None, None),
            P("dp"),
            P("dp"),
            P("dp"),
            P("segment", None),
            P("segment", "dp", None),
            P("segment", "dp", None),
        ),
        out_specs=(
            P("segment", "dp", None, None),
            P("segment", "dp", None, None),
            P("segment", None),
        ),
        check_vma=False,
    )
```

```python
import math

import jax
import jax.numpy as jnp
from jax import lax
from jax.experimental import pallas as pl
from jax.experimental.pallas import tpu as pltpu
from jax.sharding import PartitionSpec as P

MESH = pl.DeviceIdType.MESH
BF, F32 = jnp.bfloat16, jnp.float32
D, KVW, SEQ, NQ = 3584, 1024, 64, 64
NX, NZ, NC, NY = 4, 8, 2, 4
TEMP = 0.02
CHUNK = 16
CHUNKS = 2 * SEQ // CHUNK
PARTS = 4
WIDE = D // PARTS
SLABS = NX // PARTS
PACKS = D // 128
FAR_X, FAR_Z = (2, 1, 3), (4, 3, 5, 2, 6, 1, 7)
WEIGHT_ORDER = (
    2, 3, 0, 1, 0, 2, 3, 2, 0, 1, 2, 3, 0, 2, 2, 0, 1, 2, 0, 0, 0, 0, 2, 2, 2, 3, 0, 2, 2, 0, 2, 0, 1, 3, 0, 2, 1, 3,
)
EPS = 1e-06
C0 = math.sqrt(2.0 / math.pi)
EMB_P, EMB_Q, W_IN, W_OUT = 0, 1, 2, 3
ALL = slice(None)
NT = (((1,), (1,)), ((), ()))


def gelu(v):
    return 0.5 * v * (1.0 + jnp.tanh(C0 * (v + 0.044715 * v * v * v)))


def gelu_slope(v):
    t = jnp.tanh(C0 * (v + 0.044715 * v * v * v))
    return 0.5 * (1.0 + t) + 0.5 * v * (1.0 - t * t) * C0 * (1.0 + 3.0 * 0.044715 * v * v)


def kernel(
    qlen_ref, plen_ref, pos_ref, queries_ref, passages_ref, gain_hbm, wi_hbm, wo_hbm,
    grad_ref, gsum_ref,
    win, wout, win_t, wout_t, emb, embs, gain_ref, wi_ref, pair, kept, pre, scales, act, outb, gin, dpre, gacc, pooled,
    pack, near, far,
    ag_send, ag_recv, pair_sem, tok_sem, hop_send, hop_recv, red_send, red_recv,
):
    me = lax.axis_index("dp")
    seg = lax.axis_index("segment")
    x, z, c = me // (NZ * NC), (me // NC) % NZ, me % NC

    def dev(px, pz, pc):
        return ((px * NZ + pz) * NC + pc, seg)

    def xo(by):
        return (x + by + NX) % NX

    def zo(by):
        return (z + by + NZ) % NZ

    own = [
        pltpu.make_async_copy(src, dst, tok_sem.at[2 + j])
        for j, (src, dst) in enumerate(((wo_hbm, wout.at[x, z, c]), (wi_hbm, wi_ref), (gain_hbm, gain_ref)))
    ]
    for op in own:
        op.start()
    tokens = [
        pltpu.make_async_copy(ref.at[0], kept.at[pl.ds(side * SEQ, SEQ)], tok_sem.at[side])
        for side, ref in enumerate((passages_ref, queries_ref))
    ]

    @pl.when(seg == 0)
    def _():
        for op in tokens:
            op.start()

    barrier = pltpu.get_barrier_semaphore()
    mates = [dev(xo(dx), z, pc) for dx in range(NX) for pc in (c, 1 - c)][1:]
    mates += [dev(x, zo(dz), c) for dz in range(1, NZ)]
    mates += [(me, (seg + by) % NY) for by in (1, NY - 1)]
    for mate in mates:
        pl.semaphore_signal(barrier, inc=1, device_id=mate, device_id_type=MESH)
    pl.semaphore_wait(barrier, len(mates))

    def piece(tensor, colour, xs, zs, pc):
        if tensor == W_IN:
            rows = pl.ds(0, 48) if colour == 0 else pl.ds(48, 64)
            return win.at[xs, zs, rows, pl.ds(pl.multiple_of(pc * 512, 512), 512)]
        if tensor == W_OUT:
            cols = pl.ds(0, 1408) if colour == 0 else pl.ds(1408, 2176)
            return wout.at[xs, zs, pl.ds(pc, 1), :, cols]
        rows = pl.ds(32 * tensor, 8) if colour == 0 else pl.ds(32 * tensor + 8, 24)
        return emb.at[xs, zs, pl.ds(pc, 1), rows, :]

    def copy_of(tensor, slot, ref, target):
        return pltpu.make_async_remote_copy(
            src_ref=ref, dst_ref=ref,
            send_sem=ag_send.at[tensor, slot], recv_sem=ag_recv.at[tensor, slot],
            device_id=target, device_id_type=MESH,
        )

    def one(at):
        return pl.ds(at, 1)

    def gather(tensor, colour, plus):
        def send(slot, xs, zs, target):
            op = copy_of(tensor, slot, piece(tensor, colour, xs, zs, c), target)
            op.start()
            unsent.append(op.wait_send)

        def got(slot, xs, zs):
            copy_of(tensor, slot, piece(tensor, colour, xs, zs, c), dev(x, z, 1 - c)).wait_recv()

        def pass_on(slot, xs, zs):
            send(slot, xs, zs, dev(x, z, 1 - c))
            other = copy_of(tensor, slot, piece(tensor, colour, xs, zs, 1 - c), dev(x, z, 1 - c))
            pending.append(other.wait_recv)

        up, down = dev(x, zo(1), c), dev(x, zo(-1), c)
        right, left = dev(xo(1), z, c), dev(xo(-1), z, c)
        if colour == 0:
            for dx in range(1, NX):
                send(dx - 1, one(x), one(z), dev(xo(dx), z, c))
            yield
            for dx in range(1, NX):
                got(dx - 1, one(xo(-dx)), one(z))
            send(3, ALL, one(z), up)
            send(4, ALL, one(z), down)
            pass_on(42, ALL, one(z))
            for step in range(1, 4):
                yield
                got(1 + 2 * step, ALL, one(zo(-step)))
                if step < 3:
                    send(3 + 2 * step, ALL, one(zo(-step)), up)
                else:
                    send(9, pl.ds(0, 2), one(zo(-3)), up)
                got(2 + 2 * step, ALL, one(zo(step)))
                if step < 3:
                    send(4 + 2 * step, ALL, one(zo(step)), down)
                else:
                    send(10, pl.ds(2, 2), one(zo(3)), down)
                pass_on(41 + 2 * step, ALL, one(zo(-step)))
                pass_on(42 + 2 * step, ALL, one(zo(step)))
            yield
            got(9, pl.ds(0, 2), one(zo(-4)))
            got(10, pl.ds(2, 2), one(zo(4)))
            pass_on(49, ALL, one(zo(4)))
            return
        offsets = (0, -1, 1, -2, 2, -3, 3, 4)

        def sideways(j):
            at = one(zo(offsets[j]))
            send(18 + j, one(x), at, right)
            send(26 + j, one(x), at, left)

        send(11, one(x), one(z), up)
        send(12, one(x), one(z), down)
        sideways(0)
        for step in range(1, 4):
            yield
            got(9 + 2 * step, one(x), one(zo(-step)))
            if step < 3:
                send(11 + 2 * step, one(x), one(zo(-step)), up)
            elif plus:
                send(17, one(x), one(zo(-3)), up)
            sideways(2 * step - 1)
            got(10 + 2 * step, one(x), one(zo(step)))
            if step < 3:
                send(12 + 2 * step, one(x), one(zo(step)), down)
            elif not plus:
                send(17, one(x), one(zo(3)), down)
            sideways(2 * step)
        yield
        got(17, one(x), one(zo(4)))
        sideways(7)
        pass_on(50, one(x), ALL)
        for j, by in enumerate(offsets):
            yield
            got(18 + j, one(xo(-1)), one(zo(by)))
            got(26 + j, one(xo(1)), one(zo(by)))
            if j % 2 == 0:
                send(34 + j, one(xo(-1)), one(zo(by)), right)
            else:
                send(34 + j, one(xo(1)), one(zo(by)), left)
        pass_on(51, one(xo(-1)), ALL)
        pass_on(52, one(xo(1)), ALL)
        yield
        for j, by in enumerate(offsets):
            got(34 + j, one(xo(2)), one(zo(by)))
        pass_on(53, one(xo(2)), ALL)

    def exchange(tensor):
        def own_first():
            ops = [(0, by - 1, one(x), one(z), dev(xo(by), z, c), one(xo(-by)), one(z)) for by in FAR_X]
            return ops + [(1, 2 + by, one(x), one(z), dev(x, zo(by), c), one(x), one(zo(-by))) for by in FAR_Z]

        def along_z():
            return [(0, 9 + by, ALL, one(z), dev(x, zo(by), c), ALL, one(zo(-by))) for by in FAR_Z]

        def along_x():
            return [(1, 16 + by, one(x), ALL, dev(xo(by), z, c), one(xo(-by)), ALL) for by in FAR_X]

        def to_mate():
            return [(colour, 20 + colour, ALL, ALL, dev(x, z, 1 - c), ALL, ALL) for colour in range(2)]

        def send(ops):
            for colour, slot, xs, zs, target, _, _ in ops:
                copy_of(tensor, slot, piece(tensor, colour, xs, zs, c), target).start()

        def got(ops, pc=c):
            for colour, slot, _, _, target, xs, zs in ops:
                copy_of(tensor, slot, piece(tensor, colour, xs, zs, pc), target).wait_recv()

        def begin():
            send(own_first())

        def middle():
            ops = own_first()
            got(ops[: NX - 1])
            send(along_z())
            got(ops[NX - 1 :])
            send(along_x())

        def end():
            got(along_x())
            send(to_mate()[1:])
            got(along_z())
            send(to_mate()[:1])
            got(to_mate()[::-1], 1 - c)
            for colour, slot, xs, zs, target, _, _ in own_first() + along_z() + along_x() + to_mate():
                copy_of(tensor, slot, piece(tensor, colour, xs, zs, c), target).wait_send()

        return begin, middle, end

    def follow(streams, order):
        for at in order:
            next(streams[at], None)

    pending, unsent = [], []
    for op in own:
        op.wait()
    streams = [
        gather(tensor, colour, tensor == W_IN) for tensor in (W_OUT, W_IN) for colour in (1, 0)
    ]
    follow(streams, (0, 1))
    swap = pltpu.make_async_remote_copy(
        src_ref=wi_ref, dst_ref=pair, send_sem=pair_sem.at[0], recv_sem=pair_sem.at[1],
        device_id=dev(x, z, 1 - c), device_id_type=MESH,
    )
    swap.start()

    swap.wait()
    mine, theirs = wi_ref[...].astype(F32), pair[...].astype(F32)
    both = jnp.concatenate(
        [jnp.where(c == 0, mine, theirs), jnp.where(c == 0, theirs, mine)], axis=0
    )
    half = jnp.where(c == 0, both[:, :512], both[:, 512:]).astype(BF)
    win[pl.ds(x, 1), pl.ds(z, 1), :, pl.ds(pl.multiple_of(c * 512, 512), 512)] = half.reshape(1, 1, 112, 512)
    follow(streams, WEIGHT_ORDER)
    for wait in pending:
        wait()

    def flip():
        @pl.loop(0, NX)
        def _(n):
            for j in range(8):
                part = win[n, :, :, pl.ds(128 * j, 128)].reshape(896, 128)
                win_t[pl.ds(128 * j, 128), pl.ds(pl.multiple_of(n * 896, 128), 896)] = part.T
            for j in range(7):
                part = wout[n, :, :, :, pl.ds(512 * j, 512)].reshape(256, 512)
                wout_t[pl.ds(512 * j, 512), pl.ds(pl.multiple_of(n * 256, 256), 256)] = part.T

    @pl.when(seg > 0)
    def _():
        flip()
        for wait in unsent:
            wait()

    @pl.when(seg == 0)
    def _():
        for op in tokens:
            op.wait()

    def hop(step, k, part, src, dst, to):
        rows = pl.ds(pl.multiple_of(k * CHUNK, CHUNK), CHUNK)
        cols = pl.ds(part * WIDE, WIDE)
        return pltpu.make_async_remote_copy(
            src_ref=src.at[rows, cols], dst_ref=dst.at[rows, cols],
            send_sem=hop_send.at[step, k, part], recv_sem=hop_recv.at[step, k, part],
            device_id=(me, to), device_id_type=MESH,
        )

    pooled[...] = jnp.zeros_like(pooled)

    def weight(start, count, side):
        length = jnp.where(side == 0, plen_ref[0], qlen_ref[0])
        at = lax.broadcasted_iota(jnp.int32, (count, 1), 0) + start
        return jnp.where(at < length, 1.0, 0.0) / length.astype(F32)

    def norm_of(side):
        total = jnp.sum(pooled[side], axis=0, keepdims=True)
        return total, lax.rsqrt(jnp.sum(total * total, axis=-1, keepdims=True) + EPS)

    def embed(side):
        total, inv = norm_of(side)
        unit = total * inv
        for k in range(PACKS):
            pack[side, k : k + 1, :] = unit[:, k * 128 : (k + 1) * 128]
        spot = lax.broadcasted_iota(jnp.int32, (32 - PACKS, 128), 1)
        pack[side, PACKS:32, :] = jnp.where(spot == pos_ref[0], 1.0, 0.0)
        emb[pl.ds(x, 1), pl.ds(z, 1), pl.ds(c, 1), pl.ds(32 * side, 32), :] = pack[side].reshape(1, 1, 1, 32, 128)
        return unit

    query_steps, passage_steps = exchange(EMB_Q), exchange(EMB_P)

    @pl.loop(0, CHUNKS)
    def _(k):
        rows = pl.ds(pl.multiple_of(k * CHUNK, CHUNK), CHUNK)

        square = jnp.zeros((CHUNK, 1), F32)
        v = jnp.zeros((CHUNK, KVW), F32)
        for n in range(PARTS):
            cols = pl.ds(n * WIDE, WIDE)

            @pl.when(seg > 0)
            def _():
                hop(0, k, n, outb, kept, seg).wait_recv()

            stream = kept[rows, cols].astype(F32)
            square = square + jnp.sum(stream * stream, axis=-1, keepdims=True)
            gained = (stream * gain_ref[:, cols]).astype(BF)
            v = v + jnp.dot(gained, win[n * SLABS : (n + 1) * SLABS].reshape(WIDE, KVW), preferred_element_type=F32)
        scale = lax.rsqrt(square * (1.0 / D) + EPS)
        scales[rows, :] = jnp.broadcast_to(scale, (CHUNK, 128))
        v = v * scale
        pre[rows, :] = v
        act[...] = gelu(v).astype(BF)

        def rise(n):
            cols = pl.ds(n * WIDE, WIDE)
            return jnp.dot(act[...], wout[:, :, :, :, cols].reshape(KVW, WIDE), preferred_element_type=F32)

        ahead = rise(0)
        for n in range(PARTS):
            cols = pl.ds(n * WIDE, WIDE)
            v, ahead = ahead, rise(n + 1) if n + 1 < PARTS else None
            outb[rows, cols] = (kept[rows, cols].astype(F32) + v).astype(BF)

            @pl.when(seg < NY - 1)
            def _():
                hop(0, k, n, outb, kept, seg + 1).start()

        @pl.when(seg == NY - 1)
        def _():
            side = (k * CHUNK) // SEQ
            total = jnp.zeros((8, D), F32)
            for part in range(CHUNK // 16):
                sub = pl.ds(pl.multiple_of(k * CHUNK + part * 16, 16), 16)
                scaled = outb[sub, :].astype(F32) * weight(part * 16 + (k * CHUNK) % SEQ, 16, side)
                total = total + scaled[0:8] + scaled[8:16]
            pooled[side] += total

            @pl.when(k == CHUNKS // 2 - 1)
            def _():
                embed(0)
                passage_steps[0]()

            @pl.when(k == CHUNKS * 3 // 4 - 1)
            def _():
                passage_steps[1]()

    @pl.when(seg == 0)
    def _():
        flip()
        for wait in unsent:
            wait()

    flat = emb.reshape(NQ * 64, 128)

    def unpack(side):
        for k in range(PACKS):
            embs[side, :, pl.ds(k * 128, 128)] = flat[pl.ds(32 * side + k, NQ, stride=64), :]

    def product(a, b, dims):
        a0, b0 = a.astype(BF), b.astype(BF)
        a1, b1 = (a - a0.astype(F32)).astype(BF), (b - b0.astype(F32)).astype(BF)
        terms = [lax.dot_general(u, v, dims, preferred_element_type=F32) for u, v in ((a0, b1), (a1, b0), (a0, b0))]
        return terms[0] + terms[1] + terms[2]

    def excess(logits, onehot):
        expo = jnp.exp(logits - jnp.max(logits, axis=1, keepdims=True))
        return (expo / jnp.sum(expo, axis=1, keepdims=True) - onehot) / NQ

    def spread_back(side, demb):
        total, inv = norm_of(side)
        along = jnp.sum(total * demb, axis=-1, keepdims=True)
        grad = inv * demb - total * (inv * inv * inv) * along
        for part in range(SEQ // 16):
            sub = pl.ds(side * SEQ + part * 16, 16)
            gin[sub, :] = (weight(part * 16, 16, side) * grad).astype(BF)

    @pl.when(seg == NY - 1)
    def _():
        unit = embed(1)
        query_steps[0]()
        passage_steps[2]()
        unpack(0)
        unit = jnp.broadcast_to(unit, (8, D))
        logits = product(unit, embs[0], NT) / TEMP
        spot = lax.broadcasted_iota(jnp.int32, (8, NQ), 1)
        dlogits = excess(logits, jnp.where(spot == pos_ref[0], 1.0, 0.0))
        spread_back(1, product(dlogits, embs[0], (((1,), (0,)), ((), ())))[0:1] / TEMP)

    def passages_back():
        unpack(1)
        onehot = flat[pl.ds(PACKS, NQ, stride=64), :][:, 0:NQ]
        logits = product(embs[1], embs[0], NT) / TEMP
        dlogits = excess(logits, onehot)
        jj = lax.broadcasted_iota(jnp.int32, (NQ, NQ), 1)
        col = jnp.sum(jnp.where(jj == me, dlogits, 0.0), axis=1, keepdims=True)
        spread_back(0, jnp.sum(col * embs[1], axis=0, keepdims=True) / TEMP)

    gacc[...] = jnp.zeros_like(gacc)

    @pl.loop(0, CHUNKS)
    def _(step):
        k = CHUNKS - 1 - step
        rows = pl.ds(pl.multiple_of(k * CHUNK, CHUNK), CHUNK)

        back = jnp.zeros((CHUNK, KVW), F32)
        for n in range(PARTS):
            cols = pl.ds(n * WIDE, WIDE)

            @pl.when(seg < NY - 1)
            def _():
                hop(1, k, n, grad_ref, gin, seg).wait_recv()

            back = back + jnp.dot(gin[rows, cols], wout_t[cols, :], preferred_element_type=F32)
        v = pre[rows, :]
        d = back * gelu_slope(v)
        along = jnp.sum(d * v, axis=-1, keepdims=True)
        dpre[...] = d.astype(BF)
        mean = along * (1.0 / D)
        scale = scales[rows, 0:1]

        def fall(n):
            return jnp.dot(dpre[...], win_t[:, pl.ds(n * WIDE, WIDE)], preferred_element_type=F32)

        ahead = fall(0)
        for n in range(PARTS):
            cols = pl.ds(n * WIDE, WIDE)
            dnormed, ahead = ahead, fall(n + 1) if n + 1 < PARTS else None
            unit = kept[rows, cols].astype(F32) * scale
            both = dnormed * unit
            gacc[:, cols] += sum(both[j : j + 8] for j in range(8, CHUNK, 8)) + both[0:8]
            res = gin[rows, cols].astype(F32) + scale * (dnormed * gain_ref[:, cols] - unit * mean)
            grad_ref[rows, cols] = res.astype(BF)

            @pl.when(seg > 0)
            def _():
                hop(1, k, n, grad_ref, gin, seg - 1).start()

        @pl.when((seg == NY - 1) & (step == 0))
        def _():
            query_steps[1]()

        @pl.when((seg == NY - 1) & (step == CHUNKS // 2 - 1))
        def _():
            query_steps[2]()
            passages_back()

    def reduce(step, buf, at, peers):
        ops, sent = [], []
        for j, (target, source) in enumerate(peers):
            op = pltpu.make_async_remote_copy(
                src_ref=buf.at[at], dst_ref=buf.at[at],
                send_sem=red_send.at[step, j], recv_sem=red_recv.at[step, j],
                device_id=target, device_id_type=MESH,
            )
            op.start()
            sent.append(op.wait_send)
            ops.append(pltpu.make_async_remote_copy(
                src_ref=buf.at[source], dst_ref=buf.at[source],
                send_sem=red_send.at[step, j], recv_sem=red_recv.at[step, j],
                device_id=target, device_id_type=MESH,
            ).wait_recv)
        for op in ops:
            op()
        return sent

    at = x * NC + c
    gsum = jnp.sum(gacc[...], axis=0, keepdims=True)
    for k in range(PACKS):
        pack[0, k : k + 1, :] = gsum[:, k * 128 : (k + 1) * 128]
    near[at] = pack[0]
    peers = []
    for dx in FAR_X + (0,):
        for pc in (c, 1 - c) if dx else (1 - c,):
            peers.append((dev(xo(dx), z, pc), xo(-dx) * NC + pc))
    sent = reduce(0, near, at, peers)
    far[z] = jnp.sum(near[...], axis=0)
    sent += reduce(1, far, z, [(dev(x, zo(dz), c), zo(-dz)) for dz in FAR_Z])
    gsum_ref[...] = jnp.sum(far[...], axis=0)
    for op in sent:
        op()

    @pl.when(seg > 0)
    def _():
        for k in range(CHUNKS):
            for part in range(PARTS):
                hop(1, k, part, grad_ref, gin, seg).wait_send()

    @pl.when(seg < NY - 1)
    def _():
        for k in range(CHUNKS):
            for part in range(PARTS):
                hop(0, k, part, outb, kept, seg).wait_send()


def local(queries_in, passages_in, query_len, passage_len, positive, norm_gain, w_in, w_out):
    vmem, hbm = pl.BlockSpec(memory_space=pltpu.VMEM), pl.BlockSpec(memory_space=pltpu.HBM)
    smem = pl.BlockSpec(memory_space=pltpu.SMEM)
    rows = 2 * SEQ
    grads, gains = pl.pallas_call(
        kernel,
        out_shape=(
            jax.ShapeDtypeStruct((rows, D), BF),
            jax.ShapeDtypeStruct((32, 128), F32),
        ),
        in_specs=[smem] * 3 + [hbm] * 5,
        out_specs=(vmem, vmem),
        scratch_shapes=[
            pltpu.VMEM((NX, NZ, 112, KVW), BF),
            pltpu.VMEM((NX, NZ, NC, 16, D), BF),
            pltpu.VMEM((KVW, D), BF),
            pltpu.VMEM((D, KVW), BF),
            pltpu.VMEM((NX, NZ, NC, 64, 128), F32),
            pltpu.VMEM((2, NQ, D), F32),
            pltpu.VMEM((1, D), F32),
            pltpu.VMEM((56, KVW), BF),
            pltpu.VMEM((56, KVW), BF),
            pltpu.VMEM((rows, D), BF),
            pltpu.VMEM((rows, KVW), F32),
            pltpu.VMEM((rows, 128), F32),
            pltpu.VMEM((CHUNK, KVW), BF),
            pltpu.VMEM((rows, D), BF),
            pltpu.VMEM((rows, D), BF),
            pltpu.VMEM((CHUNK, KVW), BF),
            pltpu.VMEM((8, D), F32),
            pltpu.VMEM((2, 8, D), F32),
            pltpu.VMEM((2, 32, 128), F32),
            pltpu.VMEM((NX * NC, 32, 128), F32),
            pltpu.VMEM((NZ, 32, 128), F32),
            pltpu.SemaphoreType.DMA((4, 54)),
            pltpu.SemaphoreType.DMA((4, 54)),
            pltpu.SemaphoreType.DMA((2,)),
            pltpu.SemaphoreType.DMA((5,)),
            pltpu.SemaphoreType.DMA((2, CHUNKS, PARTS)),
            pltpu.SemaphoreType.DMA((2, CHUNKS, PARTS)),
            pltpu.SemaphoreType.DMA((2, 7)),
            pltpu.SemaphoreType.DMA((2, 7)),
        ],
        compiler_params=pltpu.CompilerParams(
            collective_id=0, has_side_effects=True, vmem_limit_bytes=58 * 1024 * 1024
        ),
        name="embedder_window",
    )(query_len, passage_len, positive, queries_in, passages_in, norm_gain, w_in[0], w_out[0])
    grads = grads.reshape(2, 1, 1, SEQ, D)
    return grads[1], grads[0], gains[:PACKS].reshape(1, D)


def solution(mesh):
    return jax.shard_map(
        local,
        mesh=mesh,
        in_specs=(
            P("dp", None, None),
            P("dp", None, None),
            P("dp"),
            P("dp"),
            P("dp"),
            P("segment", None),
            P("segment", "dp", None),
            P("segment", "dp", None),
        ),
        out_specs=(
            P("segment", "dp", None, None),
            P("segment", "dp", None, None),
            P("segment", None),
        ),
        check_vma=False,
    )
```
